128 devices in a mesh: fsdp: 16 (over z_hi, x, core), context: 4 (over y), tensor: 2 (over z_lo).
Axes of the slice: x: 4, y: 4, z: 4 (z_hi: 2, z_lo: 2; z = z_hi * 2 + z_lo), core: 2. Of those that a mesh axis runs over, the one named last changes fastest.
Arguments:
- tokens: bfloat16 [32768, 1536], P(('fsdp', 'context')), may hold values from -6 to 6
- teacher: bfloat16 [32768, 1536], P(('fsdp', 'context')), may hold values from -6 to 6
- segments: int32 [16, 2048], P('fsdp'), may hold values from 0 to 66, as said below
- routes: int32 [32768, 2], P(('fsdp', 'context')), may hold values from 0 to 15, all different within a row; in each aligned block of 512 rows (0 to 511, 512 to 1023, ...) at most 96 rows name the same one
- route_weight: float32 [32768, 2], P(('fsdp', 'context')), may hold values from 2 to 16
- norm_attn: bfloat16 [1536], P(('fsdp', 'context')), may hold values from 0.5 to 1.5
- w_query: bfloat16 [1536, 1536], P(('fsdp', 'context'), 'tensor'), may hold values from -0.15625 to 0.15625
- key_weight: bfloat16 [1536, 512], P(('fsdp', 'context'), 'tensor'), may hold values from -0.15625 to 0.15625
- value_weight: bfloat16 [1536, 512], P(('fsdp', 'context'), 'tensor'), may hold values from -0.15625 to 0.15625
- w_out: bfloat16 [1536, 1536], P('tensor', ('fsdp', 'context')), may hold values from -0.625 to 0.625
- norm_ffn: bfloat16 [1536], P(('fsdp', 'context')), may hold values from 0.5 to 1.5
- w_router: bfloat16 [1536, 16], P(('fsdp', 'context')), may hold values from -0.109375 to 0.109375
- w_gate: bfloat16 [16, 1536, 1024], P('fsdp', 'context', 'tensor'), may hold values from -0.15625 to 0.15625
- w_up: bfloat16 [16, 1536, 1024], P('fsdp', 'context', 'tensor'), may hold values from -0.15625 to 0.15625
- w_down: bfloat16 [16, 1024, 1536], P('fsdp', 'tensor', 'context'), may hold values from -0.5 to 0.5
Outputs:
- output: float32 [32768, 1536], P(('fsdp', 'context'))
- loss: float32 [], replicated
- grad_tokens: float32 [32768, 1536], P(('fsdp', 'context'))
- grad_norm_attn: float32 [1536], P(('fsdp', 'context'))
- grad_query: float32 [1536, 1536], P(('fsdp', 'context'), 'tensor')
- grad_key: float32 [1536, 512], P(('fsdp', 'context'), 'tensor')
- grad_value: float32 [1536, 512], P(('fsdp', 'context'), 'tensor')
- grad_out: float32 [1536, 1536], P('tensor', ('fsdp', 'context'))
- grad_norm_ffn: float32 [1536], P(('fsdp', 'context'))
- grad_router: float32 [1536, 16], P(('fsdp', 'context'))
- grad_gate: float32 [16, 1536, 1024], P('fsdp', 'context', 'tensor')
- grad_up: float32 [16, 1536, 1024], P('fsdp', 'context', 'tensor')
- grad_down: float32 [16, 1024, 1536], P('fsdp', 'tensor', 'context')
The draws below stay inside these ranges and needn't reach their ends.
Inputs may be any that keep to these rules, and one draw needn't show every extreme that they name: `segments`: each row is one sequence of 2048 positions: documents numbered 1, 2, 3 and so on from position 0 on, never falling, exactly 66 of them, then 512 // 8 to 256 tail pads numbered 0; one document covers positions 256 to 1536. `routes`: each row names two different experts; in each aligned block of 512 rows (the rows of one device) no expert is named by more than 96 rows, and in some blocks one is named by exactly 96.
All inputs are finite; a program needn't handle non-finite values.
Results may differ from the reference program's by a relative error of at most 0.015.
Values may be sent and summed in bfloat16 or wider, within the bound.
No kernel may reach another device: no remote copies, remote signals or barrier semaphores. Data moves between devices by JAX's collectives and lax.ppermute only.
A program may use at most 192 MiB of HBM per device.

```python
import math
import jax
import jax.numpy as jnp
import numpy as np
from jax import lax

MODEL_WIDTH = 1536
QUERY_HEAD_COUNT = 24
KEY_VALUE_HEADS = 8
HEAD_WIDTH = 64
FF = 1024
EXPERTS = 16
TOP = 2
TOK_DEV = 512
SEQUENCE_LENGTH = 2048
SEQUENCE_COUNT = 16
TOKENS = 32768
CAP = 96


def segment_row(key):
    key_pads = jax.random.fold_in(key, 11)
    key_front = jax.random.fold_in(key, 12)
    key_stop = jax.random.fold_in(key, 13)
    key_tail = jax.random.fold_in(key, 14)
    positions = jnp.arange(SEQUENCE_LENGTH, dtype=jnp.int32)
    extra_docs = TOK_DEV // 16
    pad_count = jax.random.randint(key_pads, (), TOK_DEV // 8, TOK_DEV // 2 + 1)
    valid_len = SEQUENCE_LENGTH - pad_count
    front_order = jax.random.permutation(key_front, SEQUENCE_LENGTH).astype(jnp.int32)
    front_ok = (positions >= 1) & (positions < TOK_DEV // 2)
    front_score = jnp.where(front_ok, front_order, -1)
    front_top, front_idx = lax.top_k(front_score, extra_docs)
    long_stop = valid_len - jax.random.randint(key_stop, (), TOK_DEV // 16 + 1, TOK_DEV // 4 + 1)
    tail_order = jax.random.permutation(key_tail, SEQUENCE_LENGTH).astype(jnp.int32)
    tail_ok = (positions > long_stop) & (positions < valid_len)
    tail_score = jnp.where(tail_ok, tail_order, -1)
    tail_top, tail_idx = lax.top_k(tail_score, extra_docs)
    flags = jnp.zeros((SEQUENCE_LENGTH,), jnp.int32)
    flags = flags.at[front_idx].set(1)
    flags = flags.at[tail_idx].set(1)
    flags = jnp.where(positions == long_stop, 1, flags)
    numbers = 1 + jnp.cumsum(flags)
    return jnp.where(positions < valid_len, numbers, 0).astype(jnp.int32)


def draw_segments(key, part):
    key = jax.random.fold_in(key, 7)
    row_keys = jax.random.split(key, SEQUENCE_COUNT)
    return jax.vmap(segment_row)(row_keys).astype(jnp.int32)


def steps_of(own_key, dims, shards, smallest, top_value):
    def one(dim, parts):
        steps = jax.random.uniform(jax.random.fold_in(jax.random.fold_in(own_key, 6), dim), (parts,), jnp.float32, smallest / len(shards), top_value / len(shards))
        return jnp.repeat(jnp.exp(steps), dims[dim] // parts).reshape((-1,) + (1,) * (len(dims) - dim - 1))

    factor_of = one(*shards[0])
    for cut in shards[1:]:
        factor_of = factor_of * one(*cut)
    return factor_of


def assign_block(own_key, own, number, rows, count, top, limit, skew):
    order = jax.random.permutation(own_key, count)
    packed, ordinary = load_shares(count, rows * top, limit, skew, True), load_shares(count, rows * top, limit, skew, False)
    places = jnp.arange(count)

    def named(tallies, turn):
        used = int((tallies > 0).sum())
        fixed = max(1, used // 4)
        passed = fixed + (places - fixed + turn * (used - fixed)) % max(1, count - fixed)
        return jnp.zeros((count,), jnp.int32).at[order[jnp.where(places < fixed, places, passed)]].set(jnp.asarray(tallies, jnp.int32))

    tallies = jnp.where(number % 4 == 0, named(packed, number // 4), named(ordinary, number - number // 4 - 1))
    mixed = jax.random.permutation(jax.random.fold_in(own, 3), count)
    source_of, taker = mixed[0:count // 2 * 2:2], mixed[1:count // 2 * 2:2]
    room = jnp.minimum(tallies[source_of] - 1, limit - tallies[taker]) // 2
    room = jnp.where((source_of == order[0]) | (taker == order[0]) | (tallies[taker] == 0), 0, jnp.maximum(room, 0))
    passed = jax.random.randint(jax.random.fold_in(own, 4), (count // 2,), 0, 1 << 20) % (room + 1)
    tallies = tallies.at[source_of].add(-passed).at[taker].add(passed)
    members = jnp.searchsorted(jnp.cumsum(tallies), jnp.arange(rows * top), side="right").astype(jnp.int32)
    table = members.reshape(top, rows).T
    table = table[jax.random.permutation(jax.random.fold_in(own, 1), rows)]
    turn = jax.random.randint(jax.random.fold_in(own, 2), (rows, 1), 0, top)
    return jnp.take_along_axis(table, (jnp.arange(top)[None, :] + turn) % top, axis=1)


def load_shares(count, total, reach, slope, full):
    weights = [(1 << 20) // math.isqrt(grade ** slope) + 1 for grade in range(1, count + 1)]
    largest = reach if full else min(reach, max(-(-total // count), total * weights[0] // sum(weights)))
    least = 1 if total - largest >= count - 1 else 0
    counts, rest = [largest] + [least] * (count - 1), total - largest - least * (count - 1)
    while rest > 0:
        movable = [i for i in range(1, count) if counts[i] < largest] or [i for i in range(1, count) if counts[i] < reach]
        mass, left = sum([weights[i] for i in movable]), rest
        for i in movable:
            more = min(reach - counts[i], max(1, left * weights[i] // mass), rest)
            counts[i] = counts[i] + more
            rest = rest - more
    return np.array(counts)


def gaussian(own_key, extent, spread, limit, cuts=(), held_as=jnp.bfloat16):
    values = spread * jax.random.normal(own_key, extent, jnp.float32)
    if cuts:
        values = values * steps_of(own_key, extent, cuts, -0.22, 0.18)
    return jnp.clip(values, -limit, limit).astype(held_as)


def setup_inputs(seed: int = 0) -> dict:
    seeds = jax.random.split(jax.random.key(seed), 16)
    tokens = gaussian(seeds[0], (TOKENS, MODEL_WIDTH), 1.0, 6.0, ((0, 64),))
    teacher = gaussian(seeds[1], (TOKENS, MODEL_WIDTH), 1.0, 6.0, ((0, 64),))
    segments = draw_segments(jax.random.fold_in(seeds[15], 71), 0)
    routes_keys = jax.random.split(jax.random.fold_in(seeds[3], 1), TOKENS // TOK_DEV)
    routes_turns = jax.random.permutation(jax.random.fold_in(seeds[3], 3), TOKENS // TOK_DEV)
    routes = jax.vmap(lambda own, number: assign_block(jax.random.fold_in(seeds[3], 2), own, number, TOK_DEV, EXPERTS, TOP, CAP, 1))(routes_keys, routes_turns).reshape((TOKENS, TOP))
    route_weight = jnp.clip(jnp.exp(math.log(16.0) - 2.0794415 * jax.random.uniform(seeds[4], (TOKENS, TOP), jnp.float32) ** steps_of(seeds[4], (TOKENS, TOP), ((0, 64),), -0.2, 0.2)), 2.0, 16.0)
    norm_attn = jnp.clip(1.0 + 0.1 * jax.random.normal(seeds[5], (MODEL_WIDTH,), jnp.float32), 0.5, 1.5).astype(jnp.bfloat16)
    w_query = gaussian(seeds[6], (MODEL_WIDTH, QUERY_HEAD_COUNT * HEAD_WIDTH), MODEL_WIDTH ** -0.5, 0.15625, ((0, 64), (1, 2)))
    key_weight = gaussian(seeds[7], (MODEL_WIDTH, KEY_VALUE_HEADS * HEAD_WIDTH), MODEL_WIDTH ** -0.5, 0.15625, ((0, 64), (1, 2)))
    value_weight = gaussian(seeds[8], (MODEL_WIDTH, KEY_VALUE_HEADS * HEAD_WIDTH), MODEL_WIDTH ** -0.5, 0.15625, ((0, 64), (1, 2)))
    w_out = gaussian(seeds[9], (QUERY_HEAD_COUNT * HEAD_WIDTH, MODEL_WIDTH), (QUERY_HEAD_COUNT * HEAD_WIDTH // 16) ** -0.5, 0.625, ((0, 2), (1, 64)))
    norm_ffn = jnp.clip(1.0 + 0.1 * jax.random.normal(seeds[10], (MODEL_WIDTH,), jnp.float32), 0.5, 1.5).astype(jnp.bfloat16)
    w_router = gaussian(seeds[11], (MODEL_WIDTH, EXPERTS), (2 * MODEL_WIDTH) ** -0.5, 0.109375, ((0, 64),))
    w_gate = gaussian(seeds[12], (EXPERTS, MODEL_WIDTH, FF), MODEL_WIDTH ** -0.5, 0.15625, ((0, 16), (1, 4), (2, 2)))
    w_up = gaussian(seeds[13], (EXPERTS, MODEL_WIDTH, FF), MODEL_WIDTH ** -0.5, 0.15625, ((0, 16), (1, 4), (2, 2)))
    w_down = gaussian(seeds[14], (EXPERTS, FF, MODEL_WIDTH), (FF // 8) ** -0.5, 0.5, ((0, 16), (1, 2), (2, 4)))
    return dict(tokens=tokens, teacher=teacher, segments=segments, routes=routes, route_weight=route_weight, norm_attn=norm_attn, w_query=w_query, key_weight=key_weight, value_weight=value_weight, w_out=w_out, norm_ffn=norm_ffn, w_router=w_router, w_gate=w_gate, w_up=w_up, w_down=w_down)


@jax.custom_vjp
def low(v):
    return lax.optimization_barrier(v.astype(jnp.bfloat16)).astype(jnp.float32)

@jax.custom_vjp
def low_back(v):
    return v

def low_keep(v):
    return (low(v), None)

def low_pass(kept, grad):
    return (grad,)

def back_keep(v):
    return (v, None)

def back_low(kept, grad):
    return (low(grad),)
low.defvjp(low_keep, low_pass)
low_back.defvjp(back_keep, back_low)
EPSILON = 1e-06
PRECISE = lax.Precision.HIGHEST
MASKED = -1e+30

def rms_norm(values, gain_vec):
    return values * lax.rsqrt(lax.optimization_barrier(jnp.mean(values * values, axis=-1, keepdims=True)) + EPSILON) * gain_vec

def both_round(values):
    return low(low_back(values))

def attend_heads(pieces):
    query_row_block, key_row_block, value_row_block, labels = pieces
    query_group_width = QUERY_HEAD_COUNT // KEY_VALUE_HEADS
    length_count = query_row_block.shape[0]
    head_row_block = query_row_block.reshape(length_count, KEY_VALUE_HEADS, query_group_width, HEAD_WIDTH)
    scores = jnp.einsum('tkgd,skd->kgts', head_row_block, key_row_block, precision=PRECISE) * HEAD_WIDTH ** (-0.5)
    scores = low_back(scores)
    places = jnp.arange(length_count, dtype=jnp.int32)
    allowed = (labels[:, None] == labels[None, :]) & (places[None, :] <= places[:, None])
    scores = jnp.where(allowed[None, None], scores, MASKED)
    weights = low(jax.nn.softmax(scores, axis=-1))
    heads_mixed_output = jnp.einsum('kgts,skd->tkgd', weights, value_row_block, precision=PRECISE)
    return heads_mixed_output.reshape(length_count, QUERY_HEAD_COUNT * HEAD_WIDTH)

def forward(resid, norm_attn, w_query, key_weight, value_weight, w_out, norm_ffn, w_router, w_gate, w_up, w_down, segments, routes, route_weight):
    blocks = TOKENS // TOK_DEV
    act_one = low(rms_norm(resid, norm_attn))
    query_row_block = both_round(jnp.dot(act_one, w_query, precision=PRECISE))
    key_row_block = both_round(jnp.dot(act_one, key_weight, precision=PRECISE))
    value_row_block = both_round(jnp.dot(act_one, value_weight, precision=PRECISE))
    heads_mixed_output = lax.map(jax.checkpoint(attend_heads), (query_row_block.reshape(SEQUENCE_COUNT, SEQUENCE_LENGTH, QUERY_HEAD_COUNT * HEAD_WIDTH), key_row_block.reshape(SEQUENCE_COUNT, SEQUENCE_LENGTH, KEY_VALUE_HEADS, HEAD_WIDTH), value_row_block.reshape(SEQUENCE_COUNT, SEQUENCE_LENGTH, KEY_VALUE_HEADS, HEAD_WIDTH), segments))
    heads_mixed_output = both_round(heads_mixed_output.reshape(TOKENS, QUERY_HEAD_COUNT * HEAD_WIDTH))
    hidden = resid + low_back(jnp.dot(heads_mixed_output, w_out, precision=PRECISE))
    act_two = low(rms_norm(hidden, norm_ffn))
    logits = low_back(jnp.dot(act_two, w_router, precision=PRECISE))
    router_probs = jax.nn.softmax(logits, axis=-1)
    gate_values = jnp.take_along_axis(router_probs, routes, axis=1) * route_weight
    route_rows = routes.reshape(blocks, TOK_DEV * TOP)
    onehot_table = (route_rows[:, :, None] == jnp.arange(EXPERTS, dtype=jnp.int32)[None, None, :]).astype(jnp.int32)
    places = lax.optimization_barrier(jnp.sum(onehot_table * jnp.cumsum(onehot_table, axis=1), axis=-1)) - 1
    slot_index = (jnp.arange(blocks, dtype=jnp.int32)[:, None] * CAP + places).reshape(-1).astype(jnp.int32)
    expert_ids = route_rows.reshape(-1).astype(jnp.int32)
    source = jnp.arange(TOKENS * TOP, dtype=jnp.int32) // TOP
    inputs = jnp.zeros((EXPERTS, blocks * CAP, MODEL_WIDTH), jnp.float32).at[expert_ids, slot_index].set(act_two[source])
    inputs = low_back(inputs)
    gate_raw = low_back(jnp.einsum('erd,edf->erf', inputs, w_gate, precision=PRECISE))
    up_raw = low_back(jnp.einsum('erd,edf->erf', inputs, w_up, precision=PRECISE))
    inner_act = low(jax.nn.silu(gate_raw) * up_raw)
    result = both_round(jnp.einsum('erf,efd->erd', inner_act, w_down, precision=PRECISE))
    picked = result[expert_ids, slot_index].reshape(TOKENS, TOP, MODEL_WIDTH)
    return hidden + lax.optimization_barrier(jnp.sum(gate_values[:, :, None] * picked, axis=1))

def reference(tokens, teacher, segments, routes, route_weight, norm_attn, w_query, key_weight, value_weight, w_out, norm_ffn, w_router, w_gate, w_up, w_down):
    floats = tuple((array.astype(jnp.float32) for array in (tokens, norm_attn, w_query, key_weight, value_weight, w_out, norm_ffn, w_router, w_gate, w_up, w_down)))
    target = teacher.astype(jnp.float32)
    valid_rows = (segments.reshape(-1) != 0).astype(jnp.float32)
    weight_route = route_weight.astype(jnp.float32)

    def objective(*params):
        output = forward(*params, segments, routes, weight_route)
        difference = output - target
        square_error = jnp.sum(valid_rows[:, None] * difference * difference)
        return (0.5 * square_error, (output, square_error))
    objective_value, pullback, extra = jax.vjp(objective, *floats, has_aux=True)
    gradients = pullback(jnp.ones_like(objective_value))
    output, square_error = extra
    loss_value = square_error / (MODEL_WIDTH * jnp.sum(valid_rows))
    return (output, loss_value, gradients[0], gradients[1], gradients[2], gradients[3], gradients[4], gradients[5], gradients[6], gradients[7], gradients[8], gradients[9], gradients[10])
```

```python
import jax
import jax.numpy as jnp
from jax import lax
from jax.sharding import Mesh
from jax.sharding import PartitionSpec as P

QUERY_HEAD_COUNT = 24
KEY_VALUE_HEADS = 8
HEAD_WIDTH = 64
TOP = 2
EXPERTS = 16
CAPACITY = 96

EPSILON = 1e-06
MASKED = -1e30

BF = jnp.bfloat16
F32 = jnp.float32
RING = ("h", "x", "y")


def dot(left, right, left_dim, right_dim):
    return lax.dot_general(
        left, right, (((left_dim,), (right_dim,)), ((), ())), preferred_element_type=F32
    )


def rms_scale(values):
    return lax.rsqrt(jnp.mean(values * values, axis=-1, keepdims=True) + EPSILON)


def norm_back(values, scale, gain_row, upstream):
    gained = upstream * gain_row
    grad_gain = jnp.sum(upstream * values * scale, axis=0, keepdims=True)
    middle = jnp.mean(values * gained, axis=-1, keepdims=True)
    return (scale * gained - values * scale * scale * scale * middle, grad_gain)


def swap(value, axis):
    return lax.ppermute(value, axis, [(0, 1), (1, 0)])


def tensor_sum(partial):
    mine = partial.astype(BF)
    other = swap(mine, "t")
    return mine.astype(F32) + other.astype(F32)


def gather_rows(shard):
    rows, cols = shard.shape
    mine = lax.all_to_all(
        jnp.broadcast_to(shard[None], (32, rows, cols)), RING, 0, 0, tiled=True
    ).reshape(8, 4 * rows, cols)
    other = swap(mine, "c")
    first = lax.axis_index("c") == 0
    both = jnp.stack([jnp.where(first, mine, other), jnp.where(first, other, mine)], axis=1)
    return both.reshape(64 * rows, cols)


def scatter_sum(partial):
    total_rows, cols = partial.shape
    rows = total_rows // 64
    parts = partial.reshape(8, 2, 4 * rows, cols)
    core = lax.axis_index("c")
    mine = lax.dynamic_index_in_dim(parts, core, 1, keepdims=False)
    theirs = lax.dynamic_index_in_dim(parts, 1 - core, 1, keepdims=False)
    paired = (mine.astype(F32) + swap(theirs, "c").astype(F32)).astype(BF)
    moved = lax.all_to_all(paired.reshape(32, rows, cols), RING, 0, 0, tiled=True)
    return jnp.sum(moved.astype(F32), axis=0)


def exchange_slots(rows):
    width = rows.shape[1]
    return lax.all_to_all(
        rows.reshape(EXPERTS, -1, width), ("h", "x", "c"), 0, 0, tiled=True
    ).reshape(-1, width)


def split_bf16(value):
    high = value.astype(BF)
    return high, (value - high.astype(F32)).astype(BF)


def local(
    tokens,
    teacher,
    segments,
    routes,
    route_weight,
    norm_attn,
    w_query,
    key_weight,
    value_weight,
    w_out,
    norm_ffn,
    w_router,
    w_gate,
    w_up,
    w_down,
):
    tok_rows, feat_width = tokens.shape
    group = QUERY_HEAD_COUNT // KEY_VALUE_HEADS
    q_width = w_query.shape[1]
    k_width = key_weight.shape[1]
    tix = lax.axis_index("t")
    yix = lax.axis_index("y")

    rows24 = w_query.shape[0]
    small = jnp.concatenate(
        [
            w_router,
            norm_attn[:, None],
            norm_ffn[:, None],
            jnp.zeros((rows24, 128 - EXPERTS - 2), BF),
        ],
        axis=1,
    )
    pack_one = gather_rows(jnp.concatenate([w_query, key_weight, value_weight, small], axis=1))
    full_query = pack_one[:, :q_width]
    full_kv = pack_one[:, q_width : q_width + 2 * k_width]
    full_small = pack_one[:, q_width + 2 * k_width :]
    small_rows = dot(jnp.eye(24, 128, dtype=BF), full_small, 1, 1)
    router_rows = small_rows[:EXPERTS].astype(BF)
    gain_one = small_rows[EXPERTS : EXPERTS + 1]
    gain_two = small_rows[EXPERTS + 1 : EXPERTS + 2]
    wo_shard, pack_one = lax.optimization_barrier((w_out.T, pack_one))
    full_out = gather_rows(wo_shard)

    resid_in = tokens.astype(F32)
    scale_one = rms_scale(resid_in)
    act_one = (resid_in * scale_one * gain_one).astype(BF)
    kv_mine = dot(act_one, full_kv, 1, 0).astype(BF)
    query_rows = dot(act_one, full_query, 1, 0).astype(BF)
    kv_all = lax.all_to_all(
        jnp.broadcast_to(kv_mine[None], (4,) + kv_mine.shape), "y", 0, 0, tiled=True
    ).reshape(4 * tok_rows, 2 * k_width)

    experts = jnp.stack([w_gate[0], w_up[0], w_down[0].T])
    experts_other = swap(experts, "t")
    experts_full = jnp.concatenate(
        [
            jnp.where(tix == 0, experts, experts_other),
            jnp.where(tix == 0, experts_other, experts),
        ],
        axis=2,
    )
    experts_full, kv_all = lax.optimization_barrier((experts_full, kv_all))
    gate_full = lax.all_gather(experts_full[0], "y", axis=0, tiled=True)
    up_full = lax.all_gather(experts_full[1], "y", axis=0, tiled=True)
    down_full = lax.all_gather(experts_full[2], "y", axis=0, tiled=True)

    seq_len = kv_all.shape[0]
    kv_heads = k_width // HEAD_WIDTH
    head_scale = HEAD_WIDTH ** (-0.5)
    first_row = yix * tok_rows
    seg_all = segments[0]
    seg_mine = lax.dynamic_slice_in_dim(seg_all, first_row, tok_rows)
    query_pos = first_row + jnp.arange(tok_rows, dtype=jnp.int32)
    key_pos = jnp.arange(seq_len, dtype=jnp.int32)
    allowed = (seg_mine[:, None] == seg_all[None, :]) & (key_pos[None, :] <= query_pos[:, None])
    query_heads = query_rows.reshape(tok_rows, kv_heads, group, HEAD_WIDTH).transpose(1, 0, 2, 3)
    key_heads = kv_all[:, :k_width].reshape(seq_len, kv_heads, HEAD_WIDTH).transpose(1, 0, 2)
    value_heads = kv_all[:, k_width:].reshape(seq_len, kv_heads, HEAD_WIDTH).transpose(1, 0, 2)

    def score_block(query_one, key_one):
        raw_scores = (
            jnp.einsum("tgd,sd->gts", query_one, key_one, preferred_element_type=F32) * head_scale
        )
        return jnp.where(allowed[None], raw_scores, MASKED)

    def head_forward(pieces):
        query_one, key_one, value_one = pieces
        scores = score_block(query_one, key_one)
        row_max = jnp.max(scores, axis=-1, keepdims=True)
        exp_scores = jnp.exp(scores - row_max)
        row_total = jnp.sum(exp_scores, axis=-1, keepdims=True)
        weights = (exp_scores / row_total).astype(BF)
        mixed_one = jnp.einsum("gts,sd->tgd", weights, value_one, preferred_element_type=F32)
        return (mixed_one.astype(BF), row_max + jnp.log(row_total))

    mixed_stack, log_total = lax.map(head_forward, (query_heads, key_heads, value_heads))
    mixed = mixed_stack.transpose(1, 0, 2, 3).reshape(tok_rows, -1)
    hidden = resid_in + tensor_sum(dot(mixed, full_out, 1, 1))
    scale_two = rms_scale(hidden)
    act_two = (hidden * scale_two * gain_two).astype(BF)

    logits = dot(router_rows, act_two, 1, 1)
    router = jax.nn.softmax(logits, axis=0)
    route_cols = routes.T
    weight_cols = route_weight.T
    expert_iota = lax.broadcasted_iota(jnp.int32, (EXPERTS, tok_rows), 0)
    named = [expert_iota == route_cols[k : k + 1] for k in range(TOP)]
    taken = (named[0] | named[1]).astype(BF)
    earlier = (
        lax.broadcasted_iota(jnp.int32, (tok_rows, tok_rows), 0)
        < lax.broadcasted_iota(jnp.int32, (tok_rows, tok_rows), 1)
    ).astype(BF)
    count_before = dot(taken, earlier, 1, 0)
    half = CAPACITY // 2
    slot_iota = lax.broadcasted_iota(jnp.int32, (EXPERTS * half, tok_rows), 0)
    picks = []
    gates = []
    for k in range(TOP):
        place = jnp.sum(jnp.where(named[k], count_before, 0.0), axis=0, keepdims=True)
        place = place.astype(jnp.int32) - tix * half
        slot = jnp.where((place >= 0) & (place < half), route_cols[k : k + 1] * half + place, -1)
        picks.append(slot_iota == slot)
        chosen = jnp.sum(jnp.where(named[k], router, 0.0), axis=0, keepdims=True)
        gates.append(chosen * weight_cols[k : k + 1])
    pick = (picks[0] | picks[1]).astype(BF)
    gated_pick = (
        jnp.where(picks[0], gates[0], 0.0) + jnp.where(picks[1], gates[1], 0.0)
    ).astype(BF)

    received = exchange_slots(dot(pick, act_two, 1, 0).astype(BF))
    gate_proj = dot(received, gate_full, 1, 0)
    up_proj = dot(received, up_full, 1, 0)
    inner = (jax.nn.silu(gate_proj) * up_proj).astype(BF)
    returned = exchange_slots(dot(inner, down_full, 1, 1).astype(BF))
    output = hidden + tensor_sum(dot(gated_pick, returned, 0, 0))

    valid = (seg_mine != 0).astype(F32)
    difference = output - teacher.astype(F32)
    grad_output = difference * valid[:, None]
    sse = jnp.sum(grad_output * difference)
    count = jnp.sum(valid)

    grad_output_low = grad_output.astype(BF)
    d_received = exchange_slots(dot(gated_pick, grad_output_low, 1, 0).astype(BF))
    slot_dots = dot(returned, grad_output_low, 1, 1)
    d_gates = jnp.concatenate(
        [jnp.sum(jnp.where(picks[k], slot_dots, 0.0), axis=0, keepdims=True) for k in range(TOP)]
    )
    d_gates = d_gates + swap(d_gates, "t")
    d_inner = dot(d_received, down_full, 1, 0)
    sig_gate = jax.nn.sigmoid(gate_proj)
    d_gate_proj = (d_inner * up_proj * sig_gate * (1.0 + gate_proj * (1.0 - sig_gate))).astype(BF)
    d_up_proj = (d_inner * gate_proj * sig_gate).astype(BF)
    d_slots = dot(d_gate_proj, gate_full, 1, 1) + dot(d_up_proj, up_full, 1, 1)
    d_returned = exchange_slots(d_slots.astype(BF))

    grad_experts = [
        lax.psum_scatter(part, "y", scatter_dimension=0, tiled=True)
        for part in (
            dot(received, d_gate_proj, 0, 0).astype(BF),
            dot(received, d_up_proj, 0, 0).astype(BF),
            dot(d_received, inner, 0, 0).astype(BF),
        )
    ]
    grad_stack = jnp.stack(grad_experts)
    ff_half = grad_stack.shape[2] // 2
    keep = jnp.where(tix == 0, grad_stack[:, :, :ff_half], grad_stack[:, :, ff_half:])
    give = jnp.where(tix == 0, grad_stack[:, :, ff_half:], grad_stack[:, :, :ff_half])
    grad_stack = keep.astype(F32) + swap(give, "t").astype(F32)

    d_router = jnp.where(named[0], d_gates[0:1] * weight_cols[0:1], 0.0) + jnp.where(
        named[1], d_gates[1:2] * weight_cols[1:2], 0.0
    )
    d_logits = (
        router * (d_router - jnp.sum(router * d_router, axis=0, keepdims=True))
    ).astype(BF)
    grad_router = dot(act_two, d_logits, 0, 1)
    d_act_two = tensor_sum(dot(pick, d_returned, 0, 0)) + dot(d_logits, router_rows, 0, 0)
    d_norm_two, grad_gain_two = norm_back(hidden, scale_two, gain_two, d_act_two)
    d_hidden = grad_output + d_norm_two
    d_attn = d_hidden.astype(BF)
    d_mixed = dot(d_attn, full_out, 1, 0).astype(BF)
    grad_out = dot(d_attn, mixed, 0, 0)

    sse_high, sse_low = split_bf16(jnp.full((1, feat_width), sse))
    count_high, count_low = split_bf16(jnp.full((1, feat_width), count))
    gain_high, gain_low = split_bf16(grad_gain_two)
    lines = jnp.concatenate(
        [gain_high, gain_low, sse_high, sse_low, count_high, count_low, jnp.zeros((2, feat_width), BF)]
    )
    extra = dot(lines, jnp.eye(8, 128 - EXPERTS, dtype=BF), 0, 0)
    summed_one = scatter_sum(jnp.concatenate([grad_out, grad_router, extra], axis=1).astype(BF))
    at = feat_width // 2
    own_out = summed_one[:, :at].T
    own_router = summed_one[:, at : at + EXPERTS]
    at = at + EXPERTS
    own_gain_two = summed_one[:, at] + summed_one[:, at + 1]
    loss_value = (summed_one[0, at + 2] + summed_one[0, at + 3]) / (
        feat_width * (summed_one[0, at + 4] + summed_one[0, at + 5])
    )

    d_heads = d_mixed.reshape(tok_rows, kv_heads, group, HEAD_WIDTH).transpose(1, 0, 2, 3)

    def head_backward(pieces):
        query_one, key_one, value_one, d_one, total_one = pieces
        scores = score_block(query_one, key_one)
        weights = jnp.exp(scores - total_one)
        d_weights = jnp.einsum("tgd,sd->gts", d_one, value_one, preferred_element_type=F32)
        row_dot = jnp.sum(weights * d_weights, axis=-1, keepdims=True)
        d_scores = (weights * (d_weights - row_dot)).astype(BF)
        d_query_one = (
            jnp.einsum("gts,sd->tgd", d_scores, key_one, preferred_element_type=F32) * head_scale
        ).astype(BF)
        d_key_one = (
            jnp.einsum("gts,tgd->sd", d_scores, query_one, preferred_element_type=F32) * head_scale
        )
        d_value_one = jnp.einsum(
            "gts,tgd->sd", weights.astype(BF), d_one, preferred_element_type=F32
        )
        return (d_query_one, d_key_one.astype(BF), d_value_one.astype(BF))

    d_query_stack, d_key_stack, d_value_stack = lax.map(
        head_backward, (query_heads, key_heads, value_heads, d_heads, log_total)
    )
    d_query = d_query_stack.transpose(1, 0, 2, 3).reshape(tok_rows, -1)
    d_kv = jnp.concatenate(
        [
            d_key_stack.transpose(1, 0, 2).reshape(seq_len, -1),
            d_value_stack.transpose(1, 0, 2).reshape(seq_len, -1),
        ],
        axis=1,
    )
    d_kv_parts = lax.all_to_all(d_kv.reshape(4, tok_rows, -1), "y", 0, 0, tiled=True)
    d_kv_mine = jnp.sum(d_kv_parts.astype(F32), axis=0).astype(BF)
    own_query = scatter_sum(dot(act_one, d_query, 0, 0).astype(BF))

    d_act_one = tensor_sum(dot(d_query, full_query, 1, 1) + dot(d_kv_mine, full_kv, 1, 1))
    d_norm_one, grad_gain_one = norm_back(resid_in, scale_one, gain_one, d_act_one)
    grad_tokens = d_hidden + d_norm_one
    gain_high, gain_low = split_bf16(grad_gain_one)
    lines = jnp.concatenate([gain_high, gain_low, jnp.zeros((6, feat_width), BF)])
    extra = dot(lines, jnp.eye(8, 128, dtype=BF), 0, 0)
    own_kv = scatter_sum(
        jnp.concatenate([dot(act_one, d_kv_mine, 0, 0), extra], axis=1).astype(BF)
    )
    own_gain_one = own_kv[:, 2 * k_width] + own_kv[:, 2 * k_width + 1]
    return (
        output,
        loss_value,
        grad_tokens,
        own_gain_one,
        own_query,
        own_kv[:, :k_width],
        own_kv[:, k_width : 2 * k_width],
        own_out,
        own_gain_two,
        own_router,
        grad_stack[0][None],
        grad_stack[1][None],
        grad_stack[2].T[None],
    )


def solution(mesh):
    fine = Mesh(mesh.devices.reshape(2, 4, 2, 4, 2), ("h", "x", "c", "y", "t"))
    fsdp = ("h", "x", "c")
    every = ("h", "x", "c", "y")
    return jax.shard_map(
        local,
        mesh=fine,
        in_specs=(
            P(every, None),
            P(every, None),
            P(fsdp, None),
            P(every, None),
            P(every, None),
            P(every),
            P(every, "t"),
            P(every, "t"),
            P(every, "t"),
            P("t", every),
            P(every),
            P(every, None),
            P(fsdp, "y", "t"),
            P(fsdp, "y", "t"),
            P(fsdp, "t", "y"),
        ),
        out_specs=(
            P(every, None),
            P(),
            P(every, None),
            P(every),
            P(every, "t"),
            P(every, "t"),
            P(every, "t"),
            P("t", every),
            P(every),
            P(every, None),
            P(fsdp, "y", "t"),
            P(fsdp, "y", "t"),
            P(fsdp, "t", "y"),
        ),
        check_vma=False,
    )
```

```python
import functools

import jax
import jax.numpy as jnp
from jax import lax
from jax.experimental import pallas as pl
from jax.experimental.pallas import tpu as pltpu
from jax.sharding import Mesh
from jax.sharding import PartitionSpec as P

QUERY_HEAD_COUNT = 24
KEY_VALUE_HEADS = 8
HEAD_WIDTH = 64
TOP = 2
EXPERTS = 16
CAPACITY = 96

EPSILON = 1e-06
MASKED = -1e30

BF = jnp.bfloat16
F32 = jnp.float32
RING = ("h", "x", "y")
GROUP = QUERY_HEAD_COUNT // KEY_VALUE_HEADS
SPAN = 512
HALF = 256


def dot(left, right, left_dim, right_dim):
    return lax.dot_general(
        left, right, (((left_dim,), (right_dim,)), ((), ())), preferred_element_type=F32
    )


def rms_scale(values):
    return lax.rsqrt(jnp.mean(values * values, axis=-1, keepdims=True) + EPSILON)


def norm_back(values, scale, gain_row, upstream):
    gained = upstream * gain_row
    grad_gain = jnp.sum(upstream * values * scale, axis=0, keepdims=True)
    middle = jnp.mean(values * gained, axis=-1, keepdims=True)
    return (scale * gained - values * scale * scale * scale * middle, grad_gain)


def swap(value, axis):
    return lax.ppermute(value, axis, [(0, 1), (1, 0)])


def both(mine, other):
    return mine.astype(F32) + other.astype(F32)


def ring_gather(shard):
    rows, cols = shard.shape
    return lax.all_to_all(jnp.broadcast_to(shard[None], (32, rows, cols)), RING, 0, 0, tiled=True)


def core_gather(mine):
    rows, cols = mine.shape[1:]
    mine = mine.reshape(8, 4 * rows, cols)
    other = swap(mine, "c")
    first = lax.axis_index("c") == 0
    pair = jnp.stack([jnp.where(first, mine, other), jnp.where(first, other, mine)], axis=1)
    return pair.reshape(64 * rows, cols)


def after(value, *earlier):
    return lax.optimization_barrier((value,) + earlier)[0]


def pair_sum(partial):
    total_rows, cols = partial.shape
    rows = total_rows // 64
    parts = partial.reshape(8, 2, 4 * rows, cols)
    core = lax.axis_index("c")
    mine = lax.dynamic_index_in_dim(parts, core, 1, keepdims=False)
    theirs = lax.dynamic_index_in_dim(parts, 1 - core, 1, keepdims=False)
    paired = (mine.astype(F32) + swap(theirs, "c").astype(F32)).astype(BF)
    return paired.reshape(32, rows, cols)


def ring_sum(paired):
    moved = lax.all_to_all(paired, RING, 0, 0, tiled=True)
    return jnp.sum(moved.astype(F32), axis=0)


def axis_parts(parts, axis, size):
    me = lax.axis_index(axis)
    mine = [lax.dynamic_index_in_dim(parts, me, 0, keepdims=False)]
    for r in range(1, size):
        block = lax.dynamic_index_in_dim(parts, (me + r) % size, 0, keepdims=False)
        mine.append(lax.ppermute(block, axis, [(i, (i + r) % size) for i in range(size)]))
    return mine


def added(parts):
    total = parts[0].astype(F32)
    for part in parts[1:]:
        total = total + part.astype(F32)
    return total


def y_parts(paired):
    rows, cols = paired.shape[1:]
    return axis_parts(paired.reshape(8, 4, rows, cols).transpose(1, 0, 2, 3), "y", 4)


def hx_sum(parts):
    by_y = added(parts).astype(BF)
    by_h = added(axis_parts(by_y.reshape(2, 4, *by_y.shape[1:]), "h", 2)).astype(BF)
    return added(axis_parts(by_h, "x", 4))


def exchange_slots(rows):
    width = rows.shape[1]
    return lax.all_to_all(
        rows.reshape(EXPERTS, -1, width), ("h", "x", "c"), 0, 0, tiled=True
    ).reshape(-1, width)


def nn(a,b):
    return lax.dot_general(a,b,(((1,),(0,)),((),())),preferred_element_type=F32)

def fold(v, op):
    return op(v.reshape(v.shape[0]//8,8,v.shape[1]),axis=0)

def write_bias(bias, seg_q, seg_k, y, half):
    width = bias.shape[2]
    for r in range(4):

        def one(r=r):
            same = seg_k[r * SPAN : (r + 1) * SPAN, :] == seg_q[...]
            if r == 0:
                key_place = lax.broadcasted_iota(jnp.int32, (SPAN, width), 0)
                query_place = lax.broadcasted_iota(jnp.int32, (SPAN, width), 1) + half * HALF
                same = same & (key_place <= query_place)
            bias[r] = jnp.where(same, 0.0, MASKED)

        pl.when(y >= r)(one)


def fwd_kernel(
    half, y_ref, q_ref, kv0, kv1, kv2, kv3, seg_q, seg_k, o_ref, lse_ref, bias, kn, vt, sc
):
    y = y_ref[0]

    @pl.when(pl.program_id(0) == 0)
    def _():
        write_bias(bias, seg_q, seg_k, y, half)

    for r, kv in enumerate((kv0, kv1, kv2, kv3)):

        def fill(r=r, kv=kv):
            kn[r] = kv[0].T
            vt[r] = kv[1]

        pl.when(y >= r)(fill)
    scale = jnp.asarray(HEAD_WIDTH**-0.5, BF)
    qs = [q_ref[h * HEAD_WIDTH : (h + 1) * HEAD_WIDTH] * scale for h in range(GROUP)]

    def scores(r, rows, tops):
        out = []
        for h in range(GROUP):
            s = nn(kn[r, rows, :], qs[h]) + bias[r, rows, :]
            sc[h, r, rows, :] = s
            out.append(jnp.maximum(tops[h], fold(s, jnp.max)))
        return tuple(out)

    own = slice(0, (half + 1) * HALF)
    low = tuple(jnp.full((8, HALF), MASKED, F32) for _ in range(GROUP))
    tops = scores(0, own, low)
    tops = lax.fori_loop(1, y + 1, lambda r, t: scores(r, slice(0, SPAN), t), tops)
    tops = [jnp.max(t, axis=0, keepdims=True) for t in tops]

    def mix(r, rows, carry):
        out = []
        for h in range(GROUP):
            total, acc = carry[h]
            p = jnp.exp(sc[h, r, rows, :] - tops[h])
            out.append((total + fold(p, jnp.sum), acc + nn(vt[r, :, rows], p.astype(BF))))
        return tuple(out)

    zero = tuple(
        (jnp.zeros((8, HALF), F32), jnp.zeros((HEAD_WIDTH, HALF), F32)) for _ in range(GROUP)
    )
    carry = mix(0, own, zero)
    carry = lax.fori_loop(1, y + 1, lambda r, c: mix(r, slice(0, SPAN), c), carry)
    for h in range(GROUP):
        total = jnp.sum(carry[h][0], axis=0, keepdims=True)
        o_ref[h * HEAD_WIDTH : (h + 1) * HEAD_WIDTH, :] = (carry[h][1] / total).astype(BF)
        lse_ref[0, h : h + 1, :] = tops[h] + jnp.log(total)


def attend(half, y, q_t, kvs, seg_q, seg_k):
    rows = GROUP * HEAD_WIDTH
    heads = q_t.shape[0] // rows
    kv_spec = pl.BlockSpec((2, HEAD_WIDTH, SPAN), lambda g: (0, g, 0))
    return pl.pallas_call(
        functools.partial(fwd_kernel, half),
        grid=(heads,),
        in_specs=[
            pl.BlockSpec(memory_space=pltpu.SMEM),
            pl.BlockSpec((rows, HALF), lambda g: (g, half)),
            kv_spec,
            kv_spec,
            kv_spec,
            kv_spec,
            pl.BlockSpec((1, HALF), lambda g: (0, half)),
            pl.BlockSpec((4 * SPAN, 1), lambda g: (0, 0)),
        ],
        out_specs=[
            pl.BlockSpec((rows, HALF), lambda g: (g, 0)),
            pl.BlockSpec((1, 8, HALF), lambda g: (g, 0, 0)),
        ],
        out_shape=[
            jax.ShapeDtypeStruct((q_t.shape[0], HALF), BF),
            jax.ShapeDtypeStruct((heads, 8, HALF), F32),
        ],
        scratch_shapes=[
            pltpu.VMEM((4, SPAN, HALF), F32),
            pltpu.VMEM((4, SPAN, HEAD_WIDTH), BF),
            pltpu.VMEM((4, HEAD_WIDTH, SPAN), BF),
            pltpu.VMEM((GROUP, 4, SPAN, HALF), F32),
        ],
        compiler_params=pltpu.CompilerParams(vmem_limit_bytes=40 << 20),
        cost_estimate=pl.CostEstimate(
            flops=14_000_000_000, bytes_accessed=6_000_000, transcendentals=6_000_000
        ),
    )(y, q_t, *kvs, seg_q, seg_k)


def bwd_kernel(y_ref, q_ref, d_ref, o_0, o_1, lse_0, lse_1, kv0, kv1, kv2, kv3, seg_q, seg_k, dq_ref, g0, g1, g2, g3, bias, kn, vn, kt, dk, dv):
    y = y_ref[0]
    @pl.when(pl.program_id(0)==0)
    def _(): write_bias(bias, seg_q, seg_k, y, 0)
    for r,kv in enumerate((kv0,kv1,kv2,kv3)):
        def fill(r=r,kv=kv):
            kn[r] = kv[0].T
            vn[r] = kv[1].T
            kt[r] = kv[0]
        pl.when(y>=r)(fill)
    dk[...] = jnp.zeros_like(dk); dv[...] = jnp.zeros_like(dv)
    scale = jnp.asarray(HEAD_WIDTH**-0.5, BF)
    for b in range(2):
        cols = slice(b*HALF,(b+1)*HALF)
        qs, qn, ds, dn, dots, lses = [],[],[],[],[],[]
        for h in range(GROUP):
            hr = slice(h*HEAD_WIDTH,(h+1)*HEAD_WIDTH)
            q = q_ref[hr, cols]*scale
            qs.append(q); qn.append(q.T)
            d = d_ref[hr, cols]
            ds.append(d); dn.append(d.T)
            dots.append(jnp.sum(d.astype(F32)*(o_0, o_1)[b][hr].astype(F32),axis=0,keepdims=True))
            lses.append((lse_0, lse_1)[b][0, h : h + 1])
        def step(r, rows, carry):
            out=[]; sum_k=None; sum_v=None
            for h in range(GROUP):
                s = nn(kn[r, rows, :], qs[h]) + bias[r, rows, cols]
                p = jnp.exp(s - lses[h])
                pv = nn(p.astype(BF), dn[h])
                dp = nn(vn[r, rows, :], ds[h])
                dsc = (p*(dp - dots[h])).astype(BF)
                pk = nn(dsc, qn[h])
                out.append(carry[h] + nn(kt[r,:,rows], dsc))
                sum_k = pk if sum_k is None else sum_k+pk
                sum_v = pv if sum_v is None else sum_v+pv
            dk[r, rows, :] += sum_k
            dv[r, rows, :] += sum_v
            return tuple(out)
        carry = step(0, slice(0,(b+1)*HALF), tuple(jnp.zeros((HEAD_WIDTH,HALF),F32) for _ in range(GROUP)))
        carry = lax.fori_loop(1, y+1, lambda r,c: step(r, slice(0,SPAN), c), carry)
        for h in range(GROUP):
            dq_ref[h*HEAD_WIDTH:(h+1)*HEAD_WIDTH, cols] = (carry[h]*HEAD_WIDTH**-0.5).astype(BF)
    for r,g in enumerate((g0,g1,g2,g3)):
        g[0] = dk[r].T.astype(BF)
        g[1] = dv[r].T.astype(BF)

def attend_back(first, count, y, q_t, d_t, outs, lses, kvs, seg_q, seg_k):
    rows = GROUP * HEAD_WIDTH
    kv_spec = pl.BlockSpec((2, HEAD_WIDTH, SPAN), lambda g: (0, first + g, 0))
    q_spec = pl.BlockSpec((rows, SPAN), lambda g: (first + g, 0))
    o_spec = pl.BlockSpec((rows, HALF), lambda g: (first + g, 0))
    lse_spec = pl.BlockSpec((1, 8, HALF), lambda g: (first + g, 0, 0))
    kv_shape = jax.ShapeDtypeStruct((2, count * HEAD_WIDTH, SPAN), BF)
    return pl.pallas_call(
        bwd_kernel,
        grid=(count,),
        in_specs=[pl.BlockSpec(memory_space=pltpu.SMEM), q_spec, q_spec]
        + [o_spec, o_spec, lse_spec, lse_spec]
        + [kv_spec] * 4
        + [pl.BlockSpec((1, SPAN), lambda g: (0, 0)), pl.BlockSpec((4 * SPAN, 1), lambda g: (0, 0))],
        out_specs=[pl.BlockSpec((rows, SPAN), lambda g: (g, 0))]
        + [pl.BlockSpec((2, HEAD_WIDTH, SPAN), lambda g: (0, g, 0))] * 4,
        out_shape=[jax.ShapeDtypeStruct((count * rows, SPAN), BF)] + [kv_shape] * 4,
        scratch_shapes=[pltpu.VMEM((4, SPAN, SPAN), F32)]
        + [pltpu.VMEM((4, SPAN, HEAD_WIDTH), BF)] * 2
        + [pltpu.VMEM((4, HEAD_WIDTH, SPAN), BF)]
        + [pltpu.VMEM((4, SPAN, HEAD_WIDTH), F32)] * 2,
        compiler_params=pltpu.CompilerParams(vmem_limit_bytes=40 << 20),
        cost_estimate=pl.CostEstimate(
            flops=28_000_000_000, bytes_accessed=6_000_000, transcendentals=6_000_000
        ),
    )(y, q_t, d_t, *outs, *lses, *kvs, seg_q, seg_k)


def split_bf16(value):
    high = value.astype(BF)
    return high, (value - high.astype(F32)).astype(BF)


def local(
    tokens,
    teacher,
    segments,
    routes,
    route_weight,
    norm_attn,
    w_query,
    key_weight,
    value_weight,
    w_out,
    norm_ffn,
    w_router,
    w_gate,
    w_up,
    w_down,
):
    tok_rows, feat_width = tokens.shape
    q_width = w_query.shape[1]
    k_width = key_weight.shape[1]
    tix = lax.axis_index("t")
    yix = lax.axis_index("y")

    small = jnp.concatenate(
        [
            w_router,
            norm_attn[:, None],
            norm_ffn[:, None],
            jnp.zeros((w_router.shape[0], 128 - EXPERTS - 2), BF),
        ],
        axis=1,
    )
    ring_kv = ring_gather(jnp.concatenate([key_weight, value_weight, small], axis=1))
    pack_kv = core_gather(ring_kv)
    ring_rest = ring_gather(jnp.concatenate([w_query, w_out.T], axis=1))
    full_kv = pack_kv[:, : 2 * k_width]
    full_small = pack_kv[:, 2 * k_width :]
    small_rows = dot(jnp.eye(24, 128, dtype=BF), full_small, 1, 1)
    router_rows = small_rows[:EXPERTS].astype(BF)
    gain_one = small_rows[EXPERTS : EXPERTS + 1]
    gain_two = small_rows[EXPERTS + 1 : EXPERTS + 2]

    resid_in = tokens.astype(F32)
    scale_one = rms_scale(resid_in)
    act_one = (resid_in * scale_one * gain_one).astype(BF)
    kv_mine = dot(full_kv, act_one, 0, 1).astype(BF).reshape(2, k_width, tok_rows)
    kvs = [kv_mine] + [
        lax.ppermute(kv_mine, "y", [(i, i + r) for i in range(4 - r)]) for r in (1, 2, 3)
    ]
    kvs[1:] = lax.optimization_barrier((*kvs[1:], ring_rest))[:3]
    pack_rest = core_gather(ring_rest)
    full_query = pack_rest[:, :q_width]
    full_out = pack_rest[:, q_width:]
    query_t = dot(full_query, act_one, 0, 1).astype(BF)

    experts = jnp.stack([w_gate[0], w_up[0], w_down[0].T])
    experts_other = after(swap(after(experts, kv_mine), "t"), kvs[1], kvs[2], kvs[3])
    experts_full = jnp.concatenate(
        [
            jnp.where(tix == 0, experts, experts_other),
            jnp.where(tix == 0, experts_other, experts),
        ],
        axis=2,
    )
    gate_full = lax.all_gather(experts_full[0], "y", axis=0, tiled=True)
    up_full = lax.all_gather(experts_full[1], "y", axis=0, tiled=True)
    down_full = lax.all_gather(experts_full[2], "y", axis=0, tiled=True)

    seg_blocks = segments[0].reshape(4, tok_rows)
    seg_mine = lax.dynamic_index_in_dim(seg_blocks, yix, 0, keepdims=False)
    seg_keys = jnp.concatenate(
        [lax.dynamic_index_in_dim(seg_blocks, (yix + 4 - r) % 4, 0, keepdims=False) for r in range(4)]
    )[:, None]
    place_y = jnp.full((1,), yix, jnp.int32)
    mixed_0, log_0 = attend(0, place_y, query_t, kvs, seg_mine[None], seg_keys)
    part_0 = dot(mixed_0, full_out, 0, 1).astype(BF)
    mixed_1, log_1 = attend(1, place_y, after(query_t, part_0), kvs, seg_mine[None], seg_keys)
    other_0 = swap(part_0, "t")
    part_1 = dot(after(mixed_1, other_0), full_out, 0, 1).astype(BF)
    other_1 = swap(part_1, "t")
    hidden = resid_in + jnp.concatenate([both(part_0, other_0), both(part_1, other_1)])
    scale_two = rms_scale(hidden)
    act_two = (hidden * scale_two * gain_two).astype(BF)

    logits = dot(router_rows, act_two, 1, 1)
    router = jax.nn.softmax(logits, axis=0)
    route_cols = routes.T
    weight_cols = route_weight.T
    expert_iota = lax.broadcasted_iota(jnp.int32, (EXPERTS, tok_rows), 0)
    named = [expert_iota == route_cols[k : k + 1] for k in range(TOP)]
    taken = (named[0] | named[1]).astype(BF)
    earlier = (
        lax.broadcasted_iota(jnp.int32, (tok_rows, tok_rows), 0)
        < lax.broadcasted_iota(jnp.int32, (tok_rows, tok_rows), 1)
    ).astype(BF)
    count_before = dot(taken, earlier, 1, 0)
    half = CAPACITY // 2
    slot_iota = lax.broadcasted_iota(jnp.int32, (EXPERTS * half, tok_rows), 0)
    picks = []
    gates = []
    for k in range(TOP):
        place = jnp.sum(jnp.where(named[k], count_before, 0.0), axis=0, keepdims=True)
        place = place.astype(jnp.int32) - tix * half
        slot = jnp.where((place >= 0) & (place < half), route_cols[k : k + 1] * half + place, -1)
        picks.append(slot_iota == slot)
        chosen = jnp.sum(jnp.where(named[k], router, 0.0), axis=0, keepdims=True)
        gates.append(chosen * weight_cols[k : k + 1])
    pick = (picks[0] | picks[1]).astype(BF)
    gated_pick = (
        jnp.where(picks[0], gates[0], 0.0) + jnp.where(picks[1], gates[1], 0.0)
    ).astype(BF)

    received = exchange_slots(dot(pick, act_two, 1, 0).astype(BF))
    gate_proj = dot(received, gate_full, 1, 0)
    up_proj = dot(received, up_full, 1, 0)
    inner = (jax.nn.silu(gate_proj) * up_proj).astype(BF)

    returned = exchange_slots(dot(inner, down_full, 1, 1).astype(BF))
    part = dot(gated_pick, returned, 0, 0).astype(BF)
    output = hidden + both(part, swap(part, "t"))
    valid = (seg_mine != 0).astype(F32)
    difference = output - teacher.astype(F32)
    grad_output = difference * valid[:, None]
    sse = jnp.sum(grad_output * difference)
    count = jnp.sum(valid)
    grad_low = grad_output.astype(BF)
    d_received = exchange_slots(dot(gated_pick, grad_low, 1, 0).astype(BF))

    slot_dots = dot(returned, grad_low, 1, 1)
    d_gates = jnp.concatenate(
        [jnp.sum(jnp.where(picks[k], slot_dots, 0.0), axis=0, keepdims=True) for k in range(TOP)]
    )
    d_gates_other = swap(d_gates, "t")
    d_received = after(d_received, d_gates_other)
    d_gates = d_gates + d_gates_other

    d_inner = dot(d_received, down_full, 1, 0)
    sig_gate = jax.nn.sigmoid(gate_proj)
    d_gate_proj = (d_inner * up_proj * sig_gate * (1.0 + gate_proj * (1.0 - sig_gate))).astype(BF)
    d_up_proj = (d_inner * gate_proj * sig_gate).astype(BF)
    d_slots = dot(d_gate_proj, gate_full, 1, 1) + dot(d_up_proj, up_full, 1, 1)
    d_returned = exchange_slots(d_slots.astype(BF))

    grad_parts = [
        dot(received, d_gate_proj, 0, 0).astype(BF),
        dot(received, d_up_proj, 0, 0).astype(BF),
        dot(d_received, inner, 0, 0).astype(BF),
    ]
    grad_experts = [
        lax.psum_scatter(part, "y", scatter_dimension=0, tiled=True) for part in grad_parts
    ]
    d_returned = after(d_returned, *grad_parts)
    grad_stack = jnp.stack(grad_experts)
    ff_half = grad_stack.shape[2] // 2
    keep = jnp.where(tix == 0, grad_stack[:, :, :ff_half], grad_stack[:, :, ff_half:])
    give = jnp.where(tix == 0, grad_stack[:, :, ff_half:], grad_stack[:, :, :ff_half])

    d_router = jnp.where(named[0], d_gates[0:1] * weight_cols[0:1], 0.0) + jnp.where(
        named[1], d_gates[1:2] * weight_cols[1:2], 0.0
    )
    d_logits = (
        router * (d_router - jnp.sum(router * d_router, axis=0, keepdims=True))
    ).astype(BF)
    grad_router = dot(act_two, d_logits, 0, 1)
    d_route = dot(d_logits, router_rows, 0, 0)
    part = dot(pick, d_returned, 0, 0).astype(BF)
    d_act_two = d_route + both(part, after(swap(part, "t"), d_route, grad_router))
    d_norm_two, grad_gain_two = norm_back(hidden, scale_two, gain_two, d_act_two)
    d_hidden = grad_output + d_norm_two
    d_attn = d_hidden.astype(BF)
    d_mixed_t = dot(full_out, d_attn, 0, 1).astype(BF)

    sse_high, sse_low = split_bf16(jnp.full((1, feat_width), sse))
    count_high, count_low = split_bf16(jnp.full((1, feat_width), count))
    gain_high, gain_low = split_bf16(grad_gain_two)
    lines = jnp.concatenate(
        [gain_high, gain_low, sse_high, sse_low, count_high, count_low, jnp.zeros((2, feat_width), BF)]
    )
    extra = dot(lines, jnp.eye(8, 128 - EXPERTS, dtype=BF), 0, 0)
    rest_small = jnp.concatenate([grad_router, extra], axis=1).astype(BF)

    saved = (d_mixed_t, (mixed_0, mixed_1), (log_0, log_1), kvs, seg_mine[None], seg_keys)

    def ring_back(parts):
        return [
            lax.ppermute(parts[r], "y", [(i, i - r) for i in range(r, 4)]) for r in (1, 2, 3)
        ]

    kv_groups = k_width // HEAD_WIDTH
    back_0 = attend_back(0, kv_groups // 2, place_y, query_t, *saved)
    others_0 = ring_back(back_0[1:])
    back_1 = attend_back(
        kv_groups // 2, kv_groups // 2, place_y, after(query_t, back_0[0]), *saved
    )
    back_1 = lax.optimization_barrier((*back_1, *others_0))[:5]
    others_1 = ring_back(back_1[1:])
    d_query_t = jnp.concatenate([back_0[0], back_1[0]])
    grad_out = dot(
        after(d_attn, d_query_t), jnp.concatenate([mixed_0, mixed_1], axis=1), 0, 1
    ).astype(BF)
    grad_query = dot(act_one, d_query_t, 0, 1).astype(BF)
    parts_one = y_parts(pair_sum(jnp.concatenate([grad_out, rest_small, grad_query], axis=1)))
    grad_stack = keep.astype(F32) + swap(after(give, d_query_t), "t").astype(F32)
    own_down = grad_stack[2].T
    d_kv_t = jnp.concatenate(
        [
            added([own, *moved])
            for own, moved in ((back_0[1], others_0), (back_1[1], others_1))
        ],
        axis=1,
    ).reshape(2 * k_width, tok_rows).astype(BF)
    d_act_part = dot(d_query_t, full_query, 0, 1) + dot(d_kv_t, full_kv, 0, 1)
    part = after(d_act_part.astype(BF), grad_stack)
    other = swap(part, "t")
    gain_high, gain_low = split_bf16(
        jnp.sum(d_act_part * resid_in * scale_one, axis=0, keepdims=True)
    )
    lines = jnp.concatenate([gain_high, gain_low, jnp.zeros((6, feat_width), BF)])
    extra = dot(lines, jnp.eye(8, 128, dtype=BF), 0, 0)
    parts_two = y_parts(
        pair_sum(jnp.concatenate([dot(act_one, d_kv_t, 0, 1), extra], axis=1).astype(BF))
    )
    summed = hx_sum(parts_one)
    own_kv = hx_sum(parts_two)
    at = feat_width // 2
    own_out = summed[:, :at].T
    own_router = summed[:, at : at + EXPERTS]
    at = at + EXPERTS
    own_gain_two = summed[:, at] + summed[:, at + 1]
    loss_value = (summed[0, at + 2] + summed[0, at + 3]) / (
        feat_width * (summed[0, at + 4] + summed[0, at + 5])
    )
    own_gain_one = own_kv[:, 2 * k_width] + own_kv[:, 2 * k_width + 1]
    own_gain_one = own_gain_one + swap(own_gain_one, "t")
    own_query = summed[:, feat_width // 2 + 128 :]
    own_down, own_out, own_kv, other = lax.optimization_barrier((own_down, own_out, own_kv, other))
    d_hidden_one, _ = norm_back(resid_in, scale_one, gain_one, both(part, other))
    grad_tokens = d_hidden + d_hidden_one
    return (
        output,
        loss_value,
        grad_tokens,
        own_gain_one,
        own_query,
        own_kv[:, :k_width],
        own_kv[:, k_width : 2 * k_width],
        own_out,
        own_gain_two,
        own_router,
        grad_stack[0][None],
        grad_stack[1][None],
        own_down[None],
    )


def solution(mesh):
    fine = Mesh(mesh.devices.reshape(2, 4, 2, 4, 2), ("h", "x", "c", "y", "t"))
    fsdp = ("h", "x", "c")
    every = ("h", "x", "c", "y")
    return jax.shard_map(
        local,
        mesh=fine,
        in_specs=(
            P(every, None),
            P(every, None),
            P(fsdp, None),
            P(every, None),
            P(every, None),
            P(every),
            P(every, "t"),
            P(every, "t"),
            P(every, "t"),
            P("t", every),
            P(every),
            P(every, None),
            P(fsdp, "y", "t"),
            P(fsdp, "y", "t"),
            P(fsdp, "t", "y"),
        ),
        out_specs=(
            P(every, None),
            P(),
            P(every, None),
            P(every),
            P(every, "t"),
            P(every, "t"),
            P(every, "t"),
            P("t", every),
            P(every),
            P(every, None),
            P(fsdp, "y", "t"),
            P(fsdp, "y", "t"),
            P(fsdp, "t", "y"),
        ),
        check_vma=False,
    )
```

```python
import functools

import jax
import jax.numpy as jnp
from jax import lax
from jax.experimental import pallas as pl
from jax.experimental.pallas import tpu as pltpu
from jax.sharding import Mesh
from jax.sharding import PartitionSpec as P

QUERY_HEAD_COUNT = 24
KEY_VALUE_HEADS = 8
HEAD_WIDTH = 64
TOP = 2
EXPERTS = 16
CAPACITY = 96

EPSILON = 1e-06
MASKED = -1e30

BF = jnp.bfloat16
F32 = jnp.float32
RING = ("h", "x", "y")
GROUP = QUERY_HEAD_COUNT // KEY_VALUE_HEADS
SPAN = 512
HALF = 256


def dot(left, right, left_dim, right_dim):
    return lax.dot_general(
        left, right, (((left_dim,), (right_dim,)), ((), ())), preferred_element_type=F32
    )


def rms_scale(values):
    return lax.rsqrt(jnp.mean(values * values, axis=-1, keepdims=True) + EPSILON)


def norm_back(values, scale, gain_row, upstream):
    gained = upstream * gain_row
    grad_gain = jnp.sum(upstream * values * scale, axis=0, keepdims=True)
    middle = jnp.mean(values * gained, axis=-1, keepdims=True)
    return (scale * gained - values * scale * scale * scale * middle, grad_gain)


def swap(value, axis):
    return lax.ppermute(value, axis, [(0, 1), (1, 0)])


def both(mine, other):
    return mine.astype(F32) + other.astype(F32)


def gather_hy(shard):
    wide = jnp.broadcast_to(shard[None], (8, *shard.shape))
    return lax.all_to_all(wide, ("h", "y"), 0, 0, tiled=True)


def gather_x(shards):
    wide = jnp.broadcast_to(shards[None], (4, *shards.shape))
    return lax.all_to_all(wide, "x", 0, 0, tiled=True)


def core_gather(mine):
    rows, cols = mine.shape[2:]
    mine = mine.reshape(4, 2, 4 * rows, cols)
    other = swap(mine, "c")
    mine, other = mine.transpose(1, 0, 2, 3), other.transpose(1, 0, 2, 3)
    first = lax.axis_index("c") == 0
    pair = jnp.stack([jnp.where(first, mine, other), jnp.where(first, other, mine)], axis=2)
    return pair.reshape(64 * rows, cols)


def after(value, *earlier):
    return lax.optimization_barrier((value,) + earlier)[0]


def axis_parts(parts, axis, size):
    me = lax.axis_index(axis)
    mine = [lax.dynamic_index_in_dim(parts, me, 0, keepdims=False)]
    for r in range(1, size):
        block = lax.dynamic_index_in_dim(parts, (me + r) % size, 0, keepdims=False)
        mine.append(lax.ppermute(block, axis, [(i, (i + r) % size) for i in range(size)]))
    return mine


def added(parts):
    total = parts[0].astype(F32)
    for part in parts[1:]:
        total = total + part.astype(F32)
    return total


def exchange_slots(rows):
    width = rows.shape[1]
    return lax.all_to_all(
        rows.reshape(EXPERTS, -1, width), ("h", "x", "c"), 0, 0, tiled=True
    ).reshape(-1, width)


def nn(a,b):
    return lax.dot_general(a,b,(((1,),(0,)),((),())),preferred_element_type=F32)

def fold(v, op):
    return op(v.reshape(v.shape[0]//8,8,v.shape[1]),axis=0)

def write_bias(bias, seg_q, seg_k, y, half):
    width = bias.shape[2]
    for r in range(4):

        def one(r=r):
            same = seg_k[r * SPAN : (r + 1) * SPAN, :] == seg_q[...]
            if r == 0:
                key_place = lax.broadcasted_iota(jnp.int32, (SPAN, width), 0)
                query_place = lax.broadcasted_iota(jnp.int32, (SPAN, width), 1) + half * HALF
                same = same & (key_place <= query_place)
            bias[r] = jnp.where(same, 0.0, MASKED)

        pl.when(y >= r)(one)


def fwd_kernel(
    half, y_ref, q_ref, kv0, kv1, kv2, kv3, seg_q, seg_k, o_ref, lse_ref, bias, kn, vt, sc
):
    y = y_ref[0]

    @pl.when(pl.program_id(0) == 0)
    def _():
        write_bias(bias, seg_q, seg_k, y, half)

    for r, kv in enumerate((kv0, kv1, kv2, kv3)):

        def fill(r=r, kv=kv):
            kn[r] = kv[0].T
            vt[r] = kv[1]

        pl.when(y >= r)(fill)
    scale = jnp.asarray(HEAD_WIDTH**-0.5, BF)
    qs = [q_ref[h * HEAD_WIDTH : (h + 1) * HEAD_WIDTH] * scale for h in range(GROUP)]

    def scores(r, rows, tops):
        out = []
        for h in range(GROUP):
            s = nn(kn[r, rows, :], qs[h]) + bias[r, rows, :]
            sc[h, r, rows, :] = s
            out.append(jnp.maximum(tops[h], fold(s, jnp.max)))
        return tuple(out)

    own = slice(0, (half + 1) * HALF)
    low = tuple(jnp.full((8, HALF), MASKED, F32) for _ in range(GROUP))
    tops = scores(0, own, low)
    tops = lax.fori_loop(1, y + 1, lambda r, t: scores(r, slice(0, SPAN), t), tops)
    tops = [jnp.max(t, axis=0, keepdims=True) for t in tops]

    def mix(r, rows, carry):
        out = []
        for h in range(GROUP):
            total, acc = carry[h]
            p = jnp.exp(sc[h, r, rows, :] - tops[h])
            out.append((total + fold(p, jnp.sum), acc + nn(vt[r, :, rows], p.astype(BF))))
        return tuple(out)

    zero = tuple(
        (jnp.zeros((8, HALF), F32), jnp.zeros((HEAD_WIDTH, HALF), F32)) for _ in range(GROUP)
    )
    carry = mix(0, own, zero)
    carry = lax.fori_loop(1, y + 1, lambda r, c: mix(r, slice(0, SPAN), c), carry)
    for h in range(GROUP):
        total = jnp.sum(carry[h][0], axis=0, keepdims=True)
        o_ref[h * HEAD_WIDTH : (h + 1) * HEAD_WIDTH, :] = (carry[h][1] / total).astype(BF)
        lse_ref[0, h : h + 1, :] = tops[h] + jnp.log(total)


def attend(half, y, q_t, kvs, seg_q, seg_k):
    rows = GROUP * HEAD_WIDTH
    heads = q_t.shape[0] // rows
    kv_spec = pl.BlockSpec((2, HEAD_WIDTH, SPAN), lambda g: (0, g, 0))
    return pl.pallas_call(
        functools.partial(fwd_kernel, half),
        grid=(heads,),
        in_specs=[
            pl.BlockSpec(memory_space=pltpu.SMEM),
            pl.BlockSpec((rows, HALF), lambda g: (g, half)),
            kv_spec,
            kv_spec,
            kv_spec,
            kv_spec,
            pl.BlockSpec((1, HALF), lambda g: (0, half)),
            pl.BlockSpec((4 * SPAN, 1), lambda g: (0, 0)),
        ],
        out_specs=[
            pl.BlockSpec((rows, HALF), lambda g: (g, 0)),
            pl.BlockSpec((1, 8, HALF), lambda g: (g, 0, 0)),
        ],
        out_shape=[
            jax.ShapeDtypeStruct((q_t.shape[0], HALF), BF),
            jax.ShapeDtypeStruct((heads, 8, HALF), F32),
        ],
        scratch_shapes=[
            pltpu.VMEM((4, SPAN, HALF), F32),
            pltpu.VMEM((4, SPAN, HEAD_WIDTH), BF),
            pltpu.VMEM((4, HEAD_WIDTH, SPAN), BF),
            pltpu.VMEM((GROUP, 4, SPAN, HALF), F32),
        ],
        compiler_params=pltpu.CompilerParams(vmem_limit_bytes=40 << 20),
        cost_estimate=pl.CostEstimate(
            flops=14_000_000_000, bytes_accessed=6_000_000, transcendentals=6_000_000
        ),
    )(y, q_t, *kvs, seg_q, seg_k)


def bwd_kernel(y_ref, q_ref, d_ref, o_0, o_1, lse_0, lse_1, kv0, kv1, kv2, kv3, seg_q, seg_k, dq_ref, g0, g1, g2, g3, bias, kn, vn, kt, dk, dv):
    y = y_ref[0]
    @pl.when(pl.program_id(0)==0)
    def _(): write_bias(bias, seg_q, seg_k, y, 0)
    for r,kv in enumerate((kv0,kv1,kv2,kv3)):
        def fill(r=r,kv=kv):
            kn[r] = kv[0].T
            vn[r] = kv[1].T
            kt[r] = kv[0]
        pl.when(y>=r)(fill)
    dk[...] = jnp.zeros_like(dk); dv[...] = jnp.zeros_like(dv)
    scale = jnp.asarray(HEAD_WIDTH**-0.5, BF)
    for b in range(2):
        cols = slice(b*HALF,(b+1)*HALF)
        qs, qn, ds, dn, dots, lses = [],[],[],[],[],[]
        for h in range(GROUP):
            hr = slice(h*HEAD_WIDTH,(h+1)*HEAD_WIDTH)
            q = q_ref[hr, cols]*scale
            qs.append(q); qn.append(q.T)
            d = d_ref[hr, cols]
            ds.append(d); dn.append(d.T)
            dots.append(jnp.sum(d.astype(F32)*(o_0, o_1)[b][hr].astype(F32),axis=0,keepdims=True))
            lses.append((lse_0, lse_1)[b][0, h : h + 1])
        def step(r, rows, carry):
            out=[]; sum_k=None; sum_v=None
            for h in range(GROUP):
                s = nn(kn[r, rows, :], qs[h]) + bias[r, rows, cols]
                p = jnp.exp(s - lses[h])
                pv = nn(p.astype(BF), dn[h])
                dp = nn(vn[r, rows, :], ds[h])
                dsc = (p*(dp - dots[h])).astype(BF)
                pk = nn(dsc, qn[h])
                out.append(carry[h] + nn(kt[r,:,rows], dsc))
                sum_k = pk if sum_k is None else sum_k+pk
                sum_v = pv if sum_v is None else sum_v+pv
            dk[r, rows, :] += sum_k
            dv[r, rows, :] += sum_v
            return tuple(out)
        carry = step(0, slice(0,(b+1)*HALF), tuple(jnp.zeros((HEAD_WIDTH,HALF),F32) for _ in range(GROUP)))
        carry = lax.fori_loop(1, y+1, lambda r,c: step(r, slice(0,SPAN), c), carry)
        for h in range(GROUP):
            dq_ref[h*HEAD_WIDTH:(h+1)*HEAD_WIDTH, cols] = (carry[h]*HEAD_WIDTH**-0.5).astype(BF)
    for r,g in enumerate((g0,g1,g2,g3)):
        g[0] = dk[r].T.astype(BF)
        g[1] = dv[r].T.astype(BF)

def attend_back(first, count, y, q_t, d_t, outs, lses, kvs, seg_q, seg_k):
    rows = GROUP * HEAD_WIDTH
    kv_spec = pl.BlockSpec((2, HEAD_WIDTH, SPAN), lambda g: (0, first + g, 0))
    q_spec = pl.BlockSpec((rows, SPAN), lambda g: (first + g, 0))
    o_spec = pl.BlockSpec((rows, HALF), lambda g: (first + g, 0))
    lse_spec = pl.BlockSpec((1, 8, HALF), lambda g: (first + g, 0, 0))
    kv_shape = jax.ShapeDtypeStruct((2, count * HEAD_WIDTH, SPAN), BF)
    return pl.pallas_call(
        bwd_kernel,
        grid=(count,),
        in_specs=[pl.BlockSpec(memory_space=pltpu.SMEM), q_spec, q_spec]
        + [o_spec, o_spec, lse_spec, lse_spec]
        + [kv_spec] * 4
        + [pl.BlockSpec((1, SPAN), lambda g: (0, 0)), pl.BlockSpec((4 * SPAN, 1), lambda g: (0, 0))],
        out_specs=[pl.BlockSpec((rows, SPAN), lambda g: (g, 0))]
        + [pl.BlockSpec((2, HEAD_WIDTH, SPAN), lambda g: (0, g, 0))] * 4,
        out_shape=[jax.ShapeDtypeStruct((count * rows, SPAN), BF)] + [kv_shape] * 4,
        scratch_shapes=[pltpu.VMEM((4, SPAN, SPAN), F32)]
        + [pltpu.VMEM((4, SPAN, HEAD_WIDTH), BF)] * 2
        + [pltpu.VMEM((4, HEAD_WIDTH, SPAN), BF)]
        + [pltpu.VMEM((4, SPAN, HEAD_WIDTH), F32)] * 2,
        compiler_params=pltpu.CompilerParams(vmem_limit_bytes=60 << 20),
        cost_estimate=pl.CostEstimate(
            flops=150_000_000_000, bytes_accessed=6_000_000, transcendentals=6_000_000
        ),
    )(y, q_t, d_t, *outs, *lses, *kvs, seg_q, seg_k)


def flat(ref):
    return ref[...].reshape(ref.shape[0] * ref.shape[2], ref.shape[3])


def experts_kernel(x_ref, gate_ref, up_ref, down_ref, g_ref, u_ref, inner_ref, out_ref, acc):
    step = pl.program_id(0)
    down_t = flat(down_ref).T

    @pl.when(step == 0)
    def _():
        acc[...] = jnp.zeros_like(acc)

    x = x_ref[...]
    g_ref[...] = nn(x, flat(gate_ref))
    u_ref[...] = nn(x, flat(up_ref))
    for m in range(x_ref.shape[0] // HALF):
        rows = slice(m * HALF, (m + 1) * HALF)
        gate = g_ref[rows]
        inner_ref[rows] = (gate * jax.nn.sigmoid(gate) * u_ref[rows]).astype(BF)
    for n in range(acc.shape[1] // SPAN):
        cols = slice(n * SPAN, (n + 1) * SPAN)
        acc[:, cols] += nn(inner_ref[...], down_t[:, cols])

    @pl.when(step == pl.num_programs(0) - 1)
    def _():
        out_ref[...] = acc[...].astype(BF)


def experts_back_kernel(
    d_ref, g_ref, u_ref, gate_ref, up_ref, down_ref, dg_ref, du_ref, out_ref, acc, inner
):
    step = pl.program_id(0)
    gate_t = flat(gate_ref).T
    up_t = flat(up_ref).T

    @pl.when(step == 0)
    def _():
        acc[...] = jnp.zeros_like(acc)

    inner[...] = nn(d_ref[...], flat(down_ref))
    for m in range(d_ref.shape[0] // HALF):
        rows = slice(m * HALF, (m + 1) * HALF)
        d_inner = inner[rows]
        gate = g_ref[rows]
        sig = jax.nn.sigmoid(gate)
        dg_ref[rows] = (d_inner * u_ref[rows] * sig * (1.0 + gate * (1.0 - sig))).astype(BF)
        du_ref[rows] = (d_inner * gate * sig).astype(BF)
    for n in range(acc.shape[1] // SPAN):
        cols = slice(n * SPAN, (n + 1) * SPAN)
        acc[:, cols] += nn(dg_ref[...], gate_t[:, cols]) + nn(du_ref[...], up_t[:, cols])

    @pl.when(step == pl.num_programs(0) - 1)
    def _():
        out_ref[...] = acc[...].astype(BF)


def expert_grads_kernel(x_ref, d_ref, dg_ref, du_ref, inner_ref, out_ref, x_t, d_t):
    @pl.when(pl.program_id(0) == 0)
    def _():
        x_t[...] = x_ref[...].T
        d_t[...] = d_ref[...].T

    depth = out_ref.shape[2]
    for i, (left, right) in enumerate(((x_t, dg_ref), (x_t, du_ref), (d_t, inner_ref))):
        for y in range(4):
            out_ref[y, i] = nn(left[y * depth : (y + 1) * depth], right[...]).astype(BF)


def expert_specs(rows, width, hidden):
    whole = pl.BlockSpec((rows, width), lambda b: (0, 0))
    weights = [
        pl.BlockSpec((4, 1, width // 4, HALF), functools.partial(lambda i, b: (0, i, 0, b), i))
        for i in range(3)
    ]
    column = pl.BlockSpec((rows, HALF), lambda b: (0, b))
    return dict(
        grid=(hidden // HALF,),
        scratch_shapes=[pltpu.VMEM((rows, width), F32)],
        compiler_params=pltpu.CompilerParams(vmem_limit_bytes=60 << 20),
        cost_estimate=pl.CostEstimate(
            flops=6 * rows * width * hidden, bytes_accessed=20_000_000, transcendentals=rows * hidden
        ),
    ), whole, weights, column


def run_experts(x, experts_full):
    rows, width = x.shape
    hidden = experts_full.shape[3]
    common, whole, weights, column = expert_specs(rows, width, hidden)
    wide = jax.ShapeDtypeStruct((rows, hidden), F32)
    return pl.pallas_call(
        experts_kernel,
        in_specs=[whole] + weights,
        out_specs=[column, column, column, whole],
        out_shape=[
            wide,
            wide,
            jax.ShapeDtypeStruct((rows, hidden), BF),
            jax.ShapeDtypeStruct((rows, width), BF),
        ],
        **common,
    )(x, experts_full, experts_full, experts_full)


def run_experts_back(d, gate, up, experts_full):
    rows, width = d.shape
    hidden = experts_full.shape[3]
    common, whole, weights, column = expert_specs(rows, width, hidden)
    low = jax.ShapeDtypeStruct((rows, hidden), BF)
    common["scratch_shapes"] = common["scratch_shapes"] + [pltpu.VMEM((rows, HALF), F32)]
    return pl.pallas_call(
        experts_back_kernel,
        in_specs=[whole, column, column] + weights,
        out_specs=[column, column, whole],
        out_shape=[low, low, jax.ShapeDtypeStruct((rows, width), BF)],
        **common,
    )(d, gate, up, experts_full, experts_full, experts_full)


def expert_grads(x, d, d_gate, d_up, inner):
    rows, width = x.shape
    hidden = inner.shape[1]
    common, whole, _, column = expert_specs(rows, width, hidden)
    common["scratch_shapes"] = [pltpu.VMEM((width, rows), BF)] * 2
    return pl.pallas_call(
        expert_grads_kernel,
        in_specs=[whole, whole, column, column, column],
        out_specs=pl.BlockSpec((4, 3, width // 4, HALF), lambda b: (0, 0, 0, b)),
        out_shape=jax.ShapeDtypeStruct((4, 3, width // 4, hidden), BF),
        **common,
    )(x, d, d_gate, d_up, inner)


def grads_kernel(plan, first_axis, core_ref, *refs):
    ins, (own_ref, other_ref, pack) = refs[:-3], refs[-3:]
    at = 0
    turned = {}
    for terms in plan:
        total = None
        for left, right, first in terms:
            if left is None:
                high = ins[right][...].astype(BF).astype(F32)
                rest = ins[right][...] - high
                total = jnp.zeros((384, 128), F32) if total is None else total
                pack[:, at : at + 128] = total
                pack[:, at + 16 : at + 24] = high.T
                pack[:, at + 24 : at + 32] = rest.T
                total = None
                at = at + 128
                continue
            if left not in turned:
                turned[left] = ins[left][...].T
            width = ins[right].shape[1]
            rows = turned[left][:, first : first + width]
            piece = dot(rows, ins[right][...], 1, 1)
            total = piece if total is None else total + piece
        if total is not None:
            pack[:, at : at + total.shape[1]] = total
            at = at + total.shape[1]
    for core in range(2):

        @pl.when(core_ref[0] == core)
        def _(core=core):
            for j in range(2):
                for y in range(4):
                    for ref, c in ((own_ref, core), (other_ref, 1 - core)):
                        row = (2 * j + c) * 96 + y * 24
                        value = pack[row : row + 24, :].astype(BF)
                        if first_axis == "x":
                            ref[j, y, 0] = value
                        else:
                            ref[y, j, 0] = value


def pack_grads(plan, first_axis, arrays, wide, cols):
    specs = []
    for i, value in enumerate(arrays):
        if i in wide:
            specs.append(pl.BlockSpec((value.shape[0], 384), lambda b: (0, b)))
        else:
            specs.append(pl.BlockSpec(value.shape, lambda b: (0, 0)))
    out = jax.ShapeDtypeStruct((4, 4, 2, 24, cols), BF)
    if first_axis == "x":
        out_spec = pl.BlockSpec((2, 4, 1, 24, cols), lambda b: (b % 2, 0, b // 2, 0, 0))
    else:
        out_spec = pl.BlockSpec((4, 2, 1, 24, cols), lambda b: (0, b % 2, b // 2, 0, 0))
    return pl.pallas_call(
        functools.partial(grads_kernel, plan, first_axis),
        grid=(arrays[wide[0]].shape[1] // 384,),
        in_specs=[pl.BlockSpec(memory_space=pltpu.SMEM)] + specs,
        out_specs=[out_spec, out_spec],
        out_shape=[out, out],
        scratch_shapes=[pltpu.VMEM((384, cols), F32)],
        compiler_params=pltpu.CompilerParams(vmem_limit_bytes=40 << 20),
        cost_estimate=pl.CostEstimate(
            flops=20_000_000_000, bytes_accessed=12_000_000, transcendentals=0
        ),
    )(jnp.full((1,), lax.axis_index("c"), jnp.int32), *arrays)


def paired(own, theirs):
    return (own.astype(F32) + swap(theirs, "c").astype(F32)).astype(BF)


def local(
    tokens,
    teacher,
    segments,
    routes,
    route_weight,
    norm_attn,
    w_query,
    key_weight,
    value_weight,
    w_out,
    norm_ffn,
    w_router,
    w_gate,
    w_up,
    w_down,
):
    tok_rows, feat_width = tokens.shape
    q_width = w_query.shape[1]
    k_width = key_weight.shape[1]
    tix = lax.axis_index("t")
    yix = lax.axis_index("y")

    small = jnp.concatenate(
        [
            w_router,
            norm_attn[:, None],
            norm_ffn[:, None],
            jnp.zeros((w_router.shape[0], 128 - EXPERTS - 2), BF),
        ],
        axis=1,
    )
    by_hy = gather_hy(jnp.concatenate([key_weight, value_weight, small, w_query, w_out.T], axis=1))
    kv_cols = 2 * k_width + 128
    pack = core_gather(gather_x(by_hy[:, :, :kv_cols]))
    full_kv = pack[:, : 2 * k_width]
    full_small = pack[:, 2 * k_width :]
    ring_rest = gather_x(by_hy[:, :, kv_cols:])
    small_rows = dot(jnp.eye(24, 128, dtype=BF), full_small, 1, 1)
    router_rows = small_rows[:EXPERTS].astype(BF)
    gain_one = small_rows[EXPERTS : EXPERTS + 1]
    gain_two = small_rows[EXPERTS + 1 : EXPERTS + 2]

    resid_in = tokens.astype(F32)
    scale_one = rms_scale(resid_in)
    act_one = (resid_in * scale_one * gain_one).astype(BF)
    kv_mine = dot(full_kv, act_one, 0, 1).astype(BF).reshape(2, k_width, tok_rows)
    kvs = [kv_mine] + [
        lax.ppermute(kv_mine, "y", [(i, i + r) for i in range(4 - r)]) for r in (1, 2, 3)
    ]
    kvs[1:] = lax.optimization_barrier((*kvs[1:], ring_rest))[:3]
    rest = core_gather(ring_rest)
    full_query = rest[:, :q_width]
    full_out = rest[:, q_width:]
    query_t = dot(full_query, act_one, 0, 1).astype(BF)

    late_gate, late_up, late_down = lax.optimization_barrier(
        (w_gate[0], w_up[0], w_down[0], kv_mine)
    )[:3]
    experts = jnp.stack([late_gate, late_up, late_down.T])
    experts_other = after(swap(experts, "t"), kvs[1], kvs[2], kvs[3])
    experts_full = jnp.concatenate([experts, experts_other], axis=2)
    experts_full = lax.all_gather(experts_full, "y", axis=0)

    seg_blocks = segments[0].reshape(4, tok_rows)
    seg_mine = lax.dynamic_index_in_dim(seg_blocks, yix, 0, keepdims=False)
    seg_keys = jnp.concatenate(
        [lax.dynamic_index_in_dim(seg_blocks, (yix + 4 - r) % 4, 0, keepdims=False) for r in range(4)]
    )[:, None]
    place_y = jnp.full((1,), yix, jnp.int32)
    mixed_0, log_0 = attend(0, place_y, query_t, kvs, seg_mine[None], seg_keys)
    part_0 = dot(mixed_0, full_out, 0, 1).astype(BF)
    mixed_1, log_1 = attend(1, place_y, after(query_t, part_0), kvs, seg_mine[None], seg_keys)
    other_0 = swap(part_0, "t")
    part_1 = dot(after(mixed_1, other_0), full_out, 0, 1).astype(BF)
    other_1 = swap(part_1, "t")
    hidden = resid_in + jnp.concatenate([both(part_0, other_0), both(part_1, other_1)])
    scale_two = rms_scale(hidden)
    act_two = (hidden * scale_two * gain_two).astype(BF)

    logits = dot(router_rows, act_two, 1, 1)
    router = jax.nn.softmax(logits, axis=0)
    route_cols = routes.T
    weight_cols = route_weight.T
    expert_iota = lax.broadcasted_iota(jnp.int32, (EXPERTS, tok_rows), 0)
    named = [expert_iota == route_cols[k : k + 1] for k in range(TOP)]
    taken = (named[0] | named[1]).astype(BF)
    earlier = (
        lax.broadcasted_iota(jnp.int32, (tok_rows, tok_rows), 0)
        < lax.broadcasted_iota(jnp.int32, (tok_rows, tok_rows), 1)
    ).astype(BF)
    count_before = dot(taken, earlier, 1, 0)
    half = CAPACITY // 2
    slot_iota = lax.broadcasted_iota(jnp.int32, (EXPERTS * half, tok_rows), 0)
    picks = []
    gates = []
    for k in range(TOP):
        place = jnp.sum(jnp.where(named[k], count_before, 0.0), axis=0, keepdims=True)
        place = place.astype(jnp.int32) - tix * half
        slot = jnp.where((place >= 0) & (place < half), route_cols[k : k + 1] * half + place, -1)
        picks.append(slot_iota == slot)
        chosen = jnp.sum(jnp.where(named[k], router, 0.0), axis=0, keepdims=True)
        gates.append(chosen * weight_cols[k : k + 1])
    pick = (picks[0] | picks[1]).astype(BF)
    gated_pick = (
        jnp.where(picks[0], gates[0], 0.0) + jnp.where(picks[1], gates[1], 0.0)
    ).astype(BF)

    received = exchange_slots(dot(pick, act_two, 1, 0).astype(BF))
    gate_proj, up_proj, inner, slots_out = run_experts(received, experts_full)
    returned = exchange_slots(slots_out)
    part = dot(gated_pick, returned, 0, 0).astype(BF)
    output = hidden + both(part, swap(part, "t"))
    valid = (seg_mine != 0).astype(F32)
    difference = output - teacher.astype(F32)
    grad_output = difference * valid[:, None]
    sse = jnp.sum(grad_output * difference)
    count = jnp.sum(valid)
    grad_low = grad_output.astype(BF)
    d_received = exchange_slots(dot(gated_pick, grad_low, 1, 0).astype(BF))

    slot_dots = dot(returned, grad_low, 1, 1)
    d_gates = jnp.concatenate(
        [jnp.sum(jnp.where(picks[k], slot_dots, 0.0), axis=0, keepdims=True) for k in range(TOP)]
    )
    d_gates_other = swap(d_gates, "t")
    d_received = after(d_received, d_gates_other)
    d_gates = d_gates + d_gates_other

    d_gate_proj, d_up_proj, d_slots = run_experts_back(
        d_received, gate_proj, up_proj, experts_full
    )
    d_returned = exchange_slots(d_slots)
    received, d_received = after(received, d_slots), after(d_received, d_slots)

    grad_parts = expert_grads(received, d_received, d_gate_proj, d_up_proj, inner)
    grad_experts = lax.psum_scatter(grad_parts, "y", scatter_dimension=0)
    d_returned = after(d_returned, grad_parts)
    ff_half = w_gate.shape[2]
    keep = grad_experts[:, :, :ff_half]
    give = grad_experts[:, :, ff_half:]

    d_router = jnp.where(named[0], d_gates[0:1] * weight_cols[0:1], 0.0) + jnp.where(
        named[1], d_gates[1:2] * weight_cols[1:2], 0.0
    )
    d_logits = (
        router * (d_router - jnp.sum(router * d_router, axis=0, keepdims=True))
    ).astype(BF)
    d_route = dot(d_logits, router_rows, 0, 0)
    part = dot(pick, d_returned, 0, 0).astype(BF)
    d_act_two = d_route + both(part, after(swap(part, "t"), d_route))
    d_norm_two, grad_gain_two = norm_back(hidden, scale_two, gain_two, d_act_two)
    d_hidden = grad_output + d_norm_two
    d_attn = d_hidden.astype(BF)
    d_mixed_t = dot(full_out, d_attn, 0, 1).astype(BF)

    saved = ((mixed_0, mixed_1), (log_0, log_1), kvs, seg_mine[None], seg_keys)
    half_groups = k_width // HEAD_WIDTH // 2
    back_0 = attend_back(0, half_groups, place_y, query_t, d_mixed_t, *saved)

    def ring_back(parts):
        return [
            lax.ppermute(parts[r], "y", [(i, i - r) for i in range(r, 4)]) for r in (1, 2, 3)
        ]

    *back_0, d_mixed_t, give = lax.optimization_barrier((*back_0, d_mixed_t, give))
    back_1 = attend_back(half_groups, half_groups, place_y, query_t, d_mixed_t, *saved)
    others_0 = ring_back(back_0[1:])
    given = swap(give, "t")
    *back_1, o1, o2, o3, given, d_attn_late, gain_late, d_logits_late, back_0[0] = (
        lax.optimization_barrier(
            (*back_1, *others_0, given, d_attn, grad_gain_two, d_logits, back_0[0])
        )
    )
    others_0 = [o1, o2, o3]

    others_1 = ring_back(back_1[1:])
    lines = jnp.concatenate(
        [
            gain_late,
            jnp.full((1, feat_width), sse),
            jnp.full((1, feat_width), count),
            jnp.zeros((5, feat_width), F32),
        ]
    )
    logits_pad = jnp.concatenate(
        [d_logits_late, jnp.zeros((128 - EXPERTS, tok_rows), BF)]
    )
    own_one, theirs_one = pack_grads(
        (
            ((0, 4, 0), (0, 5, HALF)),
            ((2, 6, 0), (None, 3, 0)),
            ((1, 7, 0),),
            ((1, 8, 0),),
        ),
        "x",
        (d_attn_late, act_one, act_two, lines, mixed_0, mixed_1, logits_pad, back_0[0], back_1[0]),
        (0, 1, 2, 3),
        feat_width // 2 + 128 + q_width,
    )
    d_act_query = dot(jnp.concatenate([back_0[0], back_1[0]]), full_query, 0, 1)
    o1, o2, o3, own_one, theirs_one, d_act_query = lax.optimization_barrier(
        (*others_1, own_one, theirs_one, d_act_query)
    )

    d_kv_t = jnp.concatenate(
        [added([back_0[1], *others_0]), added([back_1[1], o1, o2, o3])], axis=1
    ).reshape(2 * k_width, tok_rows).astype(BF)
    d_act_part = d_act_query + dot(d_kv_t, full_kv, 0, 1)
    part = d_act_part.astype(BF)
    pair_one = paired(own_one, theirs_one)
    lines = jnp.concatenate(
        [
            jnp.sum(d_act_part * resid_in * scale_one, axis=0, keepdims=True),
            jnp.zeros((7, feat_width), F32),
        ]
    )
    own_two, theirs_two = pack_grads(
        (((0, 2, 0),), ((None, 1, 0),)), "y", (act_one, lines, d_kv_t), (0, 1), 2 * k_width + 128
    )
    part, pair_one, own_two, theirs_two = lax.optimization_barrier(
        (part, pair_one, own_two, theirs_two)
    )
    other = swap(part, "t")
    parts_one = axis_parts(pair_one, "x", 4)
    ring_two = lax.all_to_all(paired(own_two, theirs_two), "y", 0, 0, tiled=True)
    grad_stack = keep.astype(F32) + given.astype(F32)
    own_down = grad_stack[2].T
    *parts_one, ring_two, own_down, other = lax.optimization_barrier(
        (*parts_one, ring_two, own_down, other)
    )
    by_x = added(parts_one).astype(BF)
    by_xy = added(axis_parts(by_x, "y", 4)).astype(BF)
    by_xy, other = lax.optimization_barrier((by_xy, other))
    summed = added(axis_parts(by_xy, "h", 2))
    by_y = jnp.sum(ring_two.astype(F32), axis=0).astype(BF)
    ring_two = lax.all_to_all(by_y.reshape(8, *by_y.shape[2:]), ("x", "h"), 0, 0, tiled=True)
    own_kv = jnp.sum(ring_two.astype(F32), axis=0)
    own_query = summed[:, feat_width // 2 + 128 :]
    at = feat_width // 2
    own_out = summed[:, :at].T
    own_router = summed[:, at : at + EXPERTS]
    at = at + EXPERTS
    own_gain_two = summed[:, at] + summed[:, at + 8]
    loss_value = (summed[0, at + 1] + summed[0, at + 9]) / (
        feat_width * (summed[0, at + 2] + summed[0, at + 10])
    )
    own_gain_one = own_kv[:, 2 * k_width + EXPERTS] + own_kv[:, 2 * k_width + EXPERTS + 8]
    own_gain_one = own_gain_one + swap(own_gain_one, "t")
    d_hidden_one, _ = norm_back(resid_in, scale_one, gain_one, both(part, other))
    grad_tokens = d_hidden + d_hidden_one
    return (
        output,
        loss_value,
        grad_tokens,
        own_gain_one,
        own_query,
        own_kv[:, :k_width],
        own_kv[:, k_width : 2 * k_width],
        own_out,
        own_gain_two,
        own_router,
        grad_stack[0][None],
        grad_stack[1][None],
        own_down[None],
    )


def solution(mesh):
    fine = Mesh(mesh.devices.reshape(2, 4, 2, 4, 2), ("h", "x", "c", "y", "t"))
    fsdp = ("h", "x", "c")
    every = ("h", "x", "c", "y")
    return jax.shard_map(
        local,
        mesh=fine,
        in_specs=(
            P(every, None),
            P(every, None),
            P(fsdp, None),
            P(every, None),
            P(every, None),
            P(every),
            P(every, "t"),
            P(every, "t"),
            P(every, "t"),
            P("t", every),
            P(every),
            P(every, None),
            P(fsdp, "y", "t"),
            P(fsdp, "y", "t"),
            P(fsdp, "t", "y"),
        ),
        out_specs=(
            P(every, None),
            P(),
            P(every, None),
            P(every),
            P(every, "t"),
            P(every, "t"),
            P(every, "t"),
            P("t", every),
            P(every),
            P(every, None),
            P(fsdp, "y", "t"),
            P(fsdp, "y", "t"),
            P(fsdp, "t", "y"),
        ),
        check_vma=False,
    )
```

```python
import functools

import jax
import jax.numpy as jnp
from jax import lax
from jax.experimental import pallas as pl
from jax.experimental.layout import Layout, with_layout_constraint
from jax.experimental.pallas import tpu as pltpu
from jax.sharding import Mesh
from jax.sharding import PartitionSpec as P

QUERY_HEAD_COUNT = 24
KEY_VALUE_HEADS = 8
HEAD_WIDTH = 64
TOP = 2
EXPERTS = 16
CAPACITY = 96

EPSILON = 1e-06
MASKED = -1e30

BF = jnp.bfloat16
F32 = jnp.float32
RING = ("h", "x", "y")
GROUP = QUERY_HEAD_COUNT // KEY_VALUE_HEADS
SPAN = 512
HALF = 256


def dot(left, right, left_dim, right_dim):
    return lax.dot_general(
        left, right, (((left_dim,), (right_dim,)), ((), ())), preferred_element_type=F32
    )


def rms_scale(values):
    return lax.rsqrt(jnp.mean(values * values, axis=-1, keepdims=True) + EPSILON)


def norm_back(values, scale, gain_row, upstream):
    gained = upstream * gain_row
    grad_gain = jnp.sum(upstream * values * scale, axis=0, keepdims=True)
    middle = jnp.mean(values * gained, axis=-1, keepdims=True)
    return (scale * gained - values * scale * scale * scale * middle, grad_gain)


def swap(value, axis):
    return lax.ppermute(value, axis, [(0, 1), (1, 0)])


def both(mine, other):
    return mine.astype(F32) + other.astype(F32)


def gather_hy(shard):
    wide = jnp.broadcast_to(shard[None], (8, *shard.shape))
    return lax.all_to_all(wide, ("h", "y"), 0, 0, tiled=True)


def gather_x(shards):
    wide = jnp.broadcast_to(shards[None], (4, *shards.shape))
    return lax.all_to_all(wide, "x", 0, 0, tiled=True)


def core_gather(mine):
    rows, cols = mine.shape[2:]
    mine = mine.reshape(4, 2, 4 * rows, cols)
    other = swap(mine, "c")
    mine, other = mine.transpose(1, 0, 2, 3), other.transpose(1, 0, 2, 3)
    first = lax.axis_index("c") == 0
    pair = jnp.stack([jnp.where(first, mine, other), jnp.where(first, other, mine)], axis=2)
    return pair.reshape(64 * rows, cols)


def after(value, *earlier):
    return lax.optimization_barrier((value,) + earlier)[0]


def axis_parts(parts, axis, size):
    me = lax.axis_index(axis)
    mine = [lax.dynamic_index_in_dim(parts, me, 0, keepdims=False)]
    for r in range(1, size):
        block = lax.dynamic_index_in_dim(parts, (me + r) % size, 0, keepdims=False)
        mine.append(lax.ppermute(block, axis, [(i, (i + r) % size) for i in range(size)]))
    return mine


def added(parts):
    total = parts[0].astype(F32)
    for part in parts[1:]:
        total = total + part.astype(F32)
    return total


def exchange_slots(rows):
    width = rows.shape[1]
    return lax.all_to_all(
        rows.reshape(EXPERTS, -1, width), ("h", "x", "c"), 0, 0, tiled=True
    ).reshape(-1, width)


def nn(a,b):
    return lax.dot_general(a,b,(((1,),(0,)),((),())),preferred_element_type=F32)

def fold(v, op):
    return op(v.reshape(v.shape[0]//8,8,v.shape[1]),axis=0)

def write_bias(bias, seg_q, seg_k, y, half):
    width = bias.shape[2]
    for r in range(4):

        def one(r=r):
            same = seg_k[r * SPAN : (r + 1) * SPAN, :] == seg_q[...]
            if r == 0:
                key_place = lax.broadcasted_iota(jnp.int32, (SPAN, width), 0)
                query_place = lax.broadcasted_iota(jnp.int32, (SPAN, width), 1) + half * HALF
                same = same & (key_place <= query_place)
            bias[r] = jnp.where(same, 0.0, MASKED)

        pl.when(y >= r)(one)


def fwd_kernel(
    half, y_ref, q_ref, kv0, kv1, kv2, kv3, seg_q, seg_k, o_ref, lse_ref, bias, kn, vt, sc
):
    y = y_ref[0]

    @pl.when(pl.program_id(0) == 0)
    def _():
        write_bias(bias, seg_q, seg_k, y, half)

    for r, kv in enumerate((kv0, kv1, kv2, kv3)):

        def fill(r=r, kv=kv):
            kn[r] = kv[0].T
            vt[r] = kv[1]

        pl.when(y >= r)(fill)
    scale = jnp.asarray(HEAD_WIDTH**-0.5, BF)
    qs = [q_ref[h * HEAD_WIDTH : (h + 1) * HEAD_WIDTH] * scale for h in range(GROUP)]

    def scores(r, rows, tops):
        out = []
        for h in range(GROUP):
            s = nn(kn[r, rows, :], qs[h]) + bias[r, rows, :]
            sc[h, r, rows, :] = s
            out.append(jnp.maximum(tops[h], fold(s, jnp.max)))
        return tuple(out)

    own = slice(0, (half + 1) * HALF)
    low = tuple(jnp.full((8, HALF), MASKED, F32) for _ in range(GROUP))
    tops = scores(0, own, low)
    tops = lax.fori_loop(1, y + 1, lambda r, t: scores(r, slice(0, SPAN), t), tops)
    tops = [jnp.max(t, axis=0, keepdims=True) for t in tops]

    def mix(r, rows, carry):
        totals, acc = carry
        out, weights = [], []
        for h in range(GROUP):
            p = jnp.exp(sc[h, r, rows, :] - tops[h])
            out.append(totals[h] + fold(p, jnp.sum))
            weights.append(p.astype(BF))
        return tuple(out), acc + nn(vt[r, :, rows], jnp.concatenate(weights, 1))

    zero = (
        tuple(jnp.zeros((8, HALF), F32) for _ in range(GROUP)),
        jnp.zeros((HEAD_WIDTH, GROUP * HALF), F32),
    )
    carry = mix(0, own, zero)
    totals, acc = lax.fori_loop(1, y + 1, lambda r, c: mix(r, slice(0, SPAN), c), carry)
    for h in range(GROUP):
        total = jnp.sum(totals[h], axis=0, keepdims=True)
        mixed = acc[:, h * HALF : (h + 1) * HALF] / total
        o_ref[h * HEAD_WIDTH : (h + 1) * HEAD_WIDTH, :] = mixed.astype(BF)
        lse_ref[0, h : h + 1, :] = tops[h] + jnp.log(total)


def attend(half, y, q_t, kvs, seg_q, seg_k):
    rows = GROUP * HEAD_WIDTH
    heads = q_t.shape[0] // rows
    kv_spec = pl.BlockSpec((2, HEAD_WIDTH, SPAN), lambda g: (0, g, 0))
    return pl.pallas_call(
        functools.partial(fwd_kernel, half),
        grid=(heads,),
        in_specs=[
            pl.BlockSpec(memory_space=pltpu.SMEM),
            pl.BlockSpec((rows, HALF), lambda g: (g, half)),
            kv_spec,
            kv_spec,
            kv_spec,
            kv_spec,
            pl.BlockSpec((1, HALF), lambda g: (0, half)),
            pl.BlockSpec((4 * SPAN, 1), lambda g: (0, 0)),
        ],
        out_specs=[
            pl.BlockSpec((rows, HALF), lambda g: (g, 0)),
            pl.BlockSpec((1, 8, HALF), lambda g: (g, 0, 0)),
        ],
        out_shape=[
            jax.ShapeDtypeStruct((q_t.shape[0], HALF), BF),
            jax.ShapeDtypeStruct((heads, 8, HALF), F32),
        ],
        scratch_shapes=[
            pltpu.VMEM((4, SPAN, HALF), F32),
            pltpu.VMEM((4, SPAN, HEAD_WIDTH), BF),
            pltpu.VMEM((4, HEAD_WIDTH, SPAN), BF),
            pltpu.VMEM((GROUP, 4, SPAN, HALF), F32),
        ],
        compiler_params=pltpu.CompilerParams(vmem_limit_bytes=40 << 20),
        cost_estimate=pl.CostEstimate(
            flops=14_000_000_000, bytes_accessed=6_000_000, transcendentals=6_000_000
        ),
    )(y, q_t, *kvs, seg_q, seg_k)


def bwd_kernel(y_ref, q_ref, d_ref, o_0, o_1, lse_0, lse_1, kv0, kv1, kv2, kv3, seg_q, seg_k, dq_ref, g0, g1, g2, g3, bias, kn, vn, kt, dvk):
    y = y_ref[0]
    @pl.when(pl.program_id(0)==0)
    def _(): write_bias(bias, seg_q, seg_k, y, 0)
    for r,kv in enumerate((kv0,kv1,kv2,kv3)):
        def fill(r=r,kv=kv):
            kn[r] = kv[0].T
            vn[r] = kv[1].T
            kt[r] = kv[0]
        pl.when(y>=r)(fill)
    dvk[...] = jnp.zeros_like(dvk)
    scale = jnp.asarray(HEAD_WIDTH**-0.5, BF)
    for b in range(2):
        cols = slice(b*HALF,(b+1)*HALF)
        qs, qn, ds, dn, dots, lses = [],[],[],[],[],[]
        for h in range(GROUP):
            hr = slice(h*HEAD_WIDTH,(h+1)*HEAD_WIDTH)
            q = q_ref[hr, cols]*scale
            qs.append(q); qn.append(q.T)
            d = d_ref[hr, cols]
            ds.append(d); dn.append(d.T)
            dots.append(jnp.sum(d.astype(F32)*(o_0, o_1)[b][hr].astype(F32),axis=0,keepdims=True))
            lses.append((lse_0, lse_1)[b][0, h : h + 1])
        right = []
        for h in range(GROUP):
            none = jnp.zeros_like(dn[h])
            right += [jnp.concatenate([dn[h], none], 1), jnp.concatenate([none, qn[h]], 1)]
        right = jnp.concatenate(right, 0)

        def step(r, rows, carry):
            left = []
            for h in range(GROUP):
                s = nn(kn[r, rows, :], qs[h]) + bias[r, rows, cols]
                p = jnp.exp(s - lses[h])
                dp = nn(vn[r, rows, :], ds[h])
                dsc = (p * (dp - dots[h])).astype(BF)
                left += [p.astype(BF), dsc]
            dvk[r, rows, :] += nn(jnp.concatenate(left, 1), right)
            return carry + nn(kt[r, :, rows], jnp.concatenate(left[1::2], 1))

        carry = step(0, slice(0, (b + 1) * HALF), jnp.zeros((HEAD_WIDTH, GROUP * HALF), F32))
        carry = lax.fori_loop(1, y+1, lambda r,c: step(r, slice(0,SPAN), c), carry)
        for h in range(GROUP):
            dq_ref[h*HEAD_WIDTH:(h+1)*HEAD_WIDTH, cols] = (
                carry[:, h * HALF : (h + 1) * HALF] * HEAD_WIDTH**-0.5
            ).astype(BF)
    for r,g in enumerate((g0,g1,g2,g3)):
        turned = dvk[r].T.astype(BF)
        g[0] = turned[HEAD_WIDTH:]
        g[1] = turned[:HEAD_WIDTH]

def attend_back(first, count, y, q_t, d_t, outs, lses, kvs, seg_q, seg_k):
    rows = GROUP * HEAD_WIDTH
    kv_spec = pl.BlockSpec((2, HEAD_WIDTH, SPAN), lambda g: (0, first + g, 0))
    q_spec = pl.BlockSpec((rows, SPAN), lambda g: (first + g, 0))
    o_spec = pl.BlockSpec((rows, HALF), lambda g: (first + g, 0))
    lse_spec = pl.BlockSpec((1, 8, HALF), lambda g: (first + g, 0, 0))
    kv_shape = jax.ShapeDtypeStruct((2, count * HEAD_WIDTH, SPAN), BF)
    return pl.pallas_call(
        bwd_kernel,
        grid=(count,),
        in_specs=[pl.BlockSpec(memory_space=pltpu.SMEM), q_spec, q_spec]
        + [o_spec, o_spec, lse_spec, lse_spec]
        + [kv_spec] * 4
        + [pl.BlockSpec((1, SPAN), lambda g: (0, 0)), pl.BlockSpec((4 * SPAN, 1), lambda g: (0, 0))],
        out_specs=[pl.BlockSpec((rows, SPAN), lambda g: (g, 0))]
        + [pl.BlockSpec((2, HEAD_WIDTH, SPAN), lambda g: (0, g, 0))] * 4,
        out_shape=[jax.ShapeDtypeStruct((count * rows, SPAN), BF)] + [kv_shape] * 4,
        scratch_shapes=[pltpu.VMEM((4, SPAN, SPAN), F32)]
        + [pltpu.VMEM((4, SPAN, HEAD_WIDTH), BF)] * 2
        + [pltpu.VMEM((4, HEAD_WIDTH, SPAN), BF)]
        + [pltpu.VMEM((4, SPAN, 2 * HEAD_WIDTH), F32)],
        compiler_params=pltpu.CompilerParams(vmem_limit_bytes=60 << 20),
        cost_estimate=pl.CostEstimate(
            flops=150_000_000_000, bytes_accessed=6_000_000, transcendentals=6_000_000
        ),
    )(y, q_t, d_t, *outs, *lses, *kvs, seg_q, seg_k)


def flat(ref):
    return ref[...].reshape(ref.shape[0] * ref.shape[3], ref.shape[4])


def experts_kernel(x_ref, gate_ref, up_ref, down_ref, g_ref, u_ref, inner_ref, out_ref, acc):
    step = pl.program_id(0)
    down_t = flat(down_ref).T

    @pl.when(step == 0)
    def _():
        acc[...] = jnp.zeros_like(acc)

    x = x_ref[...]
    g_ref[...] = nn(x, flat(gate_ref))
    u_ref[...] = nn(x, flat(up_ref))
    for m in range(x_ref.shape[0] // HALF):
        rows = slice(m * HALF, (m + 1) * HALF)
        gate = g_ref[rows]
        inner_ref[rows] = (gate * jax.nn.sigmoid(gate) * u_ref[rows]).astype(BF)
    for n in range(acc.shape[1] // SPAN):
        cols = slice(n * SPAN, (n + 1) * SPAN)
        acc[:, cols] += nn(inner_ref[...], down_t[:, cols])

    @pl.when(step == pl.num_programs(0) - 1)
    def _():
        out_ref[...] = acc[...].astype(BF)


def experts_back_kernel(
    d_ref, g_ref, u_ref, gate_ref, up_ref, down_ref, dg_ref, du_ref, out_ref, acc, inner
):
    step = pl.program_id(0)
    gate_t = flat(gate_ref).T
    up_t = flat(up_ref).T

    @pl.when(step == 0)
    def _():
        acc[...] = jnp.zeros_like(acc)

    inner[...] = nn(d_ref[...], flat(down_ref))
    for m in range(d_ref.shape[0] // HALF):
        rows = slice(m * HALF, (m + 1) * HALF)
        d_inner = inner[rows]
        gate = g_ref[rows]
        sig = jax.nn.sigmoid(gate)
        dg_ref[rows] = (d_inner * u_ref[rows] * sig * (1.0 + gate * (1.0 - sig))).astype(BF)
        du_ref[rows] = (d_inner * gate * sig).astype(BF)
    for n in range(acc.shape[1] // SPAN):
        cols = slice(n * SPAN, (n + 1) * SPAN)
        acc[:, cols] += nn(dg_ref[...], gate_t[:, cols]) + nn(du_ref[...], up_t[:, cols])

    @pl.when(step == pl.num_programs(0) - 1)
    def _():
        out_ref[...] = acc[...].astype(BF)


def expert_grads_kernel(x_ref, d_ref, dg_ref, du_ref, inner_ref, out_ref, x_t, d_t):
    @pl.when(pl.program_id(0) == 0)
    def _():
        x_t[...] = x_ref[...].T
        d_t[...] = d_ref[...].T

    depth = out_ref.shape[3]
    for i, (left, right) in enumerate(((x_t, dg_ref), (x_t, du_ref), (d_t, inner_ref))):
        for y in range(4):
            out_ref[y, 0, i] = nn(left[y * depth : (y + 1) * depth], right[...]).astype(BF)


def expert_specs(rows, width, hidden):
    whole = pl.BlockSpec((rows, width), lambda b: (0, 0))
    weights = [
        pl.BlockSpec(
            (4, 1, 1, width // 4, HALF),
            functools.partial(lambda i, b: (0, b // 2, i, 0, b % 2), i),
        )
        for i in range(3)
    ]
    column = pl.BlockSpec((rows, HALF), lambda b: (0, b))
    return dict(
        grid=(hidden // HALF,),
        scratch_shapes=[pltpu.VMEM((rows, width), F32)],
        compiler_params=pltpu.CompilerParams(vmem_limit_bytes=60 << 20),
        cost_estimate=pl.CostEstimate(
            flops=6 * rows * width * hidden, bytes_accessed=20_000_000, transcendentals=rows * hidden
        ),
    ), whole, weights, column


def run_experts(x, experts_full):
    rows, width = x.shape
    hidden = 2 * experts_full.shape[4]
    common, whole, weights, column = expert_specs(rows, width, hidden)
    wide = jax.ShapeDtypeStruct((rows, hidden), F32)
    return pl.pallas_call(
        experts_kernel,
        in_specs=[whole] + weights,
        out_specs=[column, column, column, whole],
        out_shape=[
            wide,
            wide,
            jax.ShapeDtypeStruct((rows, hidden), BF),
            jax.ShapeDtypeStruct((rows, width), BF),
        ],
        **common,
    )(x, experts_full, experts_full, experts_full)


def run_experts_back(d, gate, up, experts_full):
    rows, width = d.shape
    hidden = 2 * experts_full.shape[4]
    common, whole, weights, column = expert_specs(rows, width, hidden)
    low = jax.ShapeDtypeStruct((rows, hidden), BF)
    common["scratch_shapes"] = common["scratch_shapes"] + [pltpu.VMEM((rows, HALF), F32)]
    return pl.pallas_call(
        experts_back_kernel,
        in_specs=[whole, column, column] + weights,
        out_specs=[column, column, whole],
        out_shape=[low, low, jax.ShapeDtypeStruct((rows, width), BF)],
        **common,
    )(d, gate, up, experts_full, experts_full, experts_full)


def expert_grads(x, d, d_gate, d_up, inner):
    rows, width = x.shape
    hidden = inner.shape[1]
    common, whole, _, column = expert_specs(rows, width, hidden)
    common["scratch_shapes"] = [pltpu.VMEM((width, rows), BF)] * 2
    return pl.pallas_call(
        expert_grads_kernel,
        in_specs=[whole, whole, column, column, column],
        out_specs=pl.BlockSpec((4, 1, 3, width // 4, HALF), lambda b: (0, b // 2, 0, 0, b % 2)),
        out_shape=jax.ShapeDtypeStruct((4, 2, 3, width // 4, hidden // 2), BF),
        **common,
    )(x, d, d_gate, d_up, inner)


def grads_kernel(plan, first_axis, core_ref, *refs):
    ins, (own_ref, other_ref, pack) = refs[:-3], refs[-3:]
    at = 0
    turned = {}
    for terms in plan:
        total = None
        for left, right, first in terms:
            if left is None:
                high = ins[right][...].astype(BF).astype(F32)
                rest = ins[right][...] - high
                total = jnp.zeros((384, 128), F32) if total is None else total
                pack[:, at : at + 128] = total
                pack[:, at + 16 : at + 24] = high.T
                pack[:, at + 24 : at + 32] = rest.T
                total = None
                at = at + 128
                continue
            if left not in turned:
                turned[left] = ins[left][...].T
            width = ins[right].shape[1]
            rows = turned[left][:, first : first + width]
            piece = dot(rows, ins[right][...], 1, 1)
            total = piece if total is None else total + piece
        if total is not None:
            pack[:, at : at + total.shape[1]] = total
            at = at + total.shape[1]
    for core in range(2):

        @pl.when(core_ref[0] == core)
        def _(core=core):
            for j in range(2):
                for y in range(4):
                    for ref, c in ((own_ref, core), (other_ref, 1 - core)):
                        row = (2 * j + c) * 96 + y * 24
                        value = pack[row : row + 24, :].astype(BF)
                        if first_axis == "x":
                            ref[j, y, 0] = value
                        else:
                            ref[y, j, 0] = value


def pack_grads(plan, first_axis, arrays, wide, cols, flops):
    specs = []
    for i, value in enumerate(arrays):
        if i in wide:
            specs.append(pl.BlockSpec((value.shape[0], 384), lambda b: (0, b)))
        else:
            specs.append(pl.BlockSpec(value.shape, lambda b: (0, 0)))
    out = jax.ShapeDtypeStruct((4, 4, 2, 24, cols), BF)
    if first_axis == "x":
        out_spec = pl.BlockSpec((2, 4, 1, 24, cols), lambda b: (b % 2, 0, b // 2, 0, 0))
    else:
        out_spec = pl.BlockSpec((4, 2, 1, 24, cols), lambda b: (0, b % 2, b // 2, 0, 0))
    return pl.pallas_call(
        functools.partial(grads_kernel, plan, first_axis),
        grid=(arrays[wide[0]].shape[1] // 384,),
        in_specs=[pl.BlockSpec(memory_space=pltpu.SMEM)] + specs,
        out_specs=[out_spec, out_spec],
        out_shape=[out, out],
        scratch_shapes=[pltpu.VMEM((384, cols), F32)],
        compiler_params=pltpu.CompilerParams(
            vmem_limit_bytes=(60 if len(arrays) > 4 else 40) << 20
        ),
        cost_estimate=pl.CostEstimate(
            flops=flops, bytes_accessed=flops // 2000, transcendentals=0
        ),
    )(jnp.full((1,), lax.axis_index("c"), jnp.int32), *arrays)


def pair_blocks(own, theirs, axis):
    received = swap(theirs, "c")
    me = lax.axis_index(axis)
    blocks = []
    for r in range(4):
        mine, other = (
            lax.dynamic_index_in_dim(part, (me + r) % 4, 0, keepdims=False)
            for part in (own, received)
        )
        blocks.append(both(mine, other).astype(BF))
    return blocks


def send_blocks(blocks, axis):
    return blocks[:1] + [
        lax.ppermute(blocks[r], axis, [(i, (i + r) % 4) for i in range(4)]) for r in range(1, 4)
    ]


def local(
    tokens,
    teacher,
    segments,
    routes,
    route_weight,
    norm_attn,
    w_query,
    key_weight,
    value_weight,
    w_out,
    norm_ffn,
    w_router,
    w_gate,
    w_up,
    w_down,
):
    tok_rows, feat_width = tokens.shape
    q_width = w_query.shape[1]
    k_width = key_weight.shape[1]
    tix = lax.axis_index("t")
    yix = lax.axis_index("y")

    small = jnp.concatenate(
        [
            w_router,
            norm_attn[:, None],
            norm_ffn[:, None],
            jnp.zeros((w_router.shape[0], 128 - EXPERTS - 2), BF),
        ],
        axis=1,
    )
    experts = jnp.stack([w_gate[0], w_up[0], w_down[0].T])
    by_hy, experts = lax.optimization_barrier(
        (
            gather_hy(
                jnp.concatenate([key_weight, value_weight, small, w_query, w_out.T], axis=1)
            ),
            experts,
        )
    )
    kv_cols = 2 * k_width + 128
    wide_rest = by_hy[:, :, kv_cols:]
    wide_rest = jnp.broadcast_to(wide_rest[None], (4, *wide_rest.shape))
    ring_kv, wide_rest = lax.optimization_barrier((gather_x(by_hy[:, :, :kv_cols]), wide_rest))
    experts_other = swap(experts, "t")
    ring_rest = lax.all_to_all(wide_rest, "x", 0, 0, tiled=True)
    pack = core_gather(ring_kv)
    full_kv = pack[:, : 2 * k_width]
    full_small = pack[:, 2 * k_width :]
    small_rows = dot(jnp.eye(24, 128, dtype=BF), full_small, 1, 1)
    router_rows = small_rows[:EXPERTS].astype(BF)
    gain_one = small_rows[EXPERTS : EXPERTS + 1]
    gain_two = small_rows[EXPERTS + 1 : EXPERTS + 2]

    resid_in = tokens.astype(F32)
    scale_one = rms_scale(resid_in)
    act_one = (resid_in * scale_one * gain_one).astype(BF)
    kv_mine = dot(full_kv, act_one, 0, 1).astype(BF).reshape(2, k_width, tok_rows)
    kvs = [kv_mine] + [
        lax.ppermute(kv_mine, "y", [(i, i + r) for i in range(4 - r)]) for r in (1, 2, 3)
    ]
    experts_other, ring_rest = lax.optimization_barrier((experts_other, ring_rest))
    experts_full = jnp.stack([experts, experts_other])
    *kvs[1:], ring_rest, experts_full = lax.optimization_barrier(
        (*kvs[1:], ring_rest, experts_full)
    )
    rest = core_gather(ring_rest)
    full_query = rest[:, :q_width]
    full_out = rest[:, q_width:]
    query_t = dot(full_query, act_one, 0, 1).astype(BF)

    experts_full = lax.all_gather(experts_full, "y", axis=0)

    seg_blocks = segments[0].reshape(4, tok_rows)
    seg_mine = lax.dynamic_index_in_dim(seg_blocks, yix, 0, keepdims=False)
    seg_keys = jnp.concatenate(
        [lax.dynamic_index_in_dim(seg_blocks, (yix + 4 - r) % 4, 0, keepdims=False) for r in range(4)]
    )[:, None]
    place_y = jnp.full((1,), yix, jnp.int32)
    mixed_0, log_0 = attend(0, place_y, query_t, kvs, seg_mine[None], seg_keys)
    part_0 = dot(mixed_0, full_out, 0, 1).astype(BF)
    mixed_1, log_1 = attend(1, place_y, after(query_t, part_0), kvs, seg_mine[None], seg_keys)
    other_0 = swap(part_0, "t")
    part_1 = dot(after(mixed_1, other_0), full_out, 0, 1).astype(BF)
    other_1 = swap(part_1, "t")
    hidden = resid_in + jnp.concatenate([both(part_0, other_0), both(part_1, other_1)])
    scale_two = rms_scale(hidden)
    act_two = (hidden * scale_two * gain_two).astype(BF)

    logits = dot(router_rows, act_two, 1, 1)
    router = jax.nn.softmax(logits, axis=0)
    route_cols = routes.T
    weight_cols = route_weight.T
    expert_iota = lax.broadcasted_iota(jnp.int32, (EXPERTS, tok_rows), 0)
    named = [expert_iota == route_cols[k : k + 1] for k in range(TOP)]
    taken = (named[0] | named[1]).astype(BF)
    earlier = (
        lax.broadcasted_iota(jnp.int32, (tok_rows, tok_rows), 0)
        < lax.broadcasted_iota(jnp.int32, (tok_rows, tok_rows), 1)
    ).astype(BF)
    count_before = dot(taken, earlier, 1, 0)
    half = CAPACITY // 2
    slot_iota = lax.broadcasted_iota(jnp.int32, (EXPERTS * half, tok_rows), 0)
    picks = []
    gates = []
    for k in range(TOP):
        place = jnp.sum(jnp.where(named[k], count_before, 0.0), axis=0, keepdims=True)
        place = place.astype(jnp.int32) - tix * half
        slot = jnp.where((place >= 0) & (place < half), route_cols[k : k + 1] * half + place, -1)
        picks.append(slot_iota == slot)
        chosen = jnp.sum(jnp.where(named[k], router, 0.0), axis=0, keepdims=True)
        gates.append(chosen * weight_cols[k : k + 1])
    pick = (picks[0] | picks[1]).astype(BF)
    gated_pick = (
        jnp.where(picks[0], gates[0], 0.0) + jnp.where(picks[1], gates[1], 0.0)
    ).astype(BF)

    received, pick_t, gated_pick_t = lax.optimization_barrier(
        (exchange_slots(dot(pick, act_two, 1, 0).astype(BF)), pick.T, gated_pick.T)
    )
    gate_proj, up_proj, inner, slots_out = run_experts(received, experts_full)
    returned = exchange_slots(slots_out)
    part = dot(gated_pick_t, returned, 1, 0).astype(BF)
    output = hidden + both(part, swap(part, "t"))
    valid = (seg_mine != 0).astype(F32)
    difference = output - teacher.astype(F32)
    grad_output = difference * valid[:, None]
    sse = jnp.sum(grad_output * difference)
    count = jnp.sum(valid)
    grad_low = grad_output.astype(BF)
    d_received = exchange_slots(dot(gated_pick, grad_low, 1, 0).astype(BF))

    slot_dots = dot(returned, grad_low, 1, 1)
    d_gates = jnp.concatenate(
        [jnp.sum(jnp.where(picks[k], slot_dots, 0.0), axis=0, keepdims=True) for k in range(TOP)]
    )
    d_gates_other = swap(d_gates, "t")
    d_received = after(d_received, d_gates_other)
    d_gates = d_gates + d_gates_other

    d_gate_proj, d_up_proj, d_slots = run_experts_back(
        d_received, gate_proj, up_proj, experts_full
    )
    d_returned = exchange_slots(d_slots)
    received, d_received = after(received, d_slots), after(d_received, d_slots)

    grad_parts = expert_grads(received, d_received, d_gate_proj, d_up_proj, inner)
    grad_experts = lax.psum_scatter(grad_parts, "y", scatter_dimension=0)
    d_returned = after(d_returned, grad_parts)
    keep, give = grad_experts[0], grad_experts[1]

    d_router = jnp.where(named[0], d_gates[0:1] * weight_cols[0:1], 0.0) + jnp.where(
        named[1], d_gates[1:2] * weight_cols[1:2], 0.0
    )
    d_logits = (
        router * (d_router - jnp.sum(router * d_router, axis=0, keepdims=True))
    ).astype(BF)
    d_route = dot(d_logits, router_rows, 0, 0)
    part = dot(pick_t, d_returned, 1, 0).astype(BF)
    d_act_two = d_route + both(part, after(swap(part, "t"), d_route))
    d_norm_two, grad_gain_two = norm_back(hidden, scale_two, gain_two, d_act_two)
    d_hidden = grad_output + d_norm_two
    d_attn = d_hidden.astype(BF)
    d_mixed_t = dot(full_out, d_attn, 0, 1).astype(BF)

    saved = ((mixed_0, mixed_1), (log_0, log_1), kvs, seg_mine[None], seg_keys)
    half_groups = k_width // HEAD_WIDTH // 2
    back_0 = attend_back(0, half_groups, place_y, query_t, d_mixed_t, *saved)

    def ring_back(parts):
        return [
            lax.ppermute(parts[r], "y", [(i, i - r) for i in range(r, 4)]) for r in (1, 2, 3)
        ]

    *back_0, d_mixed_t, give = lax.optimization_barrier((*back_0, d_mixed_t, give))
    back_1 = attend_back(half_groups, half_groups, place_y, query_t, d_mixed_t, *saved)
    others_0 = ring_back(back_0[1:])
    given_0 = swap(give[:2], "t")
    *back_1, o1, o2, o3, given_0, give, d_attn_late, gain_late, d_logits_late, back_0[0] = (
        lax.optimization_barrier(
            (*back_1, *others_0, given_0, give[2], d_attn, grad_gain_two, d_logits, back_0[0])
        )
    )
    others_0 = [o1, o2, o3]

    others_1 = ring_back(back_1[1:])
    given_1 = swap(give, "t")
    lines = jnp.concatenate(
        [
            gain_late,
            jnp.full((1, feat_width), sse),
            jnp.full((1, feat_width), count),
            jnp.zeros((5, feat_width), F32),
        ]
    )
    logits_pad = jnp.concatenate(
        [d_logits_late, jnp.zeros((128 - EXPERTS, tok_rows), BF)]
    )
    own_one, theirs_one = pack_grads(
        (
            ((0, 4, 0), (0, 5, HALF)),
            ((2, 6, 0), (None, 3, 0)),
            ((1, 7, 0),),
            ((1, 8, 0),),
        ),
        "x",
        (d_attn_late, act_one, act_two, lines, mixed_0, mixed_1, logits_pad, back_0[0], back_1[0]),
        (0, 1, 2, 3),
        feat_width // 2 + 128 + q_width,
        20_000_000_000,
    )
    d_act_query = dot(jnp.concatenate([back_0[0], back_1[0]]), full_query, 0, 1)
    o1, o2, o3, given_1, own_one, theirs_one, d_act_query = lax.optimization_barrier(
        (*others_1, given_1, own_one, theirs_one, d_act_query)
    )

    d_kv_t = jnp.concatenate(
        [added([back_0[1], *others_0]), added([back_1[1], o1, o2, o3])], axis=1
    ).reshape(2 * k_width, tok_rows).astype(BF)
    d_act_part = d_act_query + dot(d_kv_t, full_kv, 0, 1)
    part = d_act_part.astype(BF)
    blocks_one = pair_blocks(own_one, theirs_one, "x")
    gain_row = jnp.sum(d_act_part * resid_in * scale_one, axis=0, keepdims=True)
    lines = jnp.concatenate(
        [gain_row, jnp.zeros((7, feat_width), F32)]
    )
    own_two, theirs_two = pack_grads(
        (((0, 2, 0),), ((None, 1, 0),)),
        "y",
        (act_one, lines, d_kv_t),
        (0, 1),
        2 * k_width + 128,
        2_000_000_000,
    )
    part, own_two, theirs_two, *blocks_one = lax.optimization_barrier(
        (part, own_two, theirs_two, *blocks_one)
    )
    other = swap(part, "t")
    parts_one = send_blocks(blocks_one, "x")
    paired_two = both(own_two, swap(theirs_two, "c")).astype(BF)
    ring_two = lax.all_to_all(paired_two, "y", 0, 0, tiled=True)
    grad_wide = keep[:2].astype(F32) + given_0.astype(F32)
    own_down = with_layout_constraint(both(keep[2], given_1).T, Layout(major_to_minor=(0, 1)))
    *parts_one, ring_two, own_down, other = lax.optimization_barrier(
        (*parts_one, ring_two, own_down, other)
    )
    by_x = added(parts_one).astype(BF)
    by_y = jnp.sum(ring_two.astype(F32), axis=0).astype(BF)
    by_xy = jnp.concatenate(
        [added(axis_parts(by_x, "y", 4)), added(axis_parts(by_y, "x", 4))], axis=2
    ).astype(BF)
    by_xy, other = lax.optimization_barrier((by_xy, other))
    summed = added(axis_parts(by_xy, "h", 2))
    own_kv = summed[:, by_x.shape[3] :]
    own_query = summed[:, feat_width // 2 + 128 : by_x.shape[3]]
    at = feat_width // 2
    own_out = summed[:, :at].T
    own_router = summed[:, at : at + EXPERTS]
    at = at + EXPERTS
    own_gain_two = summed[:, at] + summed[:, at + 8]
    loss_value = (summed[0, at + 1] + summed[0, at + 9]) / (
        feat_width * (summed[0, at + 2] + summed[0, at + 10])
    )
    own_gain_one = own_kv[:, 2 * k_width + EXPERTS] + own_kv[:, 2 * k_width + EXPERTS + 8]
    d_hidden_one, _ = norm_back(resid_in, scale_one, gain_one, both(part, other))
    grad_tokens = d_hidden + d_hidden_one
    own_gain_one = own_gain_one + swap(own_gain_one, "t")
    return (
        output,
        loss_value,
        grad_tokens,
        own_gain_one,
        own_query,
        own_kv[:, :k_width],
        own_kv[:, k_width : 2 * k_width],
        own_out,
        own_gain_two,
        own_router,
        grad_wide[0][None],
        grad_wide[1][None],
        own_down[None],
    )


def solution(mesh):
    fine = Mesh(mesh.devices.reshape(2, 4, 2, 4, 2), ("h", "x", "c", "y", "t"))
    fsdp = ("h", "x", "c")
    every = ("h", "x", "c", "y")
    return jax.shard_map(
        local,
        mesh=fine,
        in_specs=(
            P(every, None),
            P(every, None),
            P(fsdp, None),
            P(every, None),
            P(every, None),
            P(every),
            P(every, "t"),
            P(every, "t"),
            P(every, "t"),
            P("t", every),
            P(every),
            P(every, None),
            P(fsdp, "y", "t"),
            P(fsdp, "y", "t"),
            P(fsdp, "t", "y"),
        ),
        out_specs=(
            P(every, None),
            P(),
            P(every, None),
            P(every),
            P(every, "t"),
            P(every, "t"),
            P(every, "t"),
            P("t", every),
            P(every),
            P(every, None),
            P(fsdp, "y", "t"),
            P(fsdp, "y", "t"),
            P(fsdp, "t", "y"),
        ),
        check_vma=False,
    )
```

```python
import functools

import jax
import jax.numpy as jnp
from jax import lax
from jax.experimental import pallas as pl
from jax.experimental.pallas import tpu as pltpu
from jax.sharding import Mesh
from jax.sharding import PartitionSpec as P

QUERY_HEAD_COUNT = 24
KEY_VALUE_HEADS = 8
HEAD_WIDTH = 64
TOP = 2
EXPERTS = 16
CAPACITY = 96

EPSILON = 1e-06
MASKED = -1e30

BF = jnp.bfloat16
F32 = jnp.float32
RING = ("h", "x", "y")
GROUP = QUERY_HEAD_COUNT // KEY_VALUE_HEADS
SPAN = 512
HALF = 256


def dot(left, right, left_dim, right_dim):
    return lax.dot_general(
        left, right, (((left_dim,), (right_dim,)), ((), ())), preferred_element_type=F32
    )


def rms_scale(values):
    return lax.rsqrt(jnp.mean(values * values, axis=-1, keepdims=True) + EPSILON)


def norm_back(values, scale, gain_row, upstream):
    gained = upstream * gain_row
    grad_gain = jnp.sum(upstream * values * scale, axis=0, keepdims=True)
    middle = jnp.mean(values * gained, axis=-1, keepdims=True)
    return (scale * gained - values * scale * scale * scale * middle, grad_gain)


def swap(value, axis):
    return lax.ppermute(value, axis, [(0, 1), (1, 0)])


def both(mine, other):
    return mine.astype(F32) + other.astype(F32)


def gather_hy(shard):
    wide = jnp.broadcast_to(shard[None], (8, *shard.shape))
    return lax.all_to_all(wide, ("h", "y"), 0, 0, tiled=True)


def gather_x(shards):
    wide = jnp.broadcast_to(shards[None], (4, *shards.shape))
    return lax.all_to_all(wide, "x", 0, 0, tiled=True)


def core_gather(mine):
    rows, cols = mine.shape[2:]
    mine = mine.reshape(4, 2, 4 * rows, cols)
    other = swap(mine, "c")
    mine, other = mine.transpose(1, 0, 2, 3), other.transpose(1, 0, 2, 3)
    first = lax.axis_index("c") == 0
    pair = jnp.stack([jnp.where(first, mine, other), jnp.where(first, other, mine)], axis=2)
    return pair.reshape(64 * rows, cols)


def after(value, *earlier):
    return lax.optimization_barrier((value,) + earlier)[0]


def axis_parts(parts, axis, size):
    me = lax.axis_index(axis)
    mine = [lax.dynamic_index_in_dim(parts, me, 0, keepdims=False)]
    for r in range(1, size):
        block = lax.dynamic_index_in_dim(parts, (me + r) % size, 0, keepdims=False)
        mine.append(lax.ppermute(block, axis, [(i, (i + r) % size) for i in range(size)]))
    return mine


def added(parts):
    total = parts[0].astype(F32)
    for part in parts[1:]:
        total = total + part.astype(F32)
    return total


def exchange_slots(rows):
    width = rows.shape[1]
    return lax.all_to_all(
        rows.reshape(EXPERTS, -1, width), ("h", "x", "c"), 0, 0, tiled=True
    ).reshape(-1, width)


def nn(a,b):
    return lax.dot_general(a,b,(((1,),(0,)),((),())),preferred_element_type=F32)

def fold(v, op):
    return op(v.reshape(v.shape[0]//8,8,v.shape[1]),axis=0)

def write_bias(bias, seg_q, seg_k, y, half):
    width = bias.shape[2]
    for r in range(4):

        def one(r=r):
            same = seg_k[r * SPAN : (r + 1) * SPAN, :] == seg_q[...]
            if r == 0:
                key_place = lax.broadcasted_iota(jnp.int32, (SPAN, width), 0)
                query_place = lax.broadcasted_iota(jnp.int32, (SPAN, width), 1) + half * HALF
                same = same & (key_place <= query_place)
            bias[r] = jnp.where(same, 0.0, MASKED)

        pl.when(y >= r)(one)


def fwd_kernel(
    half, y_ref, q_ref, kv0, kv1, kv2, kv3, seg_q, seg_k, o_ref, lse_ref, bias, kn, vt, sc
):
    y = y_ref[0]

    @pl.when(pl.program_id(0) == 0)
    def _():
        write_bias(bias, seg_q, seg_k, y, half)

    for r, kv in enumerate((kv0, kv1, kv2, kv3)):

        def fill(r=r, kv=kv):
            kn[r] = kv[0].T
            vt[r] = kv[1]

        pl.when(y >= r)(fill)
    scale = jnp.asarray(HEAD_WIDTH**-0.5, BF)
    qs = [q_ref[h * HEAD_WIDTH : (h + 1) * HEAD_WIDTH] * scale for h in range(GROUP)]

    def scores(r, rows, tops):
        out = []
        for h in range(GROUP):
            s = nn(kn[r, rows, :], qs[h]) + bias[r, rows, :]
            sc[h, r, rows, :] = s
            out.append(jnp.maximum(tops[h], fold(s, jnp.max)))
        return tuple(out)

    own = slice(0, (half + 1) * HALF)
    low = tuple(jnp.full((8, HALF), MASKED, F32) for _ in range(GROUP))
    tops = scores(0, own, low)
    tops = lax.fori_loop(1, y + 1, lambda r, t: scores(r, slice(0, SPAN), t), tops)
    tops = [jnp.max(t, axis=0, keepdims=True) for t in tops]

    def mix(r, rows, carry):
        totals, acc = carry
        out, weights = [], []
        for h in range(GROUP):
            p = jnp.exp(sc[h, r, rows, :] - tops[h])
            out.append(totals[h] + fold(p, jnp.sum))
            weights.append(p.astype(BF))
        return tuple(out), acc + nn(vt[r, :, rows], jnp.concatenate(weights, 1))

    zero = (
        tuple(jnp.zeros((8, HALF), F32) for _ in range(GROUP)),
        jnp.zeros((HEAD_WIDTH, GROUP * HALF), F32),
    )
    carry = mix(0, own, zero)
    totals, acc = lax.fori_loop(1, y + 1, lambda r, c: mix(r, slice(0, SPAN), c), carry)
    for h in range(GROUP):
        total = jnp.sum(totals[h], axis=0, keepdims=True)
        mixed = acc[:, h * HALF : (h + 1) * HALF] / total
        o_ref[h * HEAD_WIDTH : (h + 1) * HEAD_WIDTH, :] = mixed.astype(BF)
        lse_ref[0, h : h + 1, :] = tops[h] + jnp.log(total)


def attend(half, y, q_t, kvs, seg_q, seg_k):
    rows = GROUP * HEAD_WIDTH
    heads = q_t.shape[0] // rows
    kv_spec = pl.BlockSpec((2, HEAD_WIDTH, SPAN), lambda g: (0, g, 0))
    return pl.pallas_call(
        functools.partial(fwd_kernel, half),
        grid=(heads,),
        in_specs=[
            pl.BlockSpec(memory_space=pltpu.SMEM),
            pl.BlockSpec((rows, HALF), lambda g: (g, half)),
            kv_spec,
            kv_spec,
            kv_spec,
            kv_spec,
            pl.BlockSpec((1, HALF), lambda g: (0, half)),
            pl.BlockSpec((4 * SPAN, 1), lambda g: (0, 0)),
        ],
        out_specs=[
            pl.BlockSpec((rows, HALF), lambda g: (g, 0)),
            pl.BlockSpec((1, 8, HALF), lambda g: (g, 0, 0)),
        ],
        out_shape=[
            jax.ShapeDtypeStruct((q_t.shape[0], HALF), BF),
            jax.ShapeDtypeStruct((heads, 8, HALF), F32),
        ],
        scratch_shapes=[
            pltpu.VMEM((4, SPAN, HALF), F32),
            pltpu.VMEM((4, SPAN, HEAD_WIDTH), BF),
            pltpu.VMEM((4, HEAD_WIDTH, SPAN), BF),
            pltpu.VMEM((GROUP, 4, SPAN, HALF), F32),
        ],
        compiler_params=pltpu.CompilerParams(vmem_limit_bytes=40 << 20),
        cost_estimate=pl.CostEstimate(
            flops=14_000_000_000, bytes_accessed=6_000_000, transcendentals=6_000_000
        ),
    )(y, q_t, *kvs, seg_q, seg_k)


def bwd_kernel(y_ref, q_ref, d_ref, o_0, o_1, lse_0, lse_1, kv0, kv1, kv2, kv3, seg_q, seg_k, dq_ref, g0, g1, g2, g3, bias, kn, vn, kt, dvk):
    y = y_ref[0]
    @pl.when(pl.program_id(0)==0)
    def _(): write_bias(bias, seg_q, seg_k, y, 0)
    for r,kv in enumerate((kv0,kv1,kv2,kv3)):
        def fill(r=r,kv=kv):
            kn[r] = kv[0].T
            vn[r] = kv[1].T
            kt[r] = kv[0]
        pl.when(y>=r)(fill)
    dvk[...] = jnp.zeros_like(dvk)
    scale = jnp.asarray(HEAD_WIDTH**-0.5, BF)
    for b in range(2):
        cols = slice(b*HALF,(b+1)*HALF)
        qs, qn, ds, dn, dots, lses = [],[],[],[],[],[]
        for h in range(GROUP):
            hr = slice(h*HEAD_WIDTH,(h+1)*HEAD_WIDTH)
            q = q_ref[hr, cols]*scale
            qs.append(q); qn.append(q.T)
            d = d_ref[hr, cols]
            ds.append(d); dn.append(d.T)
            dots.append(jnp.sum(d.astype(F32)*(o_0, o_1)[b][hr].astype(F32),axis=0,keepdims=True))
            lses.append((lse_0, lse_1)[b][0, h : h + 1])
        right = []
        for h in range(GROUP):
            none = jnp.zeros_like(dn[h])
            right += [jnp.concatenate([dn[h], none], 1), jnp.concatenate([none, qn[h]], 1)]
        right = jnp.concatenate(right, 0)

        def step(r, rows, carry):
            left = []
            for h in range(GROUP):
                s = nn(kn[r, rows, :], qs[h]) + bias[r, rows, cols]
                p = jnp.exp(s - lses[h])
                dp = nn(vn[r, rows, :], ds[h])
                dsc = (p * (dp - dots[h])).astype(BF)
                left += [p.astype(BF), dsc]
            dvk[r, rows, :] += nn(jnp.concatenate(left, 1), right)
            return carry + nn(kt[r, :, rows], jnp.concatenate(left[1::2], 1))

        carry = step(0, slice(0, (b + 1) * HALF), jnp.zeros((HEAD_WIDTH, GROUP * HALF), F32))
        carry = lax.fori_loop(1, y+1, lambda r,c: step(r, slice(0,SPAN), c), carry)
        for h in range(GROUP):
            dq_ref[h*HEAD_WIDTH:(h+1)*HEAD_WIDTH, cols] = (
                carry[:, h * HALF : (h + 1) * HALF] * HEAD_WIDTH**-0.5
            ).astype(BF)
    for r,g in enumerate((g0,g1,g2,g3)):
        turned = dvk[r].T.astype(BF)
        g[0] = turned[HEAD_WIDTH:]
        g[1] = turned[:HEAD_WIDTH]

def attend_back(first, count, y, q_t, d_t, outs, lses, kvs, seg_q, seg_k):
    rows = GROUP * HEAD_WIDTH
    kv_spec = pl.BlockSpec((2, HEAD_WIDTH, SPAN), lambda g: (0, first + g, 0))
    q_spec = pl.BlockSpec((rows, SPAN), lambda g: (first + g, 0))
    o_spec = pl.BlockSpec((rows, HALF), lambda g: (first + g, 0))
    lse_spec = pl.BlockSpec((1, 8, HALF), lambda g: (first + g, 0, 0))
    kv_shape = jax.ShapeDtypeStruct((2, count * HEAD_WIDTH, SPAN), BF)
    return pl.pallas_call(
        bwd_kernel,
        grid=(count,),
        in_specs=[pl.BlockSpec(memory_space=pltpu.SMEM), q_spec, q_spec]
        + [o_spec, o_spec, lse_spec, lse_spec]
        + [kv_spec] * 4
        + [pl.BlockSpec((1, SPAN), lambda g: (0, 0)), pl.BlockSpec((4 * SPAN, 1), lambda g: (0, 0))],
        out_specs=[pl.BlockSpec((rows, SPAN), lambda g: (g, 0))]
        + [pl.BlockSpec((2, HEAD_WIDTH, SPAN), lambda g: (0, g, 0))] * 4,
        out_shape=[jax.ShapeDtypeStruct((count * rows, SPAN), BF)] + [kv_shape] * 4,
        scratch_shapes=[pltpu.VMEM((4, SPAN, SPAN), F32)]
        + [pltpu.VMEM((4, SPAN, HEAD_WIDTH), BF)] * 2
        + [pltpu.VMEM((4, HEAD_WIDTH, SPAN), BF)]
        + [pltpu.VMEM((4, SPAN, 2 * HEAD_WIDTH), F32)],
        compiler_params=pltpu.CompilerParams(vmem_limit_bytes=60 << 20),
        cost_estimate=pl.CostEstimate(
            flops=150_000_000_000, bytes_accessed=6_000_000, transcendentals=6_000_000
        ),
    )(y, q_t, d_t, *outs, *lses, *kvs, seg_q, seg_k)


def flat(ref):
    return ref[...].reshape(ref.shape[0] * ref.shape[3], ref.shape[4])


def experts_kernel(x_ref, gate_ref, up_ref, down_ref, g_ref, u_ref, inner_ref, out_ref, acc):
    step = pl.program_id(0)
    down_t = flat(down_ref).T

    @pl.when(step == 0)
    def _():
        acc[...] = jnp.zeros_like(acc)

    x = x_ref[...]
    g_ref[...] = nn(x, flat(gate_ref))
    u_ref[...] = nn(x, flat(up_ref))
    for m in range(x_ref.shape[0] // HALF):
        rows = slice(m * HALF, (m + 1) * HALF)
        gate = g_ref[rows]
        inner_ref[rows] = (gate * jax.nn.sigmoid(gate) * u_ref[rows]).astype(BF)
    for n in range(acc.shape[1] // SPAN):
        cols = slice(n * SPAN, (n + 1) * SPAN)
        acc[:, cols] += nn(inner_ref[...], down_t[:, cols])

    @pl.when(step == pl.num_programs(0) - 1)
    def _():
        out_ref[...] = acc[...].astype(BF)


def experts_back_kernel(
    d_ref, g_ref, u_ref, gate_ref, up_ref, down_ref, dg_ref, du_ref, out_ref, acc, inner
):
    step = pl.program_id(0)
    gate_t = flat(gate_ref).T
    up_t = flat(up_ref).T

    @pl.when(step == 0)
    def _():
        acc[...] = jnp.zeros_like(acc)

    inner[...] = nn(d_ref[...], flat(down_ref))
    for m in range(d_ref.shape[0] // HALF):
        rows = slice(m * HALF, (m + 1) * HALF)
        d_inner = inner[rows]
        gate = g_ref[rows]
        sig = jax.nn.sigmoid(gate)
        dg_ref[rows] = (d_inner * u_ref[rows] * sig * (1.0 + gate * (1.0 - sig))).astype(BF)
        du_ref[rows] = (d_inner * gate * sig).astype(BF)
    for n in range(acc.shape[1] // SPAN):
        cols = slice(n * SPAN, (n + 1) * SPAN)
        acc[:, cols] += nn(dg_ref[...], gate_t[:, cols]) + nn(du_ref[...], up_t[:, cols])

    @pl.when(step == pl.num_programs(0) - 1)
    def _():
        out_ref[...] = acc[...].astype(BF)


def expert_grads_kernel(x_ref, d_ref, dg_ref, du_ref, inner_ref, out_ref, x_t, d_t):
    @pl.when(pl.program_id(0) == 0)
    def _():
        x_t[...] = x_ref[...].T
        d_t[...] = d_ref[...].T

    depth = out_ref.shape[3]
    for i, (left, right) in enumerate(((x_t, dg_ref), (x_t, du_ref), (d_t, inner_ref))):
        for y in range(4):
            out_ref[y, 0, i] = nn(left[y * depth : (y + 1) * depth], right[...]).astype(BF)


def expert_specs(rows, width, hidden):
    whole = pl.BlockSpec((rows, width), lambda b: (0, 0))
    weights = [
        pl.BlockSpec(
            (4, 1, 1, width // 4, HALF),
            functools.partial(lambda i, b: (0, b // 2, i, 0, b % 2), i),
        )
        for i in range(3)
    ]
    column = pl.BlockSpec((rows, HALF), lambda b: (0, b))
    return dict(
        grid=(hidden // HALF,),
        scratch_shapes=[pltpu.VMEM((rows, width), F32)],
        compiler_params=pltpu.CompilerParams(vmem_limit_bytes=60 << 20),
        cost_estimate=pl.CostEstimate(
            flops=6 * rows * width * hidden, bytes_accessed=20_000_000, transcendentals=rows * hidden
        ),
    ), whole, weights, column


def run_experts(x, experts_full):
    rows, width = x.shape
    hidden = 2 * experts_full.shape[4]
    common, whole, weights, column = expert_specs(rows, width, hidden)
    wide = jax.ShapeDtypeStruct((rows, hidden), F32)
    return pl.pallas_call(
        experts_kernel,
        in_specs=[whole] + weights,
        out_specs=[column, column, column, whole],
        out_shape=[
            wide,
            wide,
            jax.ShapeDtypeStruct((rows, hidden), BF),
            jax.ShapeDtypeStruct((rows, width), BF),
        ],
        **common,
    )(x, experts_full, experts_full, experts_full)


def run_experts_back(d, gate, up, experts_full):
    rows, width = d.shape
    hidden = 2 * experts_full.shape[4]
    common, whole, weights, column = expert_specs(rows, width, hidden)
    low = jax.ShapeDtypeStruct((rows, hidden), BF)
    common["scratch_shapes"] = common["scratch_shapes"] + [pltpu.VMEM((rows, HALF), F32)]
    return pl.pallas_call(
        experts_back_kernel,
        in_specs=[whole, column, column] + weights,
        out_specs=[column, column, whole],
        out_shape=[low, low, jax.ShapeDtypeStruct((rows, width), BF)],
        **common,
    )(d, gate, up, experts_full, experts_full, experts_full)


def expert_grads(x, d, d_gate, d_up, inner):
    rows, width = x.shape
    hidden = inner.shape[1]
    common, whole, _, column = expert_specs(rows, width, hidden)
    common["scratch_shapes"] = [pltpu.VMEM((width, rows), BF)] * 2
    return pl.pallas_call(
        expert_grads_kernel,
        in_specs=[whole, whole, column, column, column],
        out_specs=pl.BlockSpec((4, 1, 3, width // 4, HALF), lambda b: (0, b // 2, 0, 0, b % 2)),
        out_shape=jax.ShapeDtypeStruct((4, 2, 3, width // 4, hidden // 2), BF),
        **common,
    )(x, d, d_gate, d_up, inner)


def grads_kernel(plan, first_axis, core_ref, *refs):
    ins, (own_ref, other_ref, pack) = refs[:-3], refs[-3:]
    at = 0
    turned = {}
    for terms in plan:
        total = None
        for left, right, first in terms:
            if left is None:
                high = ins[right][...].astype(BF).astype(F32)
                rest = ins[right][...] - high
                total = jnp.zeros((384, 128), F32) if total is None else total
                pack[:, at : at + 128] = total
                pack[:, at + 16 : at + 24] = high.T
                pack[:, at + 24 : at + 32] = rest.T
                total = None
                at = at + 128
                continue
            if left not in turned:
                turned[left] = ins[left][...].T
            width = ins[right].shape[1]
            rows = turned[left][:, first : first + width]
            piece = dot(rows, ins[right][...], 1, 1)
            total = piece if total is None else total + piece
        if total is not None:
            pack[:, at : at + total.shape[1]] = total
            at = at + total.shape[1]
    for core in range(2):

        @pl.when(core_ref[0] == core)
        def _(core=core):
            for j in range(2):
                for y in range(4):
                    for ref, c in ((own_ref, core), (other_ref, 1 - core)):
                        row = (2 * j + c) * 96 + y * 24
                        value = pack[row : row + 24, :].astype(BF)
                        if first_axis == "x":
                            ref[j, y, 0] = value
                        else:
                            ref[y, j, 0] = value


def pack_grads(plan, first_axis, arrays, wide, cols, flops):
    specs = []
    for i, value in enumerate(arrays):
        if i in wide:
            specs.append(pl.BlockSpec((value.shape[0], 384), lambda b: (0, b)))
        else:
            specs.append(pl.BlockSpec(value.shape, lambda b: (0, 0)))
    out = jax.ShapeDtypeStruct((4, 4, 2, 24, cols), BF)
    if first_axis == "x":
        out_spec = pl.BlockSpec((2, 4, 1, 24, cols), lambda b: (b % 2, 0, b // 2, 0, 0))
    else:
        out_spec = pl.BlockSpec((4, 2, 1, 24, cols), lambda b: (0, b % 2, b // 2, 0, 0))
    return pl.pallas_call(
        functools.partial(grads_kernel, plan, first_axis),
        grid=(arrays[wide[0]].shape[1] // 384,),
        in_specs=[pl.BlockSpec(memory_space=pltpu.SMEM)] + specs,
        out_specs=[out_spec, out_spec],
        out_shape=[out, out],
        scratch_shapes=[pltpu.VMEM((384, cols), F32)],
        compiler_params=pltpu.CompilerParams(
            vmem_limit_bytes=40 << 20
        ),
        cost_estimate=pl.CostEstimate(
            flops=flops, bytes_accessed=flops // 2000, transcendentals=0
        ),
    )(jnp.full((1,), lax.axis_index("c"), jnp.int32), *arrays)


def pair_blocks(own, theirs, axis):
    received = swap(theirs, "c")
    me = lax.axis_index(axis)
    blocks = []
    for r in range(4):
        mine, other = (
            lax.dynamic_index_in_dim(part, (me + r) % 4, 0, keepdims=False)
            for part in (own, received)
        )
        blocks.append(both(mine, other).astype(BF))
    return blocks


def send_blocks(blocks, axis):
    return blocks[:1] + [
        lax.ppermute(blocks[r], axis, [(i, (i + r) % 4) for i in range(4)]) for r in range(1, 4)
    ]


def local(
    tokens,
    teacher,
    segments,
    routes,
    route_weight,
    norm_attn,
    w_query,
    key_weight,
    value_weight,
    w_out,
    norm_ffn,
    w_router,
    w_gate,
    w_up,
    w_down,
):
    tok_rows, feat_width = tokens.shape
    q_width = w_query.shape[1]
    k_width = key_weight.shape[1]
    tix = lax.axis_index("t")
    yix = lax.axis_index("y")

    small = jnp.concatenate(
        [
            w_router,
            norm_attn[:, None],
            norm_ffn[:, None],
            jnp.zeros((w_router.shape[0], 128 - EXPERTS - 2), BF),
        ],
        axis=1,
    )
    experts = jnp.stack([w_gate[0], w_up[0], w_down[0].T])
    by_hy, experts = lax.optimization_barrier(
        (
            gather_hy(
                jnp.concatenate([key_weight, value_weight, small, w_query, w_out.T], axis=1)
            ),
            experts,
        )
    )
    kv_cols = 2 * k_width + 128
    wide_rest = by_hy[:, :, kv_cols:]
    wide_rest = jnp.broadcast_to(wide_rest[None], (4, *wide_rest.shape))
    ring_kv, wide_rest = lax.optimization_barrier((gather_x(by_hy[:, :, :kv_cols]), wide_rest))
    experts_other = swap(experts, "t")
    ring_rest = lax.all_to_all(wide_rest, "x", 0, 0, tiled=True)
    pack = core_gather(ring_kv)
    full_kv = pack[:, : 2 * k_width]
    full_small = pack[:, 2 * k_width :]
    small_rows = dot(jnp.eye(24, 128, dtype=BF), full_small, 1, 1)
    router_rows = small_rows[:EXPERTS].astype(BF)
    gain_one = small_rows[EXPERTS : EXPERTS + 1]
    gain_two = small_rows[EXPERTS + 1 : EXPERTS + 2]

    resid_in = tokens.astype(F32)
    scale_one = rms_scale(resid_in)
    act_one = (resid_in * scale_one * gain_one).astype(BF)
    kv_mine = dot(full_kv, act_one, 0, 1).astype(BF).reshape(2, k_width, tok_rows)
    kvs = [kv_mine] + [
        lax.ppermute(kv_mine, "y", [(i, i + r) for i in range(4 - r)]) for r in (1, 2, 3)
    ]
    experts_other, ring_rest = lax.optimization_barrier((experts_other, ring_rest))
    experts_full = jnp.stack([experts, experts_other])
    *kvs[1:], ring_rest, experts_full = lax.optimization_barrier(
        (*kvs[1:], ring_rest, experts_full)
    )
    rest = core_gather(ring_rest)
    full_query = rest[:, :q_width]
    full_out = rest[:, q_width:]
    query_t = dot(full_query, act_one, 0, 1).astype(BF)

    experts_full = lax.all_gather(experts_full, "y", axis=0)

    seg_blocks = segments[0].reshape(4, tok_rows)
    seg_mine = lax.dynamic_index_in_dim(seg_blocks, yix, 0, keepdims=False)
    seg_keys = jnp.concatenate(
        [lax.dynamic_index_in_dim(seg_blocks, (yix + 4 - r) % 4, 0, keepdims=False) for r in range(4)]
    )[:, None]
    place_y = jnp.full((1,), yix, jnp.int32)
    mixed_0, log_0 = attend(0, place_y, query_t, kvs, seg_mine[None], seg_keys)
    part_0 = dot(mixed_0, full_out, 0, 1).astype(BF)
    mixed_1, log_1 = attend(1, place_y, after(query_t, part_0), kvs, seg_mine[None], seg_keys)
    other_0 = swap(part_0, "t")
    part_1 = dot(after(mixed_1, other_0), full_out, 0, 1).astype(BF)
    other_1 = swap(part_1, "t")
    hidden = resid_in + jnp.concatenate([both(part_0, other_0), both(part_1, other_1)])
    scale_two = rms_scale(hidden)
    act_two = (hidden * scale_two * gain_two).astype(BF)

    logits = dot(router_rows, act_two, 1, 1)
    router = jax.nn.softmax(logits, axis=0)
    route_cols = routes.T
    weight_cols = route_weight.T
    expert_iota = lax.broadcasted_iota(jnp.int32, (EXPERTS, tok_rows), 0)
    named = [expert_iota == route_cols[k : k + 1] for k in range(TOP)]
    taken = (named[0] | named[1]).astype(BF)
    earlier = (
        lax.broadcasted_iota(jnp.int32, (tok_rows, tok_rows), 0)
        < lax.broadcasted_iota(jnp.int32, (tok_rows, tok_rows), 1)
    ).astype(BF)
    count_before = dot(taken, earlier, 1, 0)
    half = CAPACITY // 2
    slot_iota = lax.broadcasted_iota(jnp.int32, (EXPERTS * half, tok_rows), 0)
    picks = []
    gates = []
    for k in range(TOP):
        place = jnp.sum(jnp.where(named[k], count_before, 0.0), axis=0, keepdims=True)
        place = place.astype(jnp.int32) - tix * half
        slot = jnp.where((place >= 0) & (place < half), route_cols[k : k + 1] * half + place, -1)
        picks.append(slot_iota == slot)
        chosen = jnp.sum(jnp.where(named[k], router, 0.0), axis=0, keepdims=True)
        gates.append(chosen * weight_cols[k : k + 1])
    pick = (picks[0] | picks[1]).astype(BF)
    gated_pick = (
        jnp.where(picks[0], gates[0], 0.0) + jnp.where(picks[1], gates[1], 0.0)
    ).astype(BF)

    received, pick_t, gated_pick_t = lax.optimization_barrier(
        (exchange_slots(dot(pick, act_two, 1, 0).astype(BF)), pick.T, gated_pick.T)
    )
    gate_proj, up_proj, inner, slots_out = run_experts(received, experts_full)
    returned = exchange_slots(slots_out)
    part = dot(gated_pick_t, returned, 1, 0).astype(BF)
    output = hidden + both(part, swap(part, "t"))
    valid = (seg_mine != 0).astype(F32)
    difference = output - teacher.astype(F32)
    grad_output = difference * valid[:, None]
    sse = jnp.sum(grad_output * difference)
    count = jnp.sum(valid)
    grad_low = grad_output.astype(BF)
    d_received = exchange_slots(dot(gated_pick, grad_low, 1, 0).astype(BF))

    slot_dots = dot(returned, grad_low, 1, 1)
    d_gates = jnp.concatenate(
        [jnp.sum(jnp.where(picks[k], slot_dots, 0.0), axis=0, keepdims=True) for k in range(TOP)]
    )
    d_gates_other = swap(d_gates, "t")
    d_received = after(d_received, d_gates_other)
    d_gates = d_gates + d_gates_other

    d_gate_proj, d_up_proj, d_slots = run_experts_back(
        d_received, gate_proj, up_proj, experts_full
    )
    d_returned = exchange_slots(d_slots)
    received, d_received = after(received, d_slots), after(d_received, d_slots)

    grad_parts = expert_grads(received, d_received, d_gate_proj, d_up_proj, inner)
    grad_experts = lax.psum_scatter(grad_parts, "y", scatter_dimension=0)
    d_returned = after(d_returned, grad_parts)
    keep, give = grad_experts[0], grad_experts[1]

    d_router = jnp.where(named[0], d_gates[0:1] * weight_cols[0:1], 0.0) + jnp.where(
        named[1], d_gates[1:2] * weight_cols[1:2], 0.0
    )
    d_logits = (
        router * (d_router - jnp.sum(router * d_router, axis=0, keepdims=True))
    ).astype(BF)
    d_route = dot(d_logits, router_rows, 0, 0)
    part = dot(pick_t, d_returned, 1, 0).astype(BF)
    d_act_two = d_route + both(part, after(swap(part, "t"), d_route))
    d_norm_two, grad_gain_two = norm_back(hidden, scale_two, gain_two, d_act_two)
    d_hidden = grad_output + d_norm_two
    d_attn = d_hidden.astype(BF)
    d_mixed_t = dot(full_out, d_attn, 0, 1).astype(BF)

    saved = ((mixed_0, mixed_1), (log_0, log_1), kvs, seg_mine[None], seg_keys)
    half_groups = k_width // HEAD_WIDTH // 2
    back_0 = attend_back(0, half_groups, place_y, query_t, d_mixed_t, *saved)

    def ring_back(parts):
        return [
            lax.ppermute(parts[r], "y", [(i, i - r) for i in range(r, 4)]) for r in (1, 2, 3)
        ]

    *back_0, d_mixed_t, give = lax.optimization_barrier((*back_0, d_mixed_t, give))
    back_1 = attend_back(half_groups, half_groups, place_y, query_t, d_mixed_t, *saved)
    others_0 = ring_back(back_0[1:])
    given_0 = swap(give[:2], "t")
    *back_1, o1, o2, o3, given_0, give, d_attn_late, gain_late, d_logits_late, back_0[0] = (
        lax.optimization_barrier(
            (*back_1, *others_0, given_0, give[2], d_attn, grad_gain_two, d_logits, back_0[0])
        )
    )
    others_0 = [o1, o2, o3]

    others_1 = ring_back(back_1[1:])
    given_1 = swap(give, "t")
    lines = jnp.concatenate(
        [
            gain_late,
            jnp.full((1, feat_width), sse),
            jnp.full((1, feat_width), count),
            jnp.zeros((5, feat_width), F32),
        ]
    )
    logits_pad = jnp.concatenate(
        [d_logits_late, jnp.zeros((128 - EXPERTS, tok_rows), BF)]
    )
    own_one, theirs_one = pack_grads(
        (
            ((0, 4, 0), (0, 5, HALF)),
            ((2, 6, 0), (None, 3, 0)),
            ((1, 7, 0),),
            ((1, 8, 0),),
        ),
        "x",
        (d_attn_late, act_one, act_two, lines, mixed_0, mixed_1, logits_pad, back_0[0], back_1[0]),
        (0, 1, 2, 3),
        feat_width // 2 + 128 + q_width,
        20_000_000_000,
    )
    d_act_query = dot(jnp.concatenate([back_0[0], back_1[0]]), full_query, 0, 1)
    o1, o2, o3, given_1, own_one, theirs_one, d_act_query = lax.optimization_barrier(
        (*others_1, given_1, own_one, theirs_one, d_act_query)
    )

    d_kv_t = jnp.concatenate(
        [added([back_0[1], *others_0]), added([back_1[1], o1, o2, o3])], axis=1
    ).reshape(2 * k_width, tok_rows).astype(BF)
    d_act_part = d_act_query + dot(d_kv_t, full_kv, 0, 1)
    part = d_act_part.astype(BF)
    blocks_one = pair_blocks(own_one, theirs_one, "x")
    gain_row = jnp.sum(d_act_part * resid_in * scale_one, axis=0, keepdims=True)
    lines = jnp.concatenate(
        [gain_row, jnp.zeros((7, feat_width), F32)]
    )
    own_two, theirs_two = pack_grads(
        (((0, 2, 0),), ((None, 1, 0),)),
        "y",
        (act_one, lines, d_kv_t),
        (0, 1),
        2 * k_width + 128,
        2_000_000_000,
    )
    part, own_two, theirs_two, *blocks_one = lax.optimization_barrier(
        (part, own_two, theirs_two, *blocks_one)
    )
    other = swap(part, "t")
    parts_one = send_blocks(blocks_one, "x")
    paired_two = both(own_two, swap(theirs_two, "c")).astype(BF)
    ring_two = lax.all_to_all(paired_two, "y", 0, 0, tiled=True)
    grad_wide = keep[:2].astype(F32) + given_0.astype(F32)
    own_down = both(keep[2], given_1).T
    *parts_one, ring_two, own_down, other = lax.optimization_barrier(
        (*parts_one, ring_two, own_down, other)
    )
    by_x = added(parts_one).astype(BF)
    by_y = jnp.sum(ring_two.astype(F32), axis=0).astype(BF)
    by_xy = jnp.concatenate(
        [added(axis_parts(by_x, "y", 4)), added(axis_parts(by_y, "x", 4))], axis=2
    ).astype(BF)
    by_xy, other = lax.optimization_barrier((by_xy, other))
    summed = added(axis_parts(by_xy, "h", 2))
    own_kv = summed[:, by_x.shape[3] :]
    own_query = summed[:, feat_width // 2 + 128 : by_x.shape[3]]
    at = feat_width // 2
    own_out = summed[:, :at].T
    own_router = summed[:, at : at + EXPERTS]
    at = at + EXPERTS
    own_gain_two = summed[:, at] + summed[:, at + 8]
    loss_value = (summed[0, at + 1] + summed[0, at + 9]) / (
        feat_width * (summed[0, at + 2] + summed[0, at + 10])
    )
    own_gain_one = own_kv[:, 2 * k_width + EXPERTS] + own_kv[:, 2 * k_width + EXPERTS + 8]
    d_hidden_one, _ = norm_back(resid_in, scale_one, gain_one, both(part, other))
    grad_tokens = d_hidden + d_hidden_one
    own_gain_one = own_gain_one + swap(own_gain_one, "t")
    return (
        output,
        loss_value,
        grad_tokens,
        own_gain_one,
        own_query,
        own_kv[:, :k_width],
        own_kv[:, k_width : 2 * k_width],
        own_out,
        own_gain_two,
        own_router,
        grad_wide[0][None],
        grad_wide[1][None],
        own_down[None],
    )


def solution(mesh):
    fine = Mesh(mesh.devices.reshape(2, 4, 2, 4, 2), ("h", "x", "c", "y", "t"))
    fsdp = ("h", "x", "c")
    every = ("h", "x", "c", "y")
    return jax.shard_map(
        local,
        mesh=fine,
        in_specs=(
            P(every, None),
            P(every, None),
            P(fsdp, None),
            P(every, None),
            P(every, None),
            P(every),
            P(every, "t"),
            P(every, "t"),
            P(every, "t"),
            P("t", every),
            P(every),
            P(every, None),
            P(fsdp, "y", "t"),
            P(fsdp, "y", "t"),
            P(fsdp, "t", "y"),
        ),
        out_specs=(
            P(every, None),
            P(),
            P(every, None),
            P(every),
            P(every, "t"),
            P(every, "t"),
            P(every, "t"),
            P("t", every),
            P(every),
            P(every, None),
            P(fsdp, "y", "t"),
            P(fsdp, "y", "t"),
            P(fsdp, "t", "y"),
        ),
        check_vma=False,
    )
```

```python
import functools

import jax
import jax.numpy as jnp
from jax import lax
from jax.experimental import pallas as pl
from jax.experimental.pallas import tpu as pltpu
from jax.sharding import Mesh
from jax.sharding import PartitionSpec as P

QUERY_HEAD_COUNT = 24
KEY_VALUE_HEADS = 8
HEAD_WIDTH = 64
TOP = 2
EXPERTS = 16
CAPACITY = 96

EPSILON = 1e-06
MASKED = -1e30

BF = jnp.bfloat16
F32 = jnp.float32
RING = ("h", "x", "y")
GROUP = QUERY_HEAD_COUNT // KEY_VALUE_HEADS
SPAN = 512
HALF = 256


def dot(left, right, left_dim, right_dim):
    return lax.dot_general(
        left, right, (((left_dim,), (right_dim,)), ((), ())), preferred_element_type=F32
    )


def rms_scale(values):
    return lax.rsqrt(jnp.mean(values * values, axis=-1, keepdims=True) + EPSILON)


def norm_back(values, scale, gain_row, upstream):
    gained = upstream * gain_row
    grad_gain = jnp.sum(upstream * values * scale, axis=0, keepdims=True)
    middle = jnp.mean(values * gained, axis=-1, keepdims=True)
    return (scale * gained - values * scale * scale * scale * middle, grad_gain)


def swap(value, axis):
    return lax.ppermute(value, axis, [(0, 1), (1, 0)])


def both(mine, other):
    return mine.astype(F32) + other.astype(F32)


def gather_hy(shard):
    wide = jnp.broadcast_to(shard[None], (8, *shard.shape))
    return lax.all_to_all(wide, ("h", "y"), 0, 0, tiled=True)


def gather_x(shards):
    wide = jnp.broadcast_to(shards[None], (4, *shards.shape))
    return lax.all_to_all(wide, "x", 0, 0, tiled=True)


def core_gather(mine):
    rows, cols = mine.shape[2:]
    mine = mine.reshape(4, 2, 4 * rows, cols)
    other = swap(mine, "c")
    mine, other = mine.transpose(1, 0, 2, 3), other.transpose(1, 0, 2, 3)
    first = lax.axis_index("c") == 0
    pair = jnp.stack([jnp.where(first, mine, other), jnp.where(first, other, mine)], axis=2)
    return pair.reshape(64 * rows, cols)


def after(value, *earlier):
    return lax.optimization_barrier((value,) + earlier)[0]


def axis_parts(parts, axis, size):
    me = lax.axis_index(axis)
    mine = [lax.dynamic_index_in_dim(parts, me, 0, keepdims=False)]
    for r in range(1, size):
        block = lax.dynamic_index_in_dim(parts, (me + r) % size, 0, keepdims=False)
        mine.append(lax.ppermute(block, axis, [(i, (i + r) % size) for i in range(size)]))
    return mine


def added(parts):
    total = parts[0].astype(F32)
    for part in parts[1:]:
        total = total + part.astype(F32)
    return total


def exchange_slots(rows):
    width = rows.shape[1]
    return lax.all_to_all(
        rows.reshape(EXPERTS, -1, width), ("h", "x", "c"), 0, 0, tiled=True
    ).reshape(-1, width)


def nn(a,b):
    return lax.dot_general(a,b,(((1,),(0,)),((),())),preferred_element_type=F32)

def fold(v, op):
    return op(v.reshape(v.shape[0]//8,8,v.shape[1]),axis=0)

def write_bias(bias, seg_q, seg_k, y, half):
    width = bias.shape[2]
    for r in range(4):

        def one(r=r):
            same = seg_k[r * SPAN : (r + 1) * SPAN, :] == seg_q[...]
            if r == 0:
                key_place = lax.broadcasted_iota(jnp.int32, (SPAN, width), 0)
                query_place = lax.broadcasted_iota(jnp.int32, (SPAN, width), 1) + half * HALF
                same = same & (key_place <= query_place)
            bias[r] = jnp.where(same, 0.0, MASKED)

        pl.when(y >= r)(one)


def fwd_kernel(
    half, y_ref, q_ref, kv0, kv1, kv2, kv3, seg_q, seg_k, o_ref, lse_ref, bias, kn, vt, sc
):
    y = y_ref[0]

    @pl.when(pl.program_id(0) == 0)
    def _():
        write_bias(bias, seg_q, seg_k, y, half)

    for r, kv in enumerate((kv0, kv1, kv2, kv3)):

        def fill(r=r, kv=kv):
            kn[r] = kv[0].T
            vt[r] = kv[1]

        pl.when(y >= r)(fill)
    scale = jnp.asarray(HEAD_WIDTH**-0.5, BF)
    qs = [q_ref[h * HEAD_WIDTH : (h + 1) * HEAD_WIDTH] * scale for h in range(GROUP)]

    def scores(r, rows, tops):
        out = []
        for h in range(GROUP):
            s = nn(kn[r, rows, :], qs[h]) + bias[r, rows, :]
            sc[h, r, rows, :] = s
            out.append(jnp.maximum(tops[h], fold(s, jnp.max)))
        return tuple(out)

    own = slice(0, (half + 1) * HALF)
    low = tuple(jnp.full((8, HALF), MASKED, F32) for _ in range(GROUP))
    tops = scores(0, own, low)
    tops = lax.fori_loop(1, y + 1, lambda r, t: scores(r, slice(0, SPAN), t), tops)
    tops = [jnp.max(t, axis=0, keepdims=True) for t in tops]

    def mix(r, rows, carry):
        totals, acc = carry
        out, weights = [], []
        for h in range(GROUP):
            p = jnp.exp(sc[h, r, rows, :] - tops[h])
            out.append(totals[h] + fold(p, jnp.sum))
            weights.append(p.astype(BF))
        return tuple(out), acc + nn(vt[r, :, rows], jnp.concatenate(weights, 1))

    zero = (
        tuple(jnp.zeros((8, HALF), F32) for _ in range(GROUP)),
        jnp.zeros((HEAD_WIDTH, GROUP * HALF), F32),
    )
    carry = mix(0, own, zero)
    totals, acc = lax.fori_loop(1, y + 1, lambda r, c: mix(r, slice(0, SPAN), c), carry)
    for h in range(GROUP):
        total = jnp.sum(totals[h], axis=0, keepdims=True)
        mixed = acc[:, h * HALF : (h + 1) * HALF] / total
        o_ref[h * HEAD_WIDTH : (h + 1) * HEAD_WIDTH, :] = mixed.astype(BF)
        lse_ref[0, h : h + 1, :] = tops[h] + jnp.log(total)


def attend(half, y, q_t, kvs, seg_q, seg_k):
    rows = GROUP * HEAD_WIDTH
    heads = q_t.shape[0] // rows
    kv_spec = pl.BlockSpec((2, HEAD_WIDTH, SPAN), lambda g: (0, g, 0))
    return pl.pallas_call(
        functools.partial(fwd_kernel, half),
        grid=(heads,),
        in_specs=[
            pl.BlockSpec(memory_space=pltpu.SMEM),
            pl.BlockSpec((rows, HALF), lambda g: (g, half)),
            kv_spec,
            kv_spec,
            kv_spec,
            kv_spec,
            pl.BlockSpec((1, HALF), lambda g: (0, half)),
            pl.BlockSpec((4 * SPAN, 1), lambda g: (0, 0)),
        ],
        out_specs=[
            pl.BlockSpec((rows, HALF), lambda g: (g, 0)),
            pl.BlockSpec((1, 8, HALF), lambda g: (g, 0, 0)),
        ],
        out_shape=[
            jax.ShapeDtypeStruct((q_t.shape[0], HALF), BF),
            jax.ShapeDtypeStruct((heads, 8, HALF), F32),
        ],
        scratch_shapes=[
            pltpu.VMEM((4, SPAN, HALF), F32),
            pltpu.VMEM((4, SPAN, HEAD_WIDTH), BF),
            pltpu.VMEM((4, HEAD_WIDTH, SPAN), BF),
            pltpu.VMEM((GROUP, 4, SPAN, HALF), F32),
        ],
        compiler_params=pltpu.CompilerParams(vmem_limit_bytes=40 << 20),
        cost_estimate=pl.CostEstimate(
            flops=14_000_000_000, bytes_accessed=6_000_000, transcendentals=6_000_000
        ),
    )(y, q_t, *kvs, seg_q, seg_k)


def bwd_kernel(y_ref, q_ref, d_ref, o_0, o_1, lse_0, lse_1, kv0, kv1, kv2, kv3, seg_q, seg_k, dq_ref, g0, g1, g2, g3, bias, kn, vn, kt, dvk):
    y = y_ref[0]
    @pl.when(pl.program_id(0)==0)
    def _(): write_bias(bias, seg_q, seg_k, y, 0)
    for r,kv in enumerate((kv0,kv1,kv2,kv3)):
        def fill(r=r,kv=kv):
            kn[r] = kv[0].T
            vn[r] = kv[1].T
            kt[r] = kv[0]
        pl.when(y>=r)(fill)
    dvk[...] = jnp.zeros_like(dvk)
    scale = jnp.asarray(HEAD_WIDTH**-0.5, BF)
    for b in range(2):
        cols = slice(b*HALF,(b+1)*HALF)
        qs, qn, ds, dn, dots, lses = [],[],[],[],[],[]
        for h in range(GROUP):
            hr = slice(h*HEAD_WIDTH,(h+1)*HEAD_WIDTH)
            q = q_ref[hr, cols]*scale
            qs.append(q); qn.append(q.T)
            d = d_ref[hr, cols]
            ds.append(d); dn.append(d.T)
            dots.append(jnp.sum(d.astype(F32)*(o_0, o_1)[b][hr].astype(F32),axis=0,keepdims=True))
            lses.append((lse_0, lse_1)[b][0, h : h + 1])
        right = []
        for h in range(GROUP):
            none = jnp.zeros_like(dn[h])
            right += [jnp.concatenate([dn[h], none], 1), jnp.concatenate([none, qn[h]], 1)]
        right = jnp.concatenate(right, 0)

        def step(r, rows, carry):
            left = []
            for h in range(GROUP):
                s = nn(kn[r, rows, :], qs[h]) + bias[r, rows, cols]
                p = jnp.exp(s - lses[h])
                dp = nn(vn[r, rows, :], ds[h])
                dsc = (p * (dp - dots[h])).astype(BF)
                left += [p.astype(BF), dsc]
            dvk[r, rows, :] += nn(jnp.concatenate(left, 1), right)
            return carry + nn(kt[r, :, rows], jnp.concatenate(left[1::2], 1))

        carry = step(0, slice(0, (b + 1) * HALF), jnp.zeros((HEAD_WIDTH, GROUP * HALF), F32))
        carry = lax.fori_loop(1, y+1, lambda r,c: step(r, slice(0,SPAN), c), carry)
        for h in range(GROUP):
            dq_ref[h*HEAD_WIDTH:(h+1)*HEAD_WIDTH, cols] = (
                carry[:, h * HALF : (h + 1) * HALF] * HEAD_WIDTH**-0.5
            ).astype(BF)
    for r,g in enumerate((g0,g1,g2,g3)):
        turned = dvk[r].T.astype(BF)
        g[0] = turned[HEAD_WIDTH:]
        g[1] = turned[:HEAD_WIDTH]

def attend_back(first, count, y, q_t, d_t, outs, lses, kvs, seg_q, seg_k):
    rows = GROUP * HEAD_WIDTH
    kv_spec = pl.BlockSpec((2, HEAD_WIDTH, SPAN), lambda g: (0, first + g, 0))
    q_spec = pl.BlockSpec((rows, SPAN), lambda g: (first + g, 0))
    o_spec = pl.BlockSpec((rows, HALF), lambda g: (first + g, 0))
    lse_spec = pl.BlockSpec((1, 8, HALF), lambda g: (first + g, 0, 0))
    kv_shape = jax.ShapeDtypeStruct((2, count * HEAD_WIDTH, SPAN), BF)
    return pl.pallas_call(
        bwd_kernel,
        grid=(count,),
        in_specs=[pl.BlockSpec(memory_space=pltpu.SMEM), q_spec, q_spec]
        + [o_spec, o_spec, lse_spec, lse_spec]
        + [kv_spec] * 4
        + [pl.BlockSpec((1, SPAN), lambda g: (0, 0)), pl.BlockSpec((4 * SPAN, 1), lambda g: (0, 0))],
        out_specs=[pl.BlockSpec((rows, SPAN), lambda g: (g, 0))]
        + [pl.BlockSpec((2, HEAD_WIDTH, SPAN), lambda g: (0, g, 0))] * 4,
        out_shape=[jax.ShapeDtypeStruct((count * rows, SPAN), BF)] + [kv_shape] * 4,
        scratch_shapes=[pltpu.VMEM((4, SPAN, SPAN), F32)]
        + [pltpu.VMEM((4, SPAN, HEAD_WIDTH), BF)] * 2
        + [pltpu.VMEM((4, HEAD_WIDTH, SPAN), BF)]
        + [pltpu.VMEM((4, SPAN, 2 * HEAD_WIDTH), F32)],
        compiler_params=pltpu.CompilerParams(vmem_limit_bytes=60 << 20),
        cost_estimate=pl.CostEstimate(
            flops=150_000_000_000, bytes_accessed=6_000_000, transcendentals=6_000_000
        ),
    )(y, q_t, d_t, *outs, *lses, *kvs, seg_q, seg_k)


def flat(ref):
    return ref[...].reshape(ref.shape[0] * ref.shape[3], ref.shape[4])


def experts_kernel(x_ref, gate_ref, up_ref, down_ref, g_ref, u_ref, inner_ref, out_ref, acc):
    step = pl.program_id(0)
    down_t = flat(down_ref).T

    @pl.when(step == 0)
    def _():
        acc[...] = jnp.zeros_like(acc)

    x = x_ref[...]
    g_ref[...] = nn(x, flat(gate_ref))
    u_ref[...] = nn(x, flat(up_ref))
    for m in range(x_ref.shape[0] // HALF):
        rows = slice(m * HALF, (m + 1) * HALF)
        gate = g_ref[rows]
        inner_ref[rows] = (gate * jax.nn.sigmoid(gate) * u_ref[rows]).astype(BF)
    for n in range(acc.shape[1] // SPAN):
        cols = slice(n * SPAN, (n + 1) * SPAN)
        acc[:, cols] += nn(inner_ref[...], down_t[:, cols])

    @pl.when(step == pl.num_programs(0) - 1)
    def _():
        out_ref[...] = acc[...].astype(BF)


def experts_back_kernel(
    d_ref, g_ref, u_ref, gate_ref, up_ref, down_ref, dg_ref, du_ref, out_ref, acc, inner
):
    step = pl.program_id(0)
    gate_t = flat(gate_ref).T
    up_t = flat(up_ref).T

    @pl.when(step == 0)
    def _():
        acc[...] = jnp.zeros_like(acc)

    inner[...] = nn(d_ref[...], flat(down_ref))
    for m in range(d_ref.shape[0] // HALF):
        rows = slice(m * HALF, (m + 1) * HALF)
        d_inner = inner[rows]
        gate = g_ref[rows]
        sig = jax.nn.sigmoid(gate)
        dg_ref[rows] = (d_inner * u_ref[rows] * sig * (1.0 + gate * (1.0 - sig))).astype(BF)
        du_ref[rows] = (d_inner * gate * sig).astype(BF)
    for n in range(acc.shape[1] // SPAN):
        cols = slice(n * SPAN, (n + 1) * SPAN)
        acc[:, cols] += nn(dg_ref[...], gate_t[:, cols]) + nn(du_ref[...], up_t[:, cols])

    @pl.when(step == pl.num_programs(0) - 1)
    def _():
        out_ref[...] = acc[...].astype(BF)


def expert_grads_kernel(x_ref, d_ref, dg_ref, du_ref, inner_ref, out_ref, x_t, d_t):
    @pl.when(pl.program_id(0) == 0)
    def _():
        x_t[...] = x_ref[...].T
        d_t[...] = d_ref[...].T

    depth = out_ref.shape[3]
    for i, (left, right) in enumerate(((x_t, dg_ref), (x_t, du_ref), (d_t, inner_ref))):
        for y in range(4):
            out_ref[y, 0, i] = nn(left[y * depth : (y + 1) * depth], right[...]).astype(BF)


def expert_specs(rows, width, hidden):
    whole = pl.BlockSpec((rows, width), lambda b: (0, 0))
    weights = [
        pl.BlockSpec(
            (4, 1, 1, width // 4, HALF),
            functools.partial(lambda i, b: (0, b // 2, i, 0, b % 2), i),
        )
        for i in range(3)
    ]
    column = pl.BlockSpec((rows, HALF), lambda b: (0, b))
    return dict(
        grid=(hidden // HALF,),
        scratch_shapes=[pltpu.VMEM((rows, width), F32)],
        compiler_params=pltpu.CompilerParams(vmem_limit_bytes=40 << 20),
        cost_estimate=pl.CostEstimate(
            flops=6 * rows * width * hidden, bytes_accessed=20_000_000, transcendentals=rows * hidden
        ),
    ), whole, weights, column


def run_experts(x, experts_full):
    rows, width = x.shape
    hidden = 2 * experts_full.shape[4]
    common, whole, weights, column = expert_specs(rows, width, hidden)
    wide = jax.ShapeDtypeStruct((rows, hidden), F32)
    return pl.pallas_call(
        experts_kernel,
        in_specs=[whole] + weights,
        out_specs=[column, column, column, whole],
        out_shape=[
            wide,
            wide,
            jax.ShapeDtypeStruct((rows, hidden), BF),
            jax.ShapeDtypeStruct((rows, width), BF),
        ],
        **common,
    )(x, experts_full, experts_full, experts_full)


def run_experts_back(d, gate, up, experts_full):
    rows, width = d.shape
    hidden = 2 * experts_full.shape[4]
    common, whole, weights, column = expert_specs(rows, width, hidden)
    low = jax.ShapeDtypeStruct((rows, hidden), BF)
    common["scratch_shapes"] = common["scratch_shapes"] + [pltpu.VMEM((rows, HALF), F32)]
    return pl.pallas_call(
        experts_back_kernel,
        in_specs=[whole, column, column] + weights,
        out_specs=[column, column, whole],
        out_shape=[low, low, jax.ShapeDtypeStruct((rows, width), BF)],
        **common,
    )(d, gate, up, experts_full, experts_full, experts_full)


def expert_grads(x, d, d_gate, d_up, inner):
    rows, width = x.shape
    hidden = inner.shape[1]
    common, whole, _, column = expert_specs(rows, width, hidden)
    common["scratch_shapes"] = [pltpu.VMEM((width, rows), BF)] * 2
    return pl.pallas_call(
        expert_grads_kernel,
        in_specs=[whole, whole, column, column, column],
        out_specs=pl.BlockSpec((4, 1, 3, width // 4, HALF), lambda b: (0, b // 2, 0, 0, b % 2)),
        out_shape=jax.ShapeDtypeStruct((4, 2, 3, width // 4, hidden // 2), BF),
        **common,
    )(x, d, d_gate, d_up, inner)


def grads_kernel(plan, first_axis, core_ref, *refs):
    ins, (own_ref, other_ref, pack) = refs[:-3], refs[-3:]
    at = 0
    turned = {}
    for terms in plan:
        total = None
        for left, right, first in terms:
            if left is None:
                high = ins[right][...].astype(BF).astype(F32)
                rest = ins[right][...] - high
                total = jnp.zeros((384, 128), F32) if total is None else total
                pack[:, at : at + 128] = total
                pack[:, at + 16 : at + 24] = high.T
                pack[:, at + 24 : at + 32] = rest.T
                total = None
                at = at + 128
                continue
            if left not in turned:
                turned[left] = ins[left][...].T
            width = ins[right].shape[1]
            rows = turned[left][:, first : first + width]
            piece = dot(rows, ins[right][...], 1, 1)
            total = piece if total is None else total + piece
        if total is not None:
            pack[:, at : at + total.shape[1]] = total
            at = at + total.shape[1]
    for core in range(2):

        @pl.when(core_ref[0] == core)
        def _(core=core):
            for j in range(2):
                for y in range(4):
                    for ref, c in ((own_ref, core), (other_ref, 1 - core)):
                        row = (2 * j + c) * 96 + y * 24
                        value = pack[row : row + 24, :].astype(BF)
                        if first_axis == "x":
                            ref[j, y, 0] = value
                        else:
                            ref[y, j, 0] = value


def pack_grads(plan, first_axis, arrays, wide, cols, flops):
    specs = []
    for i, value in enumerate(arrays):
        if i in wide:
            specs.append(pl.BlockSpec((value.shape[0], 384), lambda b: (0, b)))
        else:
            specs.append(pl.BlockSpec(value.shape, lambda b: (0, 0)))
    out = jax.ShapeDtypeStruct((4, 4, 2, 24, cols), BF)
    if first_axis == "x":
        out_spec = pl.BlockSpec((2, 4, 1, 24, cols), lambda b: (b % 2, 0, b // 2, 0, 0))
    else:
        out_spec = pl.BlockSpec((4, 2, 1, 24, cols), lambda b: (0, b % 2, b // 2, 0, 0))
    return pl.pallas_call(
        functools.partial(grads_kernel, plan, first_axis),
        grid=(arrays[wide[0]].shape[1] // 384,),
        in_specs=[pl.BlockSpec(memory_space=pltpu.SMEM)] + specs,
        out_specs=[out_spec, out_spec],
        out_shape=[out, out],
        scratch_shapes=[pltpu.VMEM((384, cols), F32)],
        compiler_params=pltpu.CompilerParams(
            vmem_limit_bytes=(60 if len(arrays) > 4 else 40) << 20
        ),
        cost_estimate=pl.CostEstimate(
            flops=flops, bytes_accessed=flops // 2000, transcendentals=0
        ),
    )(jnp.full((1,), lax.axis_index("c"), jnp.int32), *arrays)


def turned_sum_kernel(left_ref, right_ref, out_ref):
    out_ref[...] = both(left_ref[...], right_ref[...]).T


def turned_sum(left, right):
    rows, cols = left.shape
    return pl.pallas_call(
        turned_sum_kernel,
        out_shape=jax.ShapeDtypeStruct((cols, rows), F32),
        compiler_params=pltpu.CompilerParams(vmem_limit_bytes=16 << 20),
        cost_estimate=pl.CostEstimate(
            flops=2 * rows * cols, bytes_accessed=8 * rows * cols, transcendentals=0
        ),
    )(left, right)


def pair_blocks(own, theirs, axis):
    received = swap(theirs, "c")
    me = lax.axis_index(axis)
    blocks = []
    for r in range(4):
        mine, other = (
            lax.dynamic_index_in_dim(part, (me + r) % 4, 0, keepdims=False)
            for part in (own, received)
        )
        blocks.append(both(mine, other).astype(BF))
    return blocks


def send_blocks(blocks, axis):
    return blocks[:1] + [
        lax.ppermute(blocks[r], axis, [(i, (i + r) % 4) for i in range(4)]) for r in range(1, 4)
    ]


def local(
    tokens,
    teacher,
    segments,
    routes,
    route_weight,
    norm_attn,
    w_query,
    key_weight,
    value_weight,
    w_out,
    norm_ffn,
    w_router,
    w_gate,
    w_up,
    w_down,
):
    tok_rows, feat_width = tokens.shape
    q_width = w_query.shape[1]
    k_width = key_weight.shape[1]
    tix = lax.axis_index("t")
    yix = lax.axis_index("y")

    small = jnp.concatenate(
        [
            w_router,
            norm_attn[:, None],
            norm_ffn[:, None],
            jnp.zeros((w_router.shape[0], 128 - EXPERTS - 2), BF),
        ],
        axis=1,
    )
    experts = jnp.stack([w_gate[0], w_up[0], w_down[0].T])
    by_hy, experts = lax.optimization_barrier(
        (
            gather_hy(
                jnp.concatenate([key_weight, value_weight, small, w_query, w_out.T], axis=1)
            ),
            experts,
        )
    )
    kv_cols = 2 * k_width + 128
    wide_rest = by_hy[:, :, kv_cols:]
    wide_rest = jnp.broadcast_to(wide_rest[None], (4, *wide_rest.shape))
    ring_kv, wide_rest = lax.optimization_barrier((gather_x(by_hy[:, :, :kv_cols]), wide_rest))
    experts_other = swap(experts, "t")
    ring_rest = lax.all_to_all(wide_rest, "x", 0, 0, tiled=True)
    pack = core_gather(ring_kv)
    full_kv = pack[:, : 2 * k_width]
    full_small = pack[:, 2 * k_width :]
    small_rows = dot(jnp.eye(24, 128, dtype=BF), full_small, 1, 1)
    router_rows = small_rows[:EXPERTS].astype(BF)
    gain_one = small_rows[EXPERTS : EXPERTS + 1]
    gain_two = small_rows[EXPERTS + 1 : EXPERTS + 2]

    resid_in = tokens.astype(F32)
    scale_one = rms_scale(resid_in)
    act_one = (resid_in * scale_one * gain_one).astype(BF)
    kv_mine = dot(full_kv, act_one, 0, 1).astype(BF).reshape(2, k_width, tok_rows)
    kvs = [kv_mine] + [
        lax.ppermute(kv_mine, "y", [(i, i + r) for i in range(4 - r)]) for r in (1, 2, 3)
    ]
    experts_other, ring_rest = lax.optimization_barrier((experts_other, ring_rest))
    experts_full = jnp.stack([experts, experts_other])
    *kvs[1:], ring_rest, experts_full = lax.optimization_barrier(
        (*kvs[1:], ring_rest, experts_full)
    )
    rest = core_gather(ring_rest)
    full_query = rest[:, :q_width]
    full_out = rest[:, q_width:]
    query_t = dot(full_query, act_one, 0, 1).astype(BF)

    experts_full = lax.all_gather(experts_full, "y", axis=0)

    seg_blocks = segments[0].reshape(4, tok_rows)
    seg_mine = lax.dynamic_index_in_dim(seg_blocks, yix, 0, keepdims=False)
    seg_keys = jnp.concatenate(
        [lax.dynamic_index_in_dim(seg_blocks, (yix + 4 - r) % 4, 0, keepdims=False) for r in range(4)]
    )[:, None]
    place_y = jnp.full((1,), yix, jnp.int32)
    mixed_0, log_0 = attend(0, place_y, query_t, kvs, seg_mine[None], seg_keys)
    part_0 = dot(mixed_0, full_out, 0, 1).astype(BF)
    mixed_1, log_1 = attend(1, place_y, after(query_t, part_0), kvs, seg_mine[None], seg_keys)
    other_0 = swap(part_0, "t")
    part_1 = dot(after(mixed_1, other_0), full_out, 0, 1).astype(BF)
    other_1 = swap(part_1, "t")
    hidden = resid_in + jnp.concatenate([both(part_0, other_0), both(part_1, other_1)])
    scale_two = rms_scale(hidden)
    act_two = (hidden * scale_two * gain_two).astype(BF)

    logits = dot(router_rows, act_two, 1, 1)
    router = jax.nn.softmax(logits, axis=0)
    route_cols = routes.T
    weight_cols = route_weight.T
    expert_iota = lax.broadcasted_iota(jnp.int32, (EXPERTS, tok_rows), 0)
    named = [expert_iota == route_cols[k : k + 1] for k in range(TOP)]
    taken = (named[0] | named[1]).astype(BF)
    earlier = (
        lax.broadcasted_iota(jnp.int32, (tok_rows, tok_rows), 0)
        < lax.broadcasted_iota(jnp.int32, (tok_rows, tok_rows), 1)
    ).astype(BF)
    count_before = dot(taken, earlier, 1, 0)
    half = CAPACITY // 2
    slot_iota = lax.broadcasted_iota(jnp.int32, (EXPERTS * half, tok_rows), 0)
    picks = []
    gates = []
    for k in range(TOP):
        place = jnp.sum(jnp.where(named[k], count_before, 0.0), axis=0, keepdims=True)
        place = place.astype(jnp.int32) - tix * half
        slot = jnp.where((place >= 0) & (place < half), route_cols[k : k + 1] * half + place, -1)
        picks.append(slot_iota == slot)
        chosen = jnp.sum(jnp.where(named[k], router, 0.0), axis=0, keepdims=True)
        gates.append(chosen * weight_cols[k : k + 1])
    pick = (picks[0] | picks[1]).astype(BF)
    gated_pick = (
        jnp.where(picks[0], gates[0], 0.0) + jnp.where(picks[1], gates[1], 0.0)
    ).astype(BF)

    received, pick_t, gated_pick_t = lax.optimization_barrier(
        (exchange_slots(dot(pick, act_two, 1, 0).astype(BF)), pick.T, gated_pick.T)
    )
    gate_proj, up_proj, inner, slots_out = run_experts(received, experts_full)
    returned = exchange_slots(slots_out)
    part = dot(gated_pick_t, returned, 1, 0).astype(BF)
    output = hidden + both(part, swap(part, "t"))
    valid = (seg_mine != 0).astype(F32)
    difference = output - teacher.astype(F32)
    grad_output = difference * valid[:, None]
    sse = jnp.sum(grad_output * difference)
    count = jnp.sum(valid)
    grad_low = grad_output.astype(BF)
    d_received = exchange_slots(dot(gated_pick, grad_low, 1, 0).astype(BF))

    slot_dots = dot(returned, grad_low, 1, 1)
    d_gates = jnp.concatenate(
        [jnp.sum(jnp.where(picks[k], slot_dots, 0.0), axis=0, keepdims=True) for k in range(TOP)]
    )
    d_gates_other = swap(d_gates, "t")
    d_received = after(d_received, d_gates_other)
    d_gates = d_gates + d_gates_other

    d_gate_proj, d_up_proj, d_slots = run_experts_back(
        d_received, gate_proj, up_proj, experts_full
    )
    d_returned = exchange_slots(d_slots)
    received, d_received = after(received, d_slots), after(d_received, d_slots)

    grad_parts = expert_grads(received, d_received, d_gate_proj, d_up_proj, inner)
    grad_experts = lax.psum_scatter(grad_parts, "y", scatter_dimension=0)
    d_returned = after(d_returned, grad_parts)
    keep, give = grad_experts[0], grad_experts[1]

    d_router = jnp.where(named[0], d_gates[0:1] * weight_cols[0:1], 0.0) + jnp.where(
        named[1], d_gates[1:2] * weight_cols[1:2], 0.0
    )
    d_logits = (
        router * (d_router - jnp.sum(router * d_router, axis=0, keepdims=True))
    ).astype(BF)
    d_route = dot(d_logits, router_rows, 0, 0)
    part = dot(pick_t, d_returned, 1, 0).astype(BF)
    d_act_two = d_route + both(part, after(swap(part, "t"), d_route))
    d_norm_two, grad_gain_two = norm_back(hidden, scale_two, gain_two, d_act_two)
    d_hidden = grad_output + d_norm_two
    d_attn = d_hidden.astype(BF)
    d_mixed_t = dot(full_out, d_attn, 0, 1).astype(BF)

    saved = ((mixed_0, mixed_1), (log_0, log_1), kvs, seg_mine[None], seg_keys)
    half_groups = k_width // HEAD_WIDTH // 2
    back_0 = attend_back(0, half_groups, place_y, query_t, d_mixed_t, *saved)

    def ring_back(parts):
        return [
            lax.ppermute(parts[r], "y", [(i, i - r) for i in range(r, 4)]) for r in (1, 2, 3)
        ]

    *back_0, d_mixed_t, give = lax.optimization_barrier((*back_0, d_mixed_t, give))
    back_1 = attend_back(half_groups, half_groups, place_y, query_t, d_mixed_t, *saved)
    others_0 = ring_back(back_0[1:])
    given_0 = swap(give[:2], "t")
    *back_1, o1, o2, o3, given_0, give, d_attn_late, gain_late, d_logits_late, back_0[0] = (
        lax.optimization_barrier(
            (*back_1, *others_0, given_0, give[2], d_attn, grad_gain_two, d_logits, back_0[0])
        )
    )
    others_0 = [o1, o2, o3]

    others_1 = ring_back(back_1[1:])
    given_1 = swap(give, "t")
    lines = jnp.concatenate(
        [
            gain_late,
            jnp.full((1, feat_width), sse),
            jnp.full((1, feat_width), count),
            jnp.zeros((5, feat_width), F32),
        ]
    )
    logits_pad = jnp.concatenate(
        [d_logits_late, jnp.zeros((128 - EXPERTS, tok_rows), BF)]
    )
    own_one, theirs_one = pack_grads(
        (
            ((0, 4, 0), (0, 5, HALF)),
            ((2, 6, 0), (None, 3, 0)),
            ((1, 7, 0),),
            ((1, 8, 0),),
        ),
        "x",
        (d_attn_late, act_one, act_two, lines, mixed_0, mixed_1, logits_pad, back_0[0], back_1[0]),
        (0, 1, 2, 3),
        feat_width // 2 + 128 + q_width,
        20_000_000_000,
    )
    o1, o2, o3, given_1, own_one, theirs_one, dq_0, dq_1 = lax.optimization_barrier(
        (*others_1, given_1, own_one, theirs_one, back_0[0], back_1[0])
    )

    d_kv_t = jnp.concatenate(
        [added([back_0[1], *others_0]), added([back_1[1], o1, o2, o3])], axis=1
    ).reshape(2 * k_width, tok_rows).astype(BF)
    d_act_part = dot(jnp.concatenate([dq_0, dq_1]), full_query, 0, 1) + dot(d_kv_t, full_kv, 0, 1)
    part = d_act_part.astype(BF)
    blocks_one = pair_blocks(own_one, theirs_one, "x")
    gain_row = jnp.sum(d_act_part * resid_in * scale_one, axis=0, keepdims=True)
    lines = jnp.concatenate(
        [gain_row, jnp.zeros((7, feat_width), F32)]
    )
    own_two, theirs_two = pack_grads(
        (((0, 2, 0),), ((None, 1, 0),)),
        "y",
        (act_one, lines, d_kv_t),
        (0, 1),
        2 * k_width + 128,
        2_000_000_000,
    )
    part, own_two, theirs_two, *blocks_one = lax.optimization_barrier(
        (part, own_two, theirs_two, *blocks_one)
    )
    other = swap(part, "t")
    parts_one = send_blocks(blocks_one, "x")
    paired_two = both(own_two, swap(theirs_two, "c")).astype(BF)
    ring_two = lax.all_to_all(paired_two, "y", 0, 0, tiled=True)
    grad_wide = keep[:2].astype(F32) + given_0.astype(F32)
    own_down = turned_sum(keep[2], given_1)
    *parts_one, ring_two, own_down, other = lax.optimization_barrier(
        (*parts_one, ring_two, own_down, other)
    )
    by_x = added(parts_one).astype(BF)
    by_y = jnp.sum(ring_two.astype(F32), axis=0).astype(BF)
    by_xy = jnp.concatenate(
        [added(axis_parts(by_x, "y", 4)), added(axis_parts(by_y, "x", 4))], axis=2
    ).astype(BF)
    by_xy, other = lax.optimization_barrier((by_xy, other))
    summed = added(axis_parts(by_xy, "h", 2))
    own_kv = summed[:, by_x.shape[3] :]
    own_query = summed[:, feat_width // 2 + 128 : by_x.shape[3]]
    at = feat_width // 2
    own_out = summed[:, :at].T
    own_router = summed[:, at : at + EXPERTS]
    at = at + EXPERTS
    own_gain_two = summed[:, at] + summed[:, at + 8]
    loss_value = (summed[0, at + 1] + summed[0, at + 9]) / (
        feat_width * (summed[0, at + 2] + summed[0, at + 10])
    )
    own_gain_one = own_kv[:, 2 * k_width + EXPERTS] + own_kv[:, 2 * k_width + EXPERTS + 8]
    d_hidden_one, _ = norm_back(resid_in, scale_one, gain_one, both(part, other))
    grad_tokens = d_hidden + d_hidden_one
    own_gain_one = own_gain_one + swap(own_gain_one, "t")
    return (
        output,
        loss_value,
        grad_tokens,
        own_gain_one,
        own_query,
        own_kv[:, :k_width],
        own_kv[:, k_width : 2 * k_width],
        own_out,
        own_gain_two,
        own_router,
        grad_wide[0][None],
        grad_wide[1][None],
        own_down[None],
    )


def solution(mesh):
    fine = Mesh(mesh.devices.reshape(2, 4, 2, 4, 2), ("h", "x", "c", "y", "t"))
    fsdp = ("h", "x", "c")
    every = ("h", "x", "c", "y")
    return jax.shard_map(
        local,
        mesh=fine,
        in_specs=(
            P(every, None),
            P(every, None),
            P(fsdp, None),
            P(every, None),
            P(every, None),
            P(every),
            P(every, "t"),
            P(every, "t"),
            P(every, "t"),
            P("t", every),
            P(every),
            P(every, None),
            P(fsdp, "y", "t"),
            P(fsdp, "y", "t"),
            P(fsdp, "t", "y"),
        ),
        out_specs=(
            P(every, None),
            P(),
            P(every, None),
            P(every),
            P(every, "t"),
            P(every, "t"),
            P(every, "t"),
            P("t", every),
            P(every),
            P(every, None),
            P(fsdp, "y", "t"),
            P(fsdp, "y", "t"),
            P(fsdp, "t", "y"),
        ),
        check_vma=False,
    )
```

```python
import functools

import jax
import jax.numpy as jnp
from jax import lax
from jax.experimental import pallas as pl
from jax.experimental.pallas import tpu as pltpu
from jax.sharding import Mesh
from jax.sharding import PartitionSpec as P

QUERY_HEAD_COUNT = 24
KEY_VALUE_HEADS = 8
HEAD_WIDTH = 64
TOP = 2
EXPERTS = 16
CAPACITY = 96

EPSILON = 1e-06
MASKED = -1e30

BF = jnp.bfloat16
F32 = jnp.float32
RING = ("h", "x", "y")
GROUP = QUERY_HEAD_COUNT // KEY_VALUE_HEADS
SPAN = 512
HALF = 256


def dot(left, right, left_dim, right_dim):
    return lax.dot_general(
        left, right, (((left_dim,), (right_dim,)), ((), ())), preferred_element_type=F32
    )


def rms_scale(values):
    return lax.rsqrt(jnp.mean(values * values, axis=-1, keepdims=True) + EPSILON)


def norm_back(values, scale, gain_row, upstream):
    gained = upstream * gain_row
    grad_gain = jnp.sum(upstream * values * scale, axis=0, keepdims=True)
    middle = jnp.mean(values * gained, axis=-1, keepdims=True)
    return (scale * gained - values * scale * scale * scale * middle, grad_gain)


def swap(value, axis):
    return lax.ppermute(value, axis, [(0, 1), (1, 0)])


def both(mine, other):
    return mine.astype(F32) + other.astype(F32)


def gather_hy(shard):
    wide = jnp.broadcast_to(shard[None], (8, *shard.shape))
    return lax.all_to_all(wide, ("h", "y"), 0, 0, tiled=True)


def gather_x(shards):
    wide = jnp.broadcast_to(shards[None], (4, *shards.shape))
    return lax.all_to_all(wide, "x", 0, 0, tiled=True)


def core_gather(mine):
    rows, cols = mine.shape[2:]
    mine = mine.reshape(4, 2, 4 * rows, cols)
    other = swap(mine, "c")
    mine, other = mine.transpose(1, 0, 2, 3), other.transpose(1, 0, 2, 3)
    first = lax.axis_index("c") == 0
    pair = jnp.stack([jnp.where(first, mine, other), jnp.where(first, other, mine)], axis=2)
    return pair.reshape(64 * rows, cols)


def after(value, *earlier):
    return lax.optimization_barrier((value,) + earlier)[0]


def axis_parts(parts, axis, size):
    me = lax.axis_index(axis)
    mine = [lax.dynamic_index_in_dim(parts, me, 0, keepdims=False)]
    for r in range(1, size):
        block = lax.dynamic_index_in_dim(parts, (me + r) % size, 0, keepdims=False)
        mine.append(lax.ppermute(block, axis, [(i, (i + r) % size) for i in range(size)]))
    return mine


def added(parts):
    total = parts[0].astype(F32)
    for part in parts[1:]:
        total = total + part.astype(F32)
    return total


def exchange_slots(rows):
    width = rows.shape[1]
    return lax.all_to_all(
        rows.reshape(EXPERTS, -1, width), ("h", "x", "c"), 0, 0, tiled=True
    ).reshape(-1, width)


def nn(a,b):
    return lax.dot_general(a,b,(((1,),(0,)),((),())),preferred_element_type=F32)

def fold(v, op):
    return op(v.reshape(v.shape[0]//8,8,v.shape[1]),axis=0)

def write_bias(bias, seg_q, seg_k, y, half):
    width = bias.shape[2]
    for r in range(4):

        def one(r=r):
            same = seg_k[r * SPAN : (r + 1) * SPAN, :] == seg_q[...]
            if r == 0:
                key_place = lax.broadcasted_iota(jnp.int32, (SPAN, width), 0)
                query_place = lax.broadcasted_iota(jnp.int32, (SPAN, width), 1) + half * HALF
                same = same & (key_place <= query_place)
            bias[r] = jnp.where(same, 0.0, MASKED)

        pl.when(y >= r)(one)


def fwd_kernel(
    half, y_ref, q_ref, kv0, kv1, kv2, kv3, seg_q, seg_k, o_ref, lse_ref, bias, kn, vt, sc
):
    y = y_ref[0]

    @pl.when(pl.program_id(0) == 0)
    def _():
        write_bias(bias, seg_q, seg_k, y, half)

    for r, kv in enumerate((kv0, kv1, kv2, kv3)):

        def fill(r=r, kv=kv):
            kn[r] = kv[0].T
            vt[r] = kv[1]

        pl.when(y >= r)(fill)
    scale = jnp.asarray(HEAD_WIDTH**-0.5, BF)
    qs = [q_ref[h * HEAD_WIDTH : (h + 1) * HEAD_WIDTH] * scale for h in range(GROUP)]

    def scores(r, rows, tops):
        out = []
        for h in range(GROUP):
            s = nn(kn[r, rows, :], qs[h]) + bias[r, rows, :]
            sc[h, r, rows, :] = s
            out.append(jnp.maximum(tops[h], fold(s, jnp.max)))
        return tuple(out)

    own = slice(0, (half + 1) * HALF)
    low = tuple(jnp.full((8, HALF), MASKED, F32) for _ in range(GROUP))
    tops = scores(0, own, low)
    tops = lax.fori_loop(1, y + 1, lambda r, t: scores(r, slice(0, SPAN), t), tops)
    tops = [jnp.max(t, axis=0, keepdims=True) for t in tops]

    def mix(r, rows, carry):
        totals, acc = carry
        out, weights = [], []
        for h in range(GROUP):
            p = jnp.exp(sc[h, r, rows, :] - tops[h])
            out.append(totals[h] + fold(p, jnp.sum))
            weights.append(p.astype(BF))
        return tuple(out), acc + nn(vt[r, :, rows], jnp.concatenate(weights, 1))

    zero = (
        tuple(jnp.zeros((8, HALF), F32) for _ in range(GROUP)),
        jnp.zeros((HEAD_WIDTH, GROUP * HALF), F32),
    )
    carry = mix(0, own, zero)
    totals, acc = lax.fori_loop(1, y + 1, lambda r, c: mix(r, slice(0, SPAN), c), carry)
    for h in range(GROUP):
        total = jnp.sum(totals[h], axis=0, keepdims=True)
        mixed = acc[:, h * HALF : (h + 1) * HALF] / total
        o_ref[h * HEAD_WIDTH : (h + 1) * HEAD_WIDTH, :] = mixed.astype(BF)
        lse_ref[0, h : h + 1, :] = tops[h] + jnp.log(total)


def attend(half, y, q_t, kvs, seg_q, seg_k):
    rows = GROUP * HEAD_WIDTH
    heads = q_t.shape[0] // rows
    kv_spec = pl.BlockSpec((2, HEAD_WIDTH, SPAN), lambda g: (0, g, 0))
    return pl.pallas_call(
        functools.partial(fwd_kernel, half),
        grid=(heads,),
        in_specs=[
            pl.BlockSpec(memory_space=pltpu.SMEM),
            pl.BlockSpec((rows, HALF), lambda g: (g, half)),
            kv_spec,
            kv_spec,
            kv_spec,
            kv_spec,
            pl.BlockSpec((1, HALF), lambda g: (0, half)),
            pl.BlockSpec((4 * SPAN, 1), lambda g: (0, 0)),
        ],
        out_specs=[
            pl.BlockSpec((rows, HALF), lambda g: (g, 0)),
            pl.BlockSpec((1, 8, HALF), lambda g: (g, 0, 0)),
        ],
        out_shape=[
            jax.ShapeDtypeStruct((q_t.shape[0], HALF), BF),
            jax.ShapeDtypeStruct((heads, 8, HALF), F32),
        ],
        scratch_shapes=[
            pltpu.VMEM((4, SPAN, HALF), F32),
            pltpu.VMEM((4, SPAN, HEAD_WIDTH), BF),
            pltpu.VMEM((4, HEAD_WIDTH, SPAN), BF),
            pltpu.VMEM((GROUP, 4, SPAN, HALF), F32),
        ],
        compiler_params=pltpu.CompilerParams(vmem_limit_bytes=40 << 20),
        cost_estimate=pl.CostEstimate(
            flops=14_000_000_000, bytes_accessed=6_000_000, transcendentals=6_000_000
        ),
    )(y, q_t, *kvs, seg_q, seg_k)


def bwd_kernel(y_ref, q_ref, d_ref, o_0, o_1, lse_0, lse_1, kv0, kv1, kv2, kv3, seg_q, seg_k, dq_ref, g0, g1, g2, g3, bias, kn, vn, kt, dvk):
    y = y_ref[0]
    @pl.when(pl.program_id(0)==0)
    def _(): write_bias(bias, seg_q, seg_k, y, 0)
    for r,kv in enumerate((kv0,kv1,kv2,kv3)):
        def fill(r=r,kv=kv):
            kn[r] = kv[0].T
            vn[r] = kv[1].T
            kt[r] = kv[0]
        pl.when(y>=r)(fill)
    dvk[...] = jnp.zeros_like(dvk)
    scale = jnp.asarray(HEAD_WIDTH**-0.5, BF)
    for b in range(2):
        cols = slice(b*HALF,(b+1)*HALF)
        qs, qn, ds, dn, dots, lses = [],[],[],[],[],[]
        for h in range(GROUP):
            hr = slice(h*HEAD_WIDTH,(h+1)*HEAD_WIDTH)
            q = q_ref[hr, cols]*scale
            qs.append(q); qn.append(q.T)
            d = d_ref[hr, cols]
            ds.append(d); dn.append(d.T)
            dots.append(jnp.sum(d.astype(F32)*(o_0, o_1)[b][hr].astype(F32),axis=0,keepdims=True))
            lses.append((lse_0, lse_1)[b][0, h : h + 1])
        right = []
        for h in range(GROUP):
            none = jnp.zeros_like(dn[h])
            right += [jnp.concatenate([dn[h], none], 1), jnp.concatenate([none, qn[h]], 1)]
        right = jnp.concatenate(right, 0)

        def step(r, rows, carry):
            left = []
            for h in range(GROUP):
                s = nn(kn[r, rows, :], qs[h]) + bias[r, rows, cols]
                p = jnp.exp(s - lses[h])
                dp = nn(vn[r, rows, :], ds[h])
                dsc = (p * (dp - dots[h])).astype(BF)
                left += [p.astype(BF), dsc]
            dvk[r, rows, :] += nn(jnp.concatenate(left, 1), right)
            return carry + nn(kt[r, :, rows], jnp.concatenate(left[1::2], 1))

        carry = step(0, slice(0, (b + 1) * HALF), jnp.zeros((HEAD_WIDTH, GROUP * HALF), F32))
        carry = lax.fori_loop(1, y+1, lambda r,c: step(r, slice(0,SPAN), c), carry)
        for h in range(GROUP):
            dq_ref[h*HEAD_WIDTH:(h+1)*HEAD_WIDTH, cols] = (
                carry[:, h * HALF : (h + 1) * HALF] * HEAD_WIDTH**-0.5
            ).astype(BF)
    for r,g in enumerate((g0,g1,g2,g3)):
        turned = dvk[r].T.astype(BF)
        g[0] = turned[HEAD_WIDTH:]
        g[1] = turned[:HEAD_WIDTH]

def attend_back(first, count, y, q_t, d_t, outs, lses, kvs, seg_q, seg_k):
    rows = GROUP * HEAD_WIDTH
    kv_spec = pl.BlockSpec((2, HEAD_WIDTH, SPAN), lambda g: (0, first + g, 0))
    q_spec = pl.BlockSpec((rows, SPAN), lambda g: (first + g, 0))
    o_spec = pl.BlockSpec((rows, HALF), lambda g: (first + g, 0))
    lse_spec = pl.BlockSpec((1, 8, HALF), lambda g: (first + g, 0, 0))
    kv_shape = jax.ShapeDtypeStruct((2, count * HEAD_WIDTH, SPAN), BF)
    return pl.pallas_call(
        bwd_kernel,
        grid=(count,),
        in_specs=[pl.BlockSpec(memory_space=pltpu.SMEM), q_spec, q_spec]
        + [o_spec, o_spec, lse_spec, lse_spec]
        + [kv_spec] * 4
        + [pl.BlockSpec((1, SPAN), lambda g: (0, 0)), pl.BlockSpec((4 * SPAN, 1), lambda g: (0, 0))],
        out_specs=[pl.BlockSpec((rows, SPAN), lambda g: (g, 0))]
        + [pl.BlockSpec((2, HEAD_WIDTH, SPAN), lambda g: (0, g, 0))] * 4,
        out_shape=[jax.ShapeDtypeStruct((count * rows, SPAN), BF)] + [kv_shape] * 4,
        scratch_shapes=[pltpu.VMEM((4, SPAN, SPAN), F32)]
        + [pltpu.VMEM((4, SPAN, HEAD_WIDTH), BF)] * 2
        + [pltpu.VMEM((4, HEAD_WIDTH, SPAN), BF)]
        + [pltpu.VMEM((4, SPAN, 2 * HEAD_WIDTH), F32)],
        compiler_params=pltpu.CompilerParams(vmem_limit_bytes=60 << 20),
        cost_estimate=pl.CostEstimate(
            flops=150_000_000_000, bytes_accessed=6_000_000, transcendentals=6_000_000
        ),
    )(y, q_t, d_t, *outs, *lses, *kvs, seg_q, seg_k)


def flat(ref):
    return ref[...].reshape(ref.shape[0] * ref.shape[3], ref.shape[4])


def experts_kernel(x_ref, gate_ref, up_ref, down_ref, g_ref, u_ref, inner_ref, out_ref, acc):
    step = pl.program_id(0)
    down_t = flat(down_ref).T

    @pl.when(step == 0)
    def _():
        acc[...] = jnp.zeros_like(acc)

    x = x_ref[...]
    g_ref[...] = nn(x, flat(gate_ref))
    u_ref[...] = nn(x, flat(up_ref))
    for m in range(x_ref.shape[0] // HALF):
        rows = slice(m * HALF, (m + 1) * HALF)
        gate = g_ref[rows]
        inner_ref[rows] = (gate * jax.nn.sigmoid(gate) * u_ref[rows]).astype(BF)
    for n in range(acc.shape[1] // SPAN):
        cols = slice(n * SPAN, (n + 1) * SPAN)
        acc[:, cols] += nn(inner_ref[...], down_t[:, cols])

    @pl.when(step == pl.num_programs(0) - 1)
    def _():
        out_ref[...] = acc[...].astype(BF)


def experts_back_kernel(
    d_ref, g_ref, u_ref, gate_ref, up_ref, down_ref, dg_ref, du_ref, out_ref, acc, inner
):
    step = pl.program_id(0)
    gate_t = flat(gate_ref).T
    up_t = flat(up_ref).T

    @pl.when(step == 0)
    def _():
        acc[...] = jnp.zeros_like(acc)

    inner[...] = nn(d_ref[...], flat(down_ref))
    for m in range(d_ref.shape[0] // HALF):
        rows = slice(m * HALF, (m + 1) * HALF)
        d_inner = inner[rows]
        gate = g_ref[rows]
        sig = jax.nn.sigmoid(gate)
        dg_ref[rows] = (d_inner * u_ref[rows] * sig * (1.0 + gate * (1.0 - sig))).astype(BF)
        du_ref[rows] = (d_inner * gate * sig).astype(BF)
    for n in range(acc.shape[1] // SPAN):
        cols = slice(n * SPAN, (n + 1) * SPAN)
        acc[:, cols] += nn(dg_ref[...], gate_t[:, cols]) + nn(du_ref[...], up_t[:, cols])

    @pl.when(step == pl.num_programs(0) - 1)
    def _():
        out_ref[...] = acc[...].astype(BF)


def expert_grads_kernel(x_ref, d_ref, dg_ref, du_ref, inner_ref, out_ref, x_t, d_t):
    @pl.when(pl.program_id(0) == 0)
    def _():
        x_t[...] = x_ref[...].T
        d_t[...] = d_ref[...].T

    depth = out_ref.shape[3]
    for i, (left, right) in enumerate(((x_t, dg_ref), (x_t, du_ref), (d_t, inner_ref))):
        for y in range(4):
            out_ref[y, 0, i] = nn(left[y * depth : (y + 1) * depth], right[...]).astype(BF)


def expert_specs(rows, width, hidden):
    whole = pl.BlockSpec((rows, width), lambda b: (0, 0))
    weights = [
        pl.BlockSpec(
            (4, 1, 1, width // 4, HALF),
            functools.partial(lambda i, b: (0, b // 2, i, 0, b % 2), i),
        )
        for i in range(3)
    ]
    column = pl.BlockSpec((rows, HALF), lambda b: (0, b))
    return dict(
        grid=(hidden // HALF,),
        scratch_shapes=[pltpu.VMEM((rows, width), F32)],
        compiler_params=pltpu.CompilerParams(vmem_limit_bytes=60 << 20),
        cost_estimate=pl.CostEstimate(
            flops=6 * rows * width * hidden, bytes_accessed=20_000_000, transcendentals=rows * hidden
        ),
    ), whole, weights, column


def run_experts(x, experts_full):
    rows, width = x.shape
    hidden = 2 * experts_full.shape[4]
    common, whole, weights, column = expert_specs(rows, width, hidden)
    common["compiler_params"] = pltpu.CompilerParams(vmem_limit_bytes=40 << 20)
    wide = jax.ShapeDtypeStruct((rows, hidden), F32)
    return pl.pallas_call(
        experts_kernel,
        in_specs=[whole] + weights,
        out_specs=[column, column, column, whole],
        out_shape=[
            wide,
            wide,
            jax.ShapeDtypeStruct((rows, hidden), BF),
            jax.ShapeDtypeStruct((rows, width), BF),
        ],
        **common,
    )(x, experts_full, experts_full, experts_full)


def run_experts_back(d, gate, up, experts_full):
    rows, width = d.shape
    hidden = 2 * experts_full.shape[4]
    common, whole, weights, column = expert_specs(rows, width, hidden)
    low = jax.ShapeDtypeStruct((rows, hidden), BF)
    common["scratch_shapes"] = common["scratch_shapes"] + [pltpu.VMEM((rows, HALF), F32)]
    return pl.pallas_call(
        experts_back_kernel,
        in_specs=[whole, column, column] + weights,
        out_specs=[column, column, whole],
        out_shape=[low, low, jax.ShapeDtypeStruct((rows, width), BF)],
        **common,
    )(d, gate, up, experts_full, experts_full, experts_full)


def expert_grads(x, d, d_gate, d_up, inner):
    rows, width = x.shape
    hidden = inner.shape[1]
    common, whole, _, column = expert_specs(rows, width, hidden)
    common["scratch_shapes"] = [pltpu.VMEM((width, rows), BF)] * 2
    return pl.pallas_call(
        expert_grads_kernel,
        in_specs=[whole, whole, column, column, column],
        out_specs=pl.BlockSpec((4, 1, 3, width // 4, HALF), lambda b: (0, b // 2, 0, 0, b % 2)),
        out_shape=jax.ShapeDtypeStruct((4, 2, 3, width // 4, hidden // 2), BF),
        **common,
    )(x, d, d_gate, d_up, inner)


def grads_kernel(plan, first_axis, core_ref, *refs):
    ins, (own_ref, other_ref, pack) = refs[:-3], refs[-3:]
    at = 0
    turned = {}
    for terms in plan:
        total = None
        for left, right, first in terms:
            if left is None:
                high = ins[right][...].astype(BF).astype(F32)
                rest = ins[right][...] - high
                total = jnp.zeros((384, 128), F32) if total is None else total
                pack[:, at : at + 128] = total
                pack[:, at + 16 : at + 24] = high.T
                pack[:, at + 24 : at + 32] = rest.T
                total = None
                at = at + 128
                continue
            if left not in turned:
                turned[left] = ins[left][...].T
            width = ins[right].shape[1]
            rows = turned[left][:, first : first + width]
            piece = dot(rows, ins[right][...], 1, 1)
            total = piece if total is None else total + piece
        if total is not None:
            pack[:, at : at + total.shape[1]] = total
            at = at + total.shape[1]
    for core in range(2):

        @pl.when(core_ref[0] == core)
        def _(core=core):
            for j in range(2):
                for y in range(4):
                    for ref, c in ((own_ref, core), (other_ref, 1 - core)):
                        row = (2 * j + c) * 96 + y * 24
                        value = pack[row : row + 24, :].astype(BF)
                        if first_axis == "x":
                            ref[j, y, 0] = value
                        else:
                            ref[y, j, 0] = value


def pack_grads(plan, first_axis, arrays, wide, cols, flops):
    specs = []
    for i, value in enumerate(arrays):
        if i in wide:
            specs.append(pl.BlockSpec((value.shape[0], 384), lambda b: (0, b)))
        else:
            specs.append(pl.BlockSpec(value.shape, lambda b: (0, 0)))
    out = jax.ShapeDtypeStruct((4, 4, 2, 24, cols), BF)
    if first_axis == "x":
        out_spec = pl.BlockSpec((2, 4, 1, 24, cols), lambda b: (b % 2, 0, b // 2, 0, 0))
    else:
        out_spec = pl.BlockSpec((4, 2, 1, 24, cols), lambda b: (0, b % 2, b // 2, 0, 0))
    return pl.pallas_call(
        functools.partial(grads_kernel, plan, first_axis),
        grid=(arrays[wide[0]].shape[1] // 384,),
        in_specs=[pl.BlockSpec(memory_space=pltpu.SMEM)] + specs,
        out_specs=[out_spec, out_spec],
        out_shape=[out, out],
        scratch_shapes=[pltpu.VMEM((384, cols), F32)],
        compiler_params=pltpu.CompilerParams(
            vmem_limit_bytes=(60 if len(arrays) > 4 else 40) << 20
        ),
        cost_estimate=pl.CostEstimate(
            flops=flops, bytes_accessed=flops // 2000, transcendentals=0
        ),
    )(jnp.full((1,), lax.axis_index("c"), jnp.int32), *arrays)


def turned_sum_kernel(left_ref, right_ref, out_ref):
    out_ref[...] = both(left_ref[...], right_ref[...]).T


def turned_sum(left, right):
    rows, cols = left.shape
    return pl.pallas_call(
        turned_sum_kernel,
        out_shape=jax.ShapeDtypeStruct((cols, rows), F32),
        compiler_params=pltpu.CompilerParams(vmem_limit_bytes=16 << 20),
        cost_estimate=pl.CostEstimate(
            flops=2 * rows * cols, bytes_accessed=8 * rows * cols, transcendentals=0
        ),
    )(left, right)


def pair_blocks(own, theirs, axis):
    received = swap(theirs, "c")
    me = lax.axis_index(axis)
    blocks = []
    for r in range(4):
        mine, other = (
            lax.dynamic_index_in_dim(part, (me + r) % 4, 0, keepdims=False)
            for part in (own, received)
        )
        blocks.append(both(mine, other).astype(BF))
    return blocks


def send_blocks(blocks, axis):
    return blocks[:1] + [
        lax.ppermute(blocks[r], axis, [(i, (i + r) % 4) for i in range(4)]) for r in range(1, 4)
    ]


def local(
    tokens,
    teacher,
    segments,
    routes,
    route_weight,
    norm_attn,
    w_query,
    key_weight,
    value_weight,
    w_out,
    norm_ffn,
    w_router,
    w_gate,
    w_up,
    w_down,
):
    tok_rows, feat_width = tokens.shape
    q_width = w_query.shape[1]
    k_width = key_weight.shape[1]
    tix = lax.axis_index("t")
    yix = lax.axis_index("y")

    small = jnp.concatenate(
        [
            w_router,
            norm_attn[:, None],
            norm_ffn[:, None],
            jnp.zeros((w_router.shape[0], 128 - EXPERTS - 2), BF),
        ],
        axis=1,
    )
    experts = jnp.stack([w_gate[0], w_up[0], w_down[0].T])
    by_hy, experts = lax.optimization_barrier(
        (
            gather_hy(
                jnp.concatenate([key_weight, value_weight, small, w_query, w_out.T], axis=1)
            ),
            experts,
        )
    )
    kv_cols = 2 * k_width + 128
    wide_rest = by_hy[:, :, kv_cols:]
    wide_rest = jnp.broadcast_to(wide_rest[None], (4, *wide_rest.shape))
    ring_kv, wide_rest = lax.optimization_barrier((gather_x(by_hy[:, :, :kv_cols]), wide_rest))
    experts_other = swap(experts, "t")
    ring_rest = lax.all_to_all(wide_rest, "x", 0, 0, tiled=True)
    pack = core_gather(ring_kv)
    full_kv = pack[:, : 2 * k_width]
    full_small = pack[:, 2 * k_width :]
    small_rows = dot(jnp.eye(24, 128, dtype=BF), full_small, 1, 1)
    router_rows = small_rows[:EXPERTS].astype(BF)
    gain_one = small_rows[EXPERTS : EXPERTS + 1]
    gain_two = small_rows[EXPERTS + 1 : EXPERTS + 2]

    resid_in = tokens.astype(F32)
    scale_one = rms_scale(resid_in)
    act_one = (resid_in * scale_one * gain_one).astype(BF)
    kv_mine = dot(full_kv, act_one, 0, 1).astype(BF).reshape(2, k_width, tok_rows)
    kvs = [kv_mine] + [
        lax.ppermute(kv_mine, "y", [(i, i + r) for i in range(4 - r)]) for r in (1, 2, 3)
    ]
    experts_other, ring_rest = lax.optimization_barrier((experts_other, ring_rest))
    experts_full = jnp.stack([experts, experts_other])
    *kvs[1:], ring_rest, experts_full = lax.optimization_barrier(
        (*kvs[1:], ring_rest, experts_full)
    )
    rest = core_gather(ring_rest)
    full_query = rest[:, :q_width]
    full_out = rest[:, q_width:]
    query_t = dot(full_query, act_one, 0, 1).astype(BF)

    experts_full = lax.all_gather(experts_full, "y", axis=0)

    seg_blocks = segments[0].reshape(4, tok_rows)
    seg_mine = lax.dynamic_index_in_dim(seg_blocks, yix, 0, keepdims=False)
    seg_keys = jnp.concatenate(
        [lax.dynamic_index_in_dim(seg_blocks, (yix + 4 - r) % 4, 0, keepdims=False) for r in range(4)]
    )[:, None]
    place_y = jnp.full((1,), yix, jnp.int32)
    mixed_0, log_0 = attend(0, place_y, query_t, kvs, seg_mine[None], seg_keys)
    part_0 = dot(mixed_0, full_out, 0, 1).astype(BF)
    mixed_1, log_1 = attend(1, place_y, after(query_t, part_0), kvs, seg_mine[None], seg_keys)
    other_0 = swap(part_0, "t")
    part_1 = dot(after(mixed_1, other_0), full_out, 0, 1).astype(BF)
    other_1 = swap(part_1, "t")
    hidden = resid_in + jnp.concatenate([both(part_0, other_0), both(part_1, other_1)])
    scale_two = rms_scale(hidden)
    act_two = (hidden * scale_two * gain_two).astype(BF)

    logits = dot(router_rows, act_two, 1, 1)
    router = jax.nn.softmax(logits, axis=0)
    route_cols = routes.T
    weight_cols = route_weight.T
    expert_iota = lax.broadcasted_iota(jnp.int32, (EXPERTS, tok_rows), 0)
    named = [expert_iota == route_cols[k : k + 1] for k in range(TOP)]
    taken = (named[0] | named[1]).astype(BF)
    earlier = (
        lax.broadcasted_iota(jnp.int32, (tok_rows, tok_rows), 0)
        < lax.broadcasted_iota(jnp.int32, (tok_rows, tok_rows), 1)
    ).astype(BF)
    count_before = dot(taken, earlier, 1, 0)
    half = CAPACITY // 2
    slot_iota = lax.broadcasted_iota(jnp.int32, (EXPERTS * half, tok_rows), 0)
    picks = []
    gates = []
    for k in range(TOP):
        place = jnp.sum(jnp.where(named[k], count_before, 0.0), axis=0, keepdims=True)
        place = place.astype(jnp.int32) - tix * half
        slot = jnp.where((place >= 0) & (place < half), route_cols[k : k + 1] * half + place, -1)
        picks.append(slot_iota == slot)
        chosen = jnp.sum(jnp.where(named[k], router, 0.0), axis=0, keepdims=True)
        gates.append(chosen * weight_cols[k : k + 1])
    pick = (picks[0] | picks[1]).astype(BF)
    gated_pick = (
        jnp.where(picks[0], gates[0], 0.0) + jnp.where(picks[1], gates[1], 0.0)
    ).astype(BF)

    received, pick_t, gated_pick_t = lax.optimization_barrier(
        (exchange_slots(dot(pick, act_two, 1, 0).astype(BF)), pick.T, gated_pick.T)
    )
    gate_proj, up_proj, inner, slots_out = run_experts(received, experts_full)
    returned = exchange_slots(slots_out)
    part = dot(gated_pick_t, returned, 1, 0).astype(BF)
    output = hidden + both(part, swap(part, "t"))
    valid = (seg_mine != 0).astype(F32)
    difference = output - teacher.astype(F32)
    grad_output = difference * valid[:, None]
    sse = jnp.sum(grad_output * difference)
    count = jnp.sum(valid)
    grad_low = grad_output.astype(BF)
    d_received = exchange_slots(dot(gated_pick, grad_low, 1, 0).astype(BF))

    slot_dots = dot(returned, grad_low, 1, 1)
    d_gates = jnp.concatenate(
        [jnp.sum(jnp.where(picks[k], slot_dots, 0.0), axis=0, keepdims=True) for k in range(TOP)]
    )
    d_gates_other = swap(d_gates, "t")
    d_received = after(d_received, d_gates_other)
    d_gates = d_gates + d_gates_other

    d_gate_proj, d_up_proj, d_slots = run_experts_back(
        d_received, gate_proj, up_proj, experts_full
    )
    d_returned = exchange_slots(d_slots)
    received, d_received = after(received, d_slots), after(d_received, d_slots)

    grad_parts = expert_grads(received, d_received, d_gate_proj, d_up_proj, inner)
    grad_experts = lax.psum_scatter(grad_parts, "y", scatter_dimension=0)
    d_returned = after(d_returned, grad_parts)
    keep, give = grad_experts[0], grad_experts[1]

    d_router = jnp.where(named[0], d_gates[0:1] * weight_cols[0:1], 0.0) + jnp.where(
        named[1], d_gates[1:2] * weight_cols[1:2], 0.0
    )
    d_logits = (
        router * (d_router - jnp.sum(router * d_router, axis=0, keepdims=True))
    ).astype(BF)
    d_route = dot(d_logits, router_rows, 0, 0)
    part = dot(pick_t, d_returned, 1, 0).astype(BF)
    d_act_two = d_route + both(part, after(swap(part, "t"), d_route))
    d_norm_two, grad_gain_two = norm_back(hidden, scale_two, gain_two, d_act_two)
    d_hidden = grad_output + d_norm_two
    d_attn = d_hidden.astype(BF)
    d_mixed_t = dot(full_out, d_attn, 0, 1).astype(BF)

    saved = ((mixed_0, mixed_1), (log_0, log_1), kvs, seg_mine[None], seg_keys)
    half_groups = k_width // HEAD_WIDTH // 2
    back_0 = attend_back(0, half_groups, place_y, query_t, d_mixed_t, *saved)

    def ring_back(parts):
        return [
            lax.ppermute(parts[r], "y", [(i, i - r) for i in range(r, 4)]) for r in (1, 2, 3)
        ]

    *back_0, d_mixed_t, give = lax.optimization_barrier((*back_0, d_mixed_t, give))
    back_1 = attend_back(half_groups, half_groups, place_y, query_t, d_mixed_t, *saved)
    others_0 = ring_back(back_0[1:])
    given_0 = swap(give[:2], "t")
    *back_1, o1, o2, o3, given_0, give, d_attn_late, gain_late, d_logits_late, back_0[0] = (
        lax.optimization_barrier(
            (*back_1, *others_0, given_0, give[2], d_attn, grad_gain_two, d_logits, back_0[0])
        )
    )
    others_0 = [o1, o2, o3]

    others_1 = ring_back(back_1[1:])
    given_1 = swap(give, "t")
    lines = jnp.concatenate(
        [
            gain_late,
            jnp.full((1, feat_width), sse),
            jnp.full((1, feat_width), count),
            jnp.zeros((5, feat_width), F32),
        ]
    )
    logits_pad = jnp.concatenate(
        [d_logits_late, jnp.zeros((128 - EXPERTS, tok_rows), BF)]
    )
    own_one, theirs_one = pack_grads(
        (
            ((0, 4, 0), (0, 5, HALF)),
            ((2, 6, 0), (None, 3, 0)),
            ((1, 7, 0),),
            ((1, 8, 0),),
        ),
        "x",
        (d_attn_late, act_one, act_two, lines, mixed_0, mixed_1, logits_pad, back_0[0], back_1[0]),
        (0, 1, 2, 3),
        feat_width // 2 + 128 + q_width,
        20_000_000_000,
    )
    o1, o2, o3, given_1, own_one, theirs_one, dq_0, dq_1 = lax.optimization_barrier(
        (*others_1, given_1, own_one, theirs_one, back_0[0], back_1[0])
    )

    d_kv_t = jnp.concatenate(
        [added([back_0[1], *others_0]), added([back_1[1], o1, o2, o3])], axis=1
    ).reshape(2 * k_width, tok_rows).astype(BF)
    d_act_part = dot(jnp.concatenate([dq_0, dq_1]), full_query, 0, 1) + dot(d_kv_t, full_kv, 0, 1)
    part = d_act_part.astype(BF)
    blocks_one = pair_blocks(own_one, theirs_one, "x")
    gain_row = jnp.sum(d_act_part * resid_in * scale_one, axis=0, keepdims=True)
    lines = jnp.concatenate(
        [gain_row, jnp.zeros((7, feat_width), F32)]
    )
    own_two, theirs_two = pack_grads(
        (((0, 2, 0),), ((None, 1, 0),)),
        "y",
        (act_one, lines, d_kv_t),
        (0, 1),
        2 * k_width + 128,
        2_000_000_000,
    )
    part, own_two, theirs_two, *blocks_one = lax.optimization_barrier(
        (part, own_two, theirs_two, *blocks_one)
    )
    other = swap(part, "t")
    parts_one = send_blocks(blocks_one, "x")
    paired_two = both(own_two, swap(theirs_two, "c")).astype(BF)
    ring_two = lax.all_to_all(paired_two, "y", 0, 0, tiled=True)
    grad_wide = keep[:2].astype(F32) + given_0.astype(F32)
    own_down = turned_sum(keep[2], given_1)
    *parts_one, ring_two, own_down, other = lax.optimization_barrier(
        (*parts_one, ring_two, own_down, other)
    )
    by_x = added(parts_one).astype(BF)
    by_y = jnp.sum(ring_two.astype(F32), axis=0).astype(BF)
    by_xy = jnp.concatenate(
        [added(axis_parts(by_x, "y", 4)), added(axis_parts(by_y, "x", 4))], axis=2
    ).astype(BF)
    by_xy, other = lax.optimization_barrier((by_xy, other))
    summed = added(axis_parts(by_xy, "h", 2))
    own_kv = summed[:, by_x.shape[3] :]
    own_query = summed[:, feat_width // 2 + 128 : by_x.shape[3]]
    at = feat_width // 2
    own_out = summed[:, :at].T
    own_router = summed[:, at : at + EXPERTS]
    at = at + EXPERTS
    own_gain_two = summed[:, at] + summed[:, at + 8]
    loss_value = (summed[0, at + 1] + summed[0, at + 9]) / (
        feat_width * (summed[0, at + 2] + summed[0, at + 10])
    )
    own_gain_one = own_kv[:, 2 * k_width + EXPERTS] + own_kv[:, 2 * k_width + EXPERTS + 8]
    d_hidden_one, _ = norm_back(resid_in, scale_one, gain_one, both(part, other))
    grad_tokens = d_hidden + d_hidden_one
    own_gain_one = own_gain_one + swap(own_gain_one, "t")
    return (
        output,
        loss_value,
        grad_tokens,
        own_gain_one,
        own_query,
        own_kv[:, :k_width],
        own_kv[:, k_width : 2 * k_width],
        own_out,
        own_gain_two,
        own_router,
        grad_wide[0][None],
        grad_wide[1][None],
        own_down[None],
    )


def solution(mesh):
    fine = Mesh(mesh.devices.reshape(2, 4, 2, 4, 2), ("h", "x", "c", "y", "t"))
    fsdp = ("h", "x", "c")
    every = ("h", "x", "c", "y")
    return jax.shard_map(
        local,
        mesh=fine,
        in_specs=(
            P(every, None),
            P(every, None),
            P(fsdp, None),
            P(every, None),
            P(every, None),
            P(every),
            P(every, "t"),
            P(every, "t"),
            P(every, "t"),
            P("t", every),
            P(every),
            P(every, None),
            P(fsdp, "y", "t"),
            P(fsdp, "y", "t"),
            P(fsdp, "t", "y"),
        ),
        out_specs=(
            P(every, None),
            P(),
            P(every, None),
            P(every),
            P(every, "t"),
            P(every, "t"),
            P(every, "t"),
            P("t", every),
            P(every),
            P(every, None),
            P(fsdp, "y", "t"),
            P(fsdp, "y", "t"),
            P(fsdp, "t", "y"),
        ),
        check_vma=False,
    )
```

```python
import functools

import jax
import jax.numpy as jnp
from jax import lax
from jax.experimental import pallas as pl
from jax.experimental.pallas import tpu as pltpu
from jax.sharding import Mesh
from jax.sharding import PartitionSpec as P

QUERY_HEAD_COUNT = 24
KEY_VALUE_HEADS = 8
HEAD_WIDTH = 64
TOP = 2
EXPERTS = 16
CAPACITY = 96

EPSILON = 1e-06
MASKED = -1e30

BF = jnp.bfloat16
F32 = jnp.float32
RING = ("h", "x", "y")
GROUP = QUERY_HEAD_COUNT // KEY_VALUE_HEADS
SPAN = 512
HALF = 256


def dot(left, right, left_dim, right_dim):
    return lax.dot_general(
        left, right, (((left_dim,), (right_dim,)), ((), ())), preferred_element_type=F32
    )


def rms_scale(values):
    return lax.rsqrt(jnp.mean(values * values, axis=-1, keepdims=True) + EPSILON)


def norm_back(values, scale, gain_row, upstream):
    gained = upstream * gain_row
    grad_gain = jnp.sum(upstream * values * scale, axis=0, keepdims=True)
    middle = jnp.mean(values * gained, axis=-1, keepdims=True)
    return (scale * gained - values * scale * scale * scale * middle, grad_gain)


def swap(value, axis):
    return lax.ppermute(value, axis, [(0, 1), (1, 0)])


def both(mine, other):
    return mine.astype(F32) + other.astype(F32)


def gather_hy(shard):
    wide = jnp.broadcast_to(shard[None], (8, *shard.shape))
    return lax.all_to_all(wide, ("h", "y"), 0, 0, tiled=True)


def gather_x(shards):
    wide = jnp.broadcast_to(shards[None], (4, *shards.shape))
    return lax.all_to_all(wide, "x", 0, 0, tiled=True)


def core_gather(mine):
    rows, cols = mine.shape[2:]
    mine = mine.reshape(4, 2, 4 * rows, cols)
    other = swap(mine, "c")
    mine, other = mine.transpose(1, 0, 2, 3), other.transpose(1, 0, 2, 3)
    first = lax.axis_index("c") == 0
    pair = jnp.stack([jnp.where(first, mine, other), jnp.where(first, other, mine)], axis=2)
    return pair.reshape(64 * rows, cols)


def after(value, *earlier):
    return lax.optimization_barrier((value,) + earlier)[0]


def axis_parts(parts, axis, size):
    me = lax.axis_index(axis)
    mine = [lax.dynamic_index_in_dim(parts, me, 0, keepdims=False)]
    for r in range(1, size):
        block = lax.dynamic_index_in_dim(parts, (me + r) % size, 0, keepdims=False)
        mine.append(lax.ppermute(block, axis, [(i, (i + r) % size) for i in range(size)]))
    return mine


def added(parts):
    total = parts[0].astype(F32)
    for part in parts[1:]:
        total = total + part.astype(F32)
    return total


def exchange_slots(rows):
    width = rows.shape[1]
    return lax.all_to_all(
        rows.reshape(EXPERTS, -1, width), ("h", "x", "c"), 0, 0, tiled=True
    ).reshape(-1, width)


def nn(a,b):
    return lax.dot_general(a,b,(((1,),(0,)),((),())),preferred_element_type=F32)

def fold(v, op):
    return op(v.reshape(v.shape[0]//8,8,v.shape[1]),axis=0)

def write_bias(bias, seg_q, seg_k, y, half):
    width = bias.shape[2]
    for r in range(4):

        def one(r=r):
            same = seg_k[r * SPAN : (r + 1) * SPAN, :] == seg_q[...]
            if r == 0:
                key_place = lax.broadcasted_iota(jnp.int32, (SPAN, width), 0)
                query_place = lax.broadcasted_iota(jnp.int32, (SPAN, width), 1) + half * HALF
                same = same & (key_place <= query_place)
            bias[r] = jnp.where(same, 0.0, MASKED)

        pl.when(y >= r)(one)


def fwd_kernel(
    half, y_ref, q_ref, kv0, kv1, kv2, kv3, seg_q, seg_k, o_ref, lse_ref, bias, kn, vt, sc
):
    y = y_ref[0]

    @pl.when(pl.program_id(0) == 0)
    def _():
        write_bias(bias, seg_q, seg_k, y, half)

    for r, kv in enumerate((kv0, kv1, kv2, kv3)):

        def fill(r=r, kv=kv):
            kn[r] = kv[0].T
            vt[r] = kv[1]

        pl.when(y >= r)(fill)
    scale = jnp.asarray(HEAD_WIDTH**-0.5, BF)
    qs = [q_ref[h * HEAD_WIDTH : (h + 1) * HEAD_WIDTH] * scale for h in range(GROUP)]

    def scores(r, rows, tops):
        out = []
        for h in range(GROUP):
            s = nn(kn[r, rows, :], qs[h]) + bias[r, rows, :]
            sc[h, r, rows, :] = s
            out.append(jnp.maximum(tops[h], fold(s, jnp.max)))
        return tuple(out)

    own = slice(0, (half + 1) * HALF)
    low = tuple(jnp.full((8, HALF), MASKED, F32) for _ in range(GROUP))
    tops = scores(0, own, low)
    tops = lax.fori_loop(1, y + 1, lambda r, t: scores(r, slice(0, SPAN), t), tops)
    tops = [jnp.max(t, axis=0, keepdims=True) for t in tops]

    def mix(r, rows, carry):
        totals, acc = carry
        out, weights = [], []
        for h in range(GROUP):
            p = jnp.exp(sc[h, r, rows, :] - tops[h])
            out.append(totals[h] + fold(p, jnp.sum))
            weights.append(p.astype(BF))
        return tuple(out), acc + nn(vt[r, :, rows], jnp.concatenate(weights, 1))

    zero = (
        tuple(jnp.zeros((8, HALF), F32) for _ in range(GROUP)),
        jnp.zeros((HEAD_WIDTH, GROUP * HALF), F32),
    )
    carry = mix(0, own, zero)
    totals, acc = lax.fori_loop(1, y + 1, lambda r, c: mix(r, slice(0, SPAN), c), carry)
    for h in range(GROUP):
        total = jnp.sum(totals[h], axis=0, keepdims=True)
        mixed = acc[:, h * HALF : (h + 1) * HALF] / total
        o_ref[h * HEAD_WIDTH : (h + 1) * HEAD_WIDTH, :] = mixed.astype(BF)
        lse_ref[0, h : h + 1, :] = tops[h] + jnp.log(total)


def attend(half, y, q_t, kvs, seg_q, seg_k):
    rows = GROUP * HEAD_WIDTH
    heads = q_t.shape[0] // rows
    kv_spec = pl.BlockSpec((2, HEAD_WIDTH, SPAN), lambda g: (0, g, 0))
    return pl.pallas_call(
        functools.partial(fwd_kernel, half),
        grid=(heads,),
        in_specs=[
            pl.BlockSpec(memory_space=pltpu.SMEM),
            pl.BlockSpec((rows, HALF), lambda g: (g, half)),
            kv_spec,
            kv_spec,
            kv_spec,
            kv_spec,
            pl.BlockSpec((1, HALF), lambda g: (0, half)),
            pl.BlockSpec((4 * SPAN, 1), lambda g: (0, 0)),
        ],
        out_specs=[
            pl.BlockSpec((rows, HALF), lambda g: (g, 0)),
            pl.BlockSpec((1, 8, HALF), lambda g: (g, 0, 0)),
        ],
        out_shape=[
            jax.ShapeDtypeStruct((q_t.shape[0], HALF), BF),
            jax.ShapeDtypeStruct((heads, 8, HALF), F32),
        ],
        scratch_shapes=[
            pltpu.VMEM((4, SPAN, HALF), F32),
            pltpu.VMEM((4, SPAN, HEAD_WIDTH), BF),
            pltpu.VMEM((4, HEAD_WIDTH, SPAN), BF),
            pltpu.VMEM((GROUP, 4, SPAN, HALF), F32),
        ],
        compiler_params=pltpu.CompilerParams(vmem_limit_bytes=40 << 20),
        cost_estimate=pl.CostEstimate(
            flops=14_000_000_000, bytes_accessed=6_000_000, transcendentals=6_000_000
        ),
    )(y, q_t, *kvs, seg_q, seg_k)


def bwd_kernel(y_ref, q_ref, d_ref, o_0, o_1, lse_0, lse_1, kv0, kv1, kv2, kv3, seg_q, seg_k, dq_ref, g0, g1, g2, g3, bias, kn, vn, kt, dvk):
    y = y_ref[0]
    @pl.when(pl.program_id(0)==0)
    def _(): write_bias(bias, seg_q, seg_k, y, 0)
    for r,kv in enumerate((kv0,kv1,kv2,kv3)):
        def fill(r=r,kv=kv):
            kn[r] = kv[0].T
            vn[r] = kv[1].T
            kt[r] = kv[0]
        pl.when(y>=r)(fill)
    dvk[...] = jnp.zeros_like(dvk)
    scale = jnp.asarray(HEAD_WIDTH**-0.5, BF)
    for b in range(2):
        cols = slice(b*HALF,(b+1)*HALF)
        qs, qn, ds, dn, dots, lses = [],[],[],[],[],[]
        for h in range(GROUP):
            hr = slice(h*HEAD_WIDTH,(h+1)*HEAD_WIDTH)
            q = q_ref[hr, cols]*scale
            qs.append(q); qn.append(q.T)
            d = d_ref[hr, cols]
            ds.append(d); dn.append(d.T)
            dots.append(jnp.sum(d.astype(F32)*(o_0, o_1)[b][hr].astype(F32),axis=0,keepdims=True))
            lses.append((lse_0, lse_1)[b][0, h : h + 1])
        right = []
        for h in range(GROUP):
            none = jnp.zeros_like(dn[h])
            right += [jnp.concatenate([dn[h], none], 1), jnp.concatenate([none, qn[h]], 1)]
        right = jnp.concatenate(right, 0)

        def step(r, rows, carry):
            left = []
            for h in range(GROUP):
                s = nn(kn[r, rows, :], qs[h]) + bias[r, rows, cols]
                p = jnp.exp(s - lses[h])
                dp = nn(vn[r, rows, :], ds[h])
                dsc = (p * (dp - dots[h])).astype(BF)
                left += [p.astype(BF), dsc]
            dvk[r, rows, :] += nn(jnp.concatenate(left, 1), right)
            return carry + nn(kt[r, :, rows], jnp.concatenate(left[1::2], 1))

        carry = step(0, slice(0, (b + 1) * HALF), jnp.zeros((HEAD_WIDTH, GROUP * HALF), F32))
        carry = lax.fori_loop(1, y+1, lambda r,c: step(r, slice(0,SPAN), c), carry)
        for h in range(GROUP):
            dq_ref[h*HEAD_WIDTH:(h+1)*HEAD_WIDTH, cols] = (
                carry[:, h * HALF : (h + 1) * HALF] * HEAD_WIDTH**-0.5
            ).astype(BF)
    for r,g in enumerate((g0,g1,g2,g3)):
        turned = dvk[r].T.astype(BF)
        g[0] = turned[HEAD_WIDTH:]
        g[1] = turned[:HEAD_WIDTH]

def attend_back(first, count, y, q_t, d_t, outs, lses, kvs, seg_q, seg_k):
    rows = GROUP * HEAD_WIDTH
    kv_spec = pl.BlockSpec((2, HEAD_WIDTH, SPAN), lambda g: (0, first + g, 0))
    q_spec = pl.BlockSpec((rows, SPAN), lambda g: (first + g, 0))
    o_spec = pl.BlockSpec((rows, HALF), lambda g: (first + g, 0))
    lse_spec = pl.BlockSpec((1, 8, HALF), lambda g: (first + g, 0, 0))
    kv_shape = jax.ShapeDtypeStruct((2, count * HEAD_WIDTH, SPAN), BF)
    return pl.pallas_call(
        bwd_kernel,
        grid=(count,),
        in_specs=[pl.BlockSpec(memory_space=pltpu.SMEM), q_spec, q_spec]
        + [o_spec, o_spec, lse_spec, lse_spec]
        + [kv_spec] * 4
        + [pl.BlockSpec((1, SPAN), lambda g: (0, 0)), pl.BlockSpec((4 * SPAN, 1), lambda g: (0, 0))],
        out_specs=[pl.BlockSpec((rows, SPAN), lambda g: (g, 0))]
        + [pl.BlockSpec((2, HEAD_WIDTH, SPAN), lambda g: (0, g, 0))] * 4,
        out_shape=[jax.ShapeDtypeStruct((count * rows, SPAN), BF)] + [kv_shape] * 4,
        scratch_shapes=[pltpu.VMEM((4, SPAN, SPAN), F32)]
        + [pltpu.VMEM((4, SPAN, HEAD_WIDTH), BF)] * 2
        + [pltpu.VMEM((4, HEAD_WIDTH, SPAN), BF)]
        + [pltpu.VMEM((4, SPAN, 2 * HEAD_WIDTH), F32)],
        compiler_params=pltpu.CompilerParams(vmem_limit_bytes=60 << 20),
        cost_estimate=pl.CostEstimate(
            flops=150_000_000_000, bytes_accessed=6_000_000, transcendentals=6_000_000
        ),
    )(y, q_t, d_t, *outs, *lses, *kvs, seg_q, seg_k)


def flat(ref):
    return ref[...].reshape(ref.shape[0] * ref.shape[3], ref.shape[4])


def experts_kernel(x_ref, gate_ref, up_ref, down_ref, g_ref, u_ref, inner_ref, out_ref, acc):
    step = pl.program_id(0)
    down_t = flat(down_ref).T

    @pl.when(step == 0)
    def _():
        acc[...] = jnp.zeros_like(acc)

    x = x_ref[...]
    g_ref[...] = nn(x, flat(gate_ref))
    u_ref[...] = nn(x, flat(up_ref))
    for m in range(x_ref.shape[0] // HALF):
        rows = slice(m * HALF, (m + 1) * HALF)
        gate = g_ref[rows]
        inner_ref[rows] = (gate * jax.nn.sigmoid(gate) * u_ref[rows]).astype(BF)
    for n in range(acc.shape[1] // SPAN):
        cols = slice(n * SPAN, (n + 1) * SPAN)
        acc[:, cols] += nn(inner_ref[...], down_t[:, cols])

    @pl.when(step == pl.num_programs(0) - 1)
    def _():
        out_ref[...] = acc[...].astype(BF)


def experts_back_kernel(
    d_ref, g_ref, u_ref, gate_ref, up_ref, down_ref, dg_ref, du_ref, out_ref, acc, inner
):
    step = pl.program_id(0)
    gate_t = flat(gate_ref).T
    up_t = flat(up_ref).T

    @pl.when(step == 0)
    def _():
        acc[...] = jnp.zeros_like(acc)

    inner[...] = nn(d_ref[...], flat(down_ref))
    for m in range(d_ref.shape[0] // HALF):
        rows = slice(m * HALF, (m + 1) * HALF)
        d_inner = inner[rows]
        gate = g_ref[rows]
        sig = jax.nn.sigmoid(gate)
        dg_ref[rows] = (d_inner * u_ref[rows] * sig * (1.0 + gate * (1.0 - sig))).astype(BF)
        du_ref[rows] = (d_inner * gate * sig).astype(BF)
    for n in range(acc.shape[1] // SPAN):
        cols = slice(n * SPAN, (n + 1) * SPAN)
        acc[:, cols] += nn(dg_ref[...], gate_t[:, cols]) + nn(du_ref[...], up_t[:, cols])

    @pl.when(step == pl.num_programs(0) - 1)
    def _():
        out_ref[...] = acc[...].astype(BF)


def expert_grads_kernel(x_ref, d_ref, dg_ref, du_ref, inner_ref, out_ref, x_t, d_t):
    @pl.when(pl.program_id(0) == 0)
    def _():
        x_t[...] = x_ref[...].T
        d_t[...] = d_ref[...].T

    depth = out_ref.shape[3]
    for i, (left, right) in enumerate(((x_t, dg_ref), (x_t, du_ref), (d_t, inner_ref))):
        for y in range(4):
            out_ref[y, 0, i] = nn(left[y * depth : (y + 1) * depth], right[...]).astype(BF)


def expert_specs(rows, width, hidden):
    whole = pl.BlockSpec((rows, width), lambda b: (0, 0))
    weights = [
        pl.BlockSpec(
            (4, 1, 1, width // 4, HALF),
            functools.partial(lambda i, b: (0, b // 2, i, 0, b % 2), i),
        )
        for i in range(3)
    ]
    column = pl.BlockSpec((rows, HALF), lambda b: (0, b))
    return dict(
        grid=(hidden // HALF,),
        scratch_shapes=[pltpu.VMEM((rows, width), F32)],
        compiler_params=pltpu.CompilerParams(vmem_limit_bytes=60 << 20),
        cost_estimate=pl.CostEstimate(
            flops=6 * rows * width * hidden, bytes_accessed=20_000_000, transcendentals=rows * hidden
        ),
    ), whole, weights, column


def run_experts(x, experts_full):
    rows, width = x.shape
    hidden = 2 * experts_full.shape[4]
    common, whole, weights, column = expert_specs(rows, width, hidden)
    common["compiler_params"] = pltpu.CompilerParams(vmem_limit_bytes=40 << 20)
    wide = jax.ShapeDtypeStruct((rows, hidden), F32)
    return pl.pallas_call(
        experts_kernel,
        in_specs=[whole] + weights,
        out_specs=[column, column, column, whole],
        out_shape=[
            wide,
            wide,
            jax.ShapeDtypeStruct((rows, hidden), BF),
            jax.ShapeDtypeStruct((rows, width), BF),
        ],
        **common,
    )(x, experts_full, experts_full, experts_full)


def run_experts_back(d, gate, up, experts_full):
    rows, width = d.shape
    hidden = 2 * experts_full.shape[4]
    common, whole, weights, column = expert_specs(rows, width, hidden)
    low = jax.ShapeDtypeStruct((rows, hidden), BF)
    common["scratch_shapes"] = common["scratch_shapes"] + [pltpu.VMEM((rows, HALF), F32)]
    return pl.pallas_call(
        experts_back_kernel,
        in_specs=[whole, column, column] + weights,
        out_specs=[column, column, whole],
        out_shape=[low, low, jax.ShapeDtypeStruct((rows, width), BF)],
        **common,
    )(d, gate, up, experts_full, experts_full, experts_full)


def expert_grads(x, d, d_gate, d_up, inner):
    rows, width = x.shape
    hidden = inner.shape[1]
    common, whole, _, column = expert_specs(rows, width, hidden)
    common["scratch_shapes"] = [pltpu.VMEM((width, rows), BF)] * 2
    return pl.pallas_call(
        expert_grads_kernel,
        in_specs=[whole, whole, column, column, column],
        out_specs=pl.BlockSpec((4, 1, 3, width // 4, HALF), lambda b: (0, b // 2, 0, 0, b % 2)),
        out_shape=jax.ShapeDtypeStruct((4, 2, 3, width // 4, hidden // 2), BF),
        **common,
    )(x, d, d_gate, d_up, inner)


def grads_kernel(plan, first_axis, core_ref, *refs):
    ins, (own_ref, other_ref, pack) = refs[:-3], refs[-3:]
    at = 0
    turned = {}
    for terms in plan:
        total = None
        for left, right, first in terms:
            if left is None:
                high = ins[right][...].astype(BF).astype(F32)
                rest = ins[right][...] - high
                total = jnp.zeros((384, 128), F32) if total is None else total
                pack[:, at : at + 128] = total
                pack[:, at + 16 : at + 24] = high.T
                pack[:, at + 24 : at + 32] = rest.T
                total = None
                at = at + 128
                continue
            if left not in turned:
                turned[left] = ins[left][...].T
            width = ins[right].shape[1]
            rows = turned[left][:, first : first + width]
            piece = dot(rows, ins[right][...], 1, 1)
            total = piece if total is None else total + piece
        if total is not None:
            pack[:, at : at + total.shape[1]] = total
            at = at + total.shape[1]
    for core in range(2):

        @pl.when(core_ref[0] == core)
        def _(core=core):
            for j in range(2):
                for y in range(4):
                    for ref, c in ((own_ref, core), (other_ref, 1 - core)):
                        row = (2 * j + c) * 96 + y * 24
                        value = pack[row : row + 24, :].astype(BF)
                        if first_axis == "x":
                            ref[j, y, 0] = value
                        else:
                            ref[y, j, 0] = value


def pack_grads(plan, first_axis, arrays, wide, cols, flops):
    specs = []
    for i, value in enumerate(arrays):
        if i in wide:
            specs.append(pl.BlockSpec((value.shape[0], 384), lambda b: (0, b)))
        else:
            specs.append(pl.BlockSpec(value.shape, lambda b: (0, 0)))
    out = jax.ShapeDtypeStruct((4, 4, 2, 24, cols), BF)
    if first_axis == "x":
        out_spec = pl.BlockSpec((2, 4, 1, 24, cols), lambda b: (b % 2, 0, b // 2, 0, 0))
    else:
        out_spec = pl.BlockSpec((4, 2, 1, 24, cols), lambda b: (0, b % 2, b // 2, 0, 0))
    return pl.pallas_call(
        functools.partial(grads_kernel, plan, first_axis),
        grid=(arrays[wide[0]].shape[1] // 384,),
        in_specs=[pl.BlockSpec(memory_space=pltpu.SMEM)] + specs,
        out_specs=[out_spec, out_spec],
        out_shape=[out, out],
        scratch_shapes=[pltpu.VMEM((384, cols), F32)],
        compiler_params=pltpu.CompilerParams(
            vmem_limit_bytes=(60 if len(arrays) > 4 else 40) << 20
        ),
        cost_estimate=pl.CostEstimate(
            flops=flops, bytes_accessed=flops // 2000, transcendentals=0
        ),
    )(jnp.full((1,), lax.axis_index("c"), jnp.int32), *arrays)


def token_grads_kernel(tokens_ref, gain_ref, mine_ref, other_ref, later_ref, out_ref):
    resid = tokens_ref[...].astype(F32)
    scale = rms_scale(resid)
    gained = both(mine_ref[...], other_ref[...]) * gain_ref[...]
    middle = jnp.mean(resid * gained, axis=-1, keepdims=True)
    out_ref[...] = later_ref[...] + (scale * gained - resid * scale * scale * scale * middle)


def token_grads(tokens, gain_row, mine, other, later):
    rows, width = tokens.shape
    block = pl.BlockSpec((128, width), lambda b: (b, 0))
    return pl.pallas_call(
        token_grads_kernel,
        grid=(rows // 128,),
        in_specs=[block, pl.BlockSpec((1, width), lambda b: (0, 0)), block, block, block],
        out_specs=block,
        out_shape=jax.ShapeDtypeStruct((rows, width), F32),
        compiler_params=pltpu.CompilerParams(vmem_limit_bytes=24 << 20),
        cost_estimate=pl.CostEstimate(
            flops=12 * rows * width, bytes_accessed=14 * rows * width, transcendentals=rows
        ),
    )(tokens, gain_row, mine, other, later)


def turned_sum_kernel(left_ref, right_ref, out_ref):
    out_ref[...] = both(left_ref[...], right_ref[...]).T


def turned_sum(left, right):
    rows, cols = left.shape
    return pl.pallas_call(
        turned_sum_kernel,
        out_shape=jax.ShapeDtypeStruct((cols, rows), F32),
        compiler_params=pltpu.CompilerParams(vmem_limit_bytes=16 << 20),
        cost_estimate=pl.CostEstimate(
            flops=2 * rows * cols, bytes_accessed=8 * rows * cols, transcendentals=0
        ),
    )(left, right)


def pair_blocks(own, theirs, axis):
    received = swap(theirs, "c")
    me = lax.axis_index(axis)
    blocks = []
    for r in range(4):
        mine, other = (
            lax.dynamic_index_in_dim(part, (me + r) % 4, 0, keepdims=False)
            for part in (own, received)
        )
        blocks.append(both(mine, other).astype(BF))
    return blocks


def send_blocks(blocks, axis):
    return blocks[:1] + [
        lax.ppermute(blocks[r], axis, [(i, (i + r) % 4) for i in range(4)]) for r in range(1, 4)
    ]


def local(
    tokens,
    teacher,
    segments,
    routes,
    route_weight,
    norm_attn,
    w_query,
    key_weight,
    value_weight,
    w_out,
    norm_ffn,
    w_router,
    w_gate,
    w_up,
    w_down,
):
    tok_rows, feat_width = tokens.shape
    q_width = w_query.shape[1]
    k_width = key_weight.shape[1]
    tix = lax.axis_index("t")
    yix = lax.axis_index("y")

    small = jnp.concatenate(
        [
            w_router,
            norm_attn[:, None],
            norm_ffn[:, None],
            jnp.zeros((w_router.shape[0], 128 - EXPERTS - 2), BF),
        ],
        axis=1,
    )
    experts = jnp.stack([w_gate[0], w_up[0], w_down[0].T])
    by_hy, experts = lax.optimization_barrier(
        (
            gather_hy(
                jnp.concatenate([key_weight, value_weight, small, w_query, w_out.T], axis=1)
            ),
            experts,
        )
    )
    kv_cols = 2 * k_width + 128
    wide_rest = by_hy[:, :, kv_cols:]
    wide_rest = jnp.broadcast_to(wide_rest[None], (4, *wide_rest.shape))
    ring_kv, wide_rest = lax.optimization_barrier((gather_x(by_hy[:, :, :kv_cols]), wide_rest))
    experts_other = swap(experts, "t")
    ring_rest = lax.all_to_all(wide_rest, "x", 0, 0, tiled=True)
    pack = core_gather(ring_kv)
    full_kv = pack[:, : 2 * k_width]
    full_small = pack[:, 2 * k_width :]
    small_rows = dot(jnp.eye(24, 128, dtype=BF), full_small, 1, 1)
    router_rows = small_rows[:EXPERTS].astype(BF)
    gain_one = small_rows[EXPERTS : EXPERTS + 1]
    gain_two = small_rows[EXPERTS + 1 : EXPERTS + 2]

    resid_in = tokens.astype(F32)
    scale_one = rms_scale(resid_in)
    act_one = (resid_in * scale_one * gain_one).astype(BF)
    kv_mine = dot(full_kv, act_one, 0, 1).astype(BF).reshape(2, k_width, tok_rows)
    kvs = [kv_mine] + [
        lax.ppermute(kv_mine, "y", [(i, i + r) for i in range(4 - r)]) for r in (1, 2, 3)
    ]
    experts_other, ring_rest = lax.optimization_barrier((experts_other, ring_rest))
    experts_full = jnp.stack([experts, experts_other])
    *kvs[1:], ring_rest, experts_full = lax.optimization_barrier(
        (*kvs[1:], ring_rest, experts_full)
    )
    rest = core_gather(ring_rest)
    full_query = rest[:, :q_width]
    full_out = rest[:, q_width:]
    query_t = dot(full_query, act_one, 0, 1).astype(BF)

    experts_full = lax.all_gather(experts_full, "y", axis=0)

    seg_blocks = segments[0].reshape(4, tok_rows)
    seg_mine = lax.dynamic_index_in_dim(seg_blocks, yix, 0, keepdims=False)
    seg_keys = jnp.concatenate(
        [lax.dynamic_index_in_dim(seg_blocks, (yix + 4 - r) % 4, 0, keepdims=False) for r in range(4)]
    )[:, None]
    place_y = jnp.full((1,), yix, jnp.int32)
    mixed_0, log_0 = attend(0, place_y, query_t, kvs, seg_mine[None], seg_keys)
    part_0 = dot(mixed_0, full_out, 0, 1).astype(BF)
    mixed_1, log_1 = attend(1, place_y, after(query_t, part_0), kvs, seg_mine[None], seg_keys)
    other_0 = swap(part_0, "t")
    part_1 = dot(after(mixed_1, other_0), full_out, 0, 1).astype(BF)
    other_1 = swap(part_1, "t")
    hidden = resid_in + jnp.concatenate([both(part_0, other_0), both(part_1, other_1)])
    scale_two = rms_scale(hidden)
    act_two = (hidden * scale_two * gain_two).astype(BF)

    logits = dot(router_rows, act_two, 1, 1)
    router = jax.nn.softmax(logits, axis=0)
    route_cols = routes.T
    weight_cols = route_weight.T
    expert_iota = lax.broadcasted_iota(jnp.int32, (EXPERTS, tok_rows), 0)
    named = [expert_iota == route_cols[k : k + 1] for k in range(TOP)]
    taken = (named[0] | named[1]).astype(BF)
    earlier = (
        lax.broadcasted_iota(jnp.int32, (tok_rows, tok_rows), 0)
        < lax.broadcasted_iota(jnp.int32, (tok_rows, tok_rows), 1)
    ).astype(BF)
    count_before = dot(taken, earlier, 1, 0)
    half = CAPACITY // 2
    slot_iota = lax.broadcasted_iota(jnp.int32, (EXPERTS * half, tok_rows), 0)
    picks = []
    gates = []
    for k in range(TOP):
        place = jnp.sum(jnp.where(named[k], count_before, 0.0), axis=0, keepdims=True)
        place = place.astype(jnp.int32) - tix * half
        slot = jnp.where((place >= 0) & (place < half), route_cols[k : k + 1] * half + place, -1)
        picks.append(slot_iota == slot)
        chosen = jnp.sum(jnp.where(named[k], router, 0.0), axis=0, keepdims=True)
        gates.append(chosen * weight_cols[k : k + 1])
    pick = (picks[0] | picks[1]).astype(BF)
    gated_pick = (
        jnp.where(picks[0], gates[0], 0.0) + jnp.where(picks[1], gates[1], 0.0)
    ).astype(BF)

    received, pick_t, gated_pick_t = lax.optimization_barrier(
        (exchange_slots(dot(pick, act_two, 1, 0).astype(BF)), pick.T, gated_pick.T)
    )
    gate_proj, up_proj, inner, slots_out = run_experts(received, experts_full)
    returned = exchange_slots(slots_out)
    part = dot(gated_pick_t, returned, 1, 0).astype(BF)
    output = hidden + both(part, swap(part, "t"))
    valid = (seg_mine != 0).astype(F32)
    difference = output - teacher.astype(F32)
    grad_output = difference * valid[:, None]
    sse = jnp.sum(grad_output * difference)
    count = jnp.sum(valid)
    grad_low = grad_output.astype(BF)
    d_received = exchange_slots(dot(gated_pick, grad_low, 1, 0).astype(BF))

    slot_dots = dot(returned, grad_low, 1, 1)
    d_gates = jnp.concatenate(
        [jnp.sum(jnp.where(picks[k], slot_dots, 0.0), axis=0, keepdims=True) for k in range(TOP)]
    )
    d_gates_other = swap(d_gates, "t")
    d_received = after(d_received, d_gates_other)
    d_gates = d_gates + d_gates_other

    d_gate_proj, d_up_proj, d_slots = run_experts_back(
        d_received, gate_proj, up_proj, experts_full
    )
    d_returned = exchange_slots(d_slots)
    received, d_received = after(received, d_slots), after(d_received, d_slots)

    grad_parts = expert_grads(received, d_received, d_gate_proj, d_up_proj, inner)
    grad_experts = lax.psum_scatter(grad_parts, "y", scatter_dimension=0)
    d_returned = after(d_returned, grad_parts)
    keep, give = grad_experts[0], grad_experts[1]

    d_router = jnp.where(named[0], d_gates[0:1] * weight_cols[0:1], 0.0) + jnp.where(
        named[1], d_gates[1:2] * weight_cols[1:2], 0.0
    )
    d_logits = (
        router * (d_router - jnp.sum(router * d_router, axis=0, keepdims=True))
    ).astype(BF)
    d_route = dot(d_logits, router_rows, 0, 0)
    part = dot(pick_t, d_returned, 1, 0).astype(BF)
    d_act_two = d_route + both(part, after(swap(part, "t"), d_route))
    d_norm_two, grad_gain_two = norm_back(hidden, scale_two, gain_two, d_act_two)
    d_hidden = grad_output + d_norm_two
    d_attn = d_hidden.astype(BF)
    d_mixed_t = dot(full_out, d_attn, 0, 1).astype(BF)

    saved = ((mixed_0, mixed_1), (log_0, log_1), kvs, seg_mine[None], seg_keys)
    half_groups = k_width // HEAD_WIDTH // 2
    back_0 = attend_back(0, half_groups, place_y, query_t, d_mixed_t, *saved)

    def ring_back(parts):
        return [
            lax.ppermute(parts[r], "y", [(i, i - r) for i in range(r, 4)]) for r in (1, 2, 3)
        ]

    *back_0, d_mixed_t, give = lax.optimization_barrier((*back_0, d_mixed_t, give))
    back_1 = attend_back(half_groups, half_groups, place_y, query_t, d_mixed_t, *saved)
    others_0 = ring_back(back_0[1:])
    given_0 = swap(give[:2], "t")
    *back_1, o1, o2, o3, given_0, give, d_attn_late, gain_late, d_logits_late, back_0[0] = (
        lax.optimization_barrier(
            (*back_1, *others_0, given_0, give[2], d_attn, grad_gain_two, d_logits, back_0[0])
        )
    )
    others_0 = [o1, o2, o3]

    others_1 = ring_back(back_1[1:])
    given_1 = swap(give, "t")
    lines = jnp.concatenate(
        [
            gain_late,
            jnp.full((1, feat_width), sse),
            jnp.full((1, feat_width), count),
            jnp.zeros((5, feat_width), F32),
        ]
    )
    logits_pad = jnp.concatenate(
        [d_logits_late, jnp.zeros((128 - EXPERTS, tok_rows), BF)]
    )
    own_one, theirs_one = pack_grads(
        (
            ((0, 4, 0), (0, 5, HALF)),
            ((2, 6, 0), (None, 3, 0)),
            ((1, 7, 0),),
            ((1, 8, 0),),
        ),
        "x",
        (d_attn_late, act_one, act_two, lines, mixed_0, mixed_1, logits_pad, back_0[0], back_1[0]),
        (0, 1, 2, 3),
        feat_width // 2 + 128 + q_width,
        20_000_000_000,
    )
    o1, o2, o3, given_1, own_one, theirs_one, dq_0, dq_1 = lax.optimization_barrier(
        (*others_1, given_1, own_one, theirs_one, back_0[0], back_1[0])
    )

    d_kv_t = jnp.concatenate(
        [added([back_0[1], *others_0]), added([back_1[1], o1, o2, o3])], axis=1
    ).reshape(2 * k_width, tok_rows).astype(BF)
    d_act_part = dot(jnp.concatenate([dq_0, dq_1]), full_query, 0, 1) + dot(d_kv_t, full_kv, 0, 1)
    part = d_act_part.astype(BF)
    blocks_one = pair_blocks(own_one, theirs_one, "x")
    gain_row = jnp.sum(d_act_part * resid_in * scale_one, axis=0, keepdims=True)
    lines = jnp.concatenate(
        [gain_row, jnp.zeros((7, feat_width), F32)]
    )
    own_two, theirs_two = pack_grads(
        (((0, 2, 0),), ((None, 1, 0),)),
        "y",
        (act_one, lines, d_kv_t),
        (0, 1),
        2 * k_width + 128,
        2_000_000_000,
    )
    part, own_two, theirs_two, *blocks_one = lax.optimization_barrier(
        (part, own_two, theirs_two, *blocks_one)
    )
    other = swap(part, "t")
    parts_one = send_blocks(blocks_one, "x")
    paired_two = both(own_two, swap(theirs_two, "c")).astype(BF)
    ring_two = lax.all_to_all(paired_two, "y", 0, 0, tiled=True)
    grad_wide = keep[:2].astype(F32) + given_0.astype(F32)
    own_down = turned_sum(keep[2], given_1)
    *parts_one, ring_two, own_down, other = lax.optimization_barrier(
        (*parts_one, ring_two, own_down, other)
    )
    by_x = added(parts_one).astype(BF)
    by_y = jnp.sum(ring_two.astype(F32), axis=0).astype(BF)
    by_xy = jnp.concatenate(
        [added(axis_parts(by_x, "y", 4)), added(axis_parts(by_y, "x", 4))], axis=2
    ).astype(BF)
    by_xy, other = lax.optimization_barrier((by_xy, other))
    summed = added(axis_parts(by_xy, "h", 2))
    own_kv = summed[:, by_x.shape[3] :]
    own_query = summed[:, feat_width // 2 + 128 : by_x.shape[3]]
    at = feat_width // 2
    own_out = summed[:, :at].T
    own_router = summed[:, at : at + EXPERTS]
    at = at + EXPERTS
    own_gain_two = summed[:, at] + summed[:, at + 8]
    loss_value = (summed[0, at + 1] + summed[0, at + 9]) / (
        feat_width * (summed[0, at + 2] + summed[0, at + 10])
    )
    own_gain_one = own_kv[:, 2 * k_width + EXPERTS] + own_kv[:, 2 * k_width + EXPERTS + 8]
    grad_tokens = token_grads(tokens, gain_one, part, other, d_hidden)
    own_gain_one = own_gain_one + swap(own_gain_one, "t")
    return (
        output,
        loss_value,
        grad_tokens,
        own_gain_one,
        own_query,
        own_kv[:, :k_width],
        own_kv[:, k_width : 2 * k_width],
        own_out,
        own_gain_two,
        own_router,
        grad_wide[0][None],
        grad_wide[1][None],
        own_down[None],
    )


def solution(mesh):
    fine = Mesh(mesh.devices.reshape(2, 4, 2, 4, 2), ("h", "x", "c", "y", "t"))
    fsdp = ("h", "x", "c")
    every = ("h", "x", "c", "y")
    return jax.shard_map(
        local,
        mesh=fine,
        in_specs=(
            P(every, None),
            P(every, None),
            P(fsdp, None),
            P(every, None),
            P(every, None),
            P(every),
            P(every, "t"),
            P(every, "t"),
            P(every, "t"),
            P("t", every),
            P(every),
            P(every, None),
            P(fsdp, "y", "t"),
            P(fsdp, "y", "t"),
            P(fsdp, "t", "y"),
        ),
        out_specs=(
            P(every, None),
            P(),
            P(every, None),
            P(every),
            P(every, "t"),
            P(every, "t"),
            P(every, "t"),
            P("t", every),
            P(every),
            P(every, None),
            P(fsdp, "y", "t"),
            P(fsdp, "y", "t"),
            P(fsdp, "t", "y"),
        ),
        check_vma=False,
    )
```

```python
import functools

import jax
import jax.numpy as jnp
from jax import lax
from jax.experimental import pallas as pl
from jax.experimental.pallas import tpu as pltpu
from jax.sharding import Mesh
from jax.sharding import PartitionSpec as P

QUERY_HEAD_COUNT = 24
KEY_VALUE_HEADS = 8
HEAD_WIDTH = 64
TOP = 2
EXPERTS = 16
CAPACITY = 96

EPSILON = 1e-06
MASKED = -1e30

BF = jnp.bfloat16
F32 = jnp.float32
RING = ("h", "x", "y")
GROUP = QUERY_HEAD_COUNT // KEY_VALUE_HEADS
SPAN = 512
HALF = 256


def dot(left, right, left_dim, right_dim):
    return lax.dot_general(
        left, right, (((left_dim,), (right_dim,)), ((), ())), preferred_element_type=F32
    )


def rms_scale(values):
    return lax.rsqrt(jnp.mean(values * values, axis=-1, keepdims=True) + EPSILON)


def norm_back(values, scale, gain_row, upstream):
    gained = upstream * gain_row
    grad_gain = jnp.sum(upstream * values * scale, axis=0, keepdims=True)
    middle = jnp.mean(values * gained, axis=-1, keepdims=True)
    return (scale * gained - values * scale * scale * scale * middle, grad_gain)


def swap(value, axis):
    return lax.ppermute(value, axis, [(0, 1), (1, 0)])


def both(mine, other):
    return mine.astype(F32) + other.astype(F32)


def gather_hy(shard):
    wide = jnp.broadcast_to(shard[None], (8, *shard.shape))
    return lax.all_to_all(wide, ("h", "y"), 0, 0, tiled=True)


def gather_x(shards):
    wide = jnp.broadcast_to(shards[None], (4, *shards.shape))
    return lax.all_to_all(wide, "x", 0, 0, tiled=True)


def core_gather(mine):
    rows, cols = mine.shape[2:]
    mine = mine.reshape(4, 2, 4 * rows, cols)
    other = swap(mine, "c")
    mine, other = mine.transpose(1, 0, 2, 3), other.transpose(1, 0, 2, 3)
    first = lax.axis_index("c") == 0
    pair = jnp.stack([jnp.where(first, mine, other), jnp.where(first, other, mine)], axis=2)
    return pair.reshape(64 * rows, cols)


def after(value, *earlier):
    return lax.optimization_barrier((value,) + earlier)[0]


def axis_parts(parts, axis, size):
    me = lax.axis_index(axis)
    mine = [lax.dynamic_index_in_dim(parts, me, 0, keepdims=False)]
    for r in range(1, size):
        block = lax.dynamic_index_in_dim(parts, (me + r) % size, 0, keepdims=False)
        mine.append(lax.ppermute(block, axis, [(i, (i + r) % size) for i in range(size)]))
    return mine


def added(parts):
    total = parts[0].astype(F32)
    for part in parts[1:]:
        total = total + part.astype(F32)
    return total


def exchange_slots(rows):
    width = rows.shape[1]
    return lax.all_to_all(
        rows.reshape(EXPERTS, -1, width), ("h", "x", "c"), 0, 0, tiled=True
    ).reshape(-1, width)


def nn(a,b):
    return lax.dot_general(a,b,(((1,),(0,)),((),())),preferred_element_type=F32)

def fold(v, op):
    return op(v.reshape(v.shape[0]//8,8,v.shape[1]),axis=0)

def write_bias(bias, seg_q, seg_k, y, half):
    width = bias.shape[2]
    for r in range(4):

        def one(r=r):
            same = seg_k[r * SPAN : (r + 1) * SPAN, :] == seg_q[...]
            if r == 0:
                key_place = lax.broadcasted_iota(jnp.int32, (SPAN, width), 0)
                query_place = lax.broadcasted_iota(jnp.int32, (SPAN, width), 1) + half * HALF
                same = same & (key_place <= query_place)
            bias[r] = jnp.where(same, 0.0, MASKED)

        pl.when(y >= r)(one)


def fwd_kernel(
    half, y_ref, q_ref, kv0, kv1, kv2, kv3, seg_q, seg_k, o_ref, lse_ref, bias, kn, vt, sc
):
    y = y_ref[0]

    @pl.when(pl.program_id(0) == 0)
    def _():
        write_bias(bias, seg_q, seg_k, y, half)

    for r, kv in enumerate((kv0, kv1, kv2, kv3)):

        def fill(r=r, kv=kv):
            kn[r] = kv[0].T
            vt[r] = kv[1]

        pl.when(y >= r)(fill)
    scale = jnp.asarray(HEAD_WIDTH**-0.5, BF)
    qs = [q_ref[h * HEAD_WIDTH : (h + 1) * HEAD_WIDTH] * scale for h in range(GROUP)]

    def scores(r, rows, tops):
        out = []
        for h in range(GROUP):
            s = nn(kn[r, rows, :], qs[h]) + bias[r, rows, :]
            sc[h, r, rows, :] = s
            out.append(jnp.maximum(tops[h], fold(s, jnp.max)))
        return tuple(out)

    own = slice(0, (half + 1) * HALF)
    low = tuple(jnp.full((8, HALF), MASKED, F32) for _ in range(GROUP))
    tops = scores(0, own, low)
    tops = lax.fori_loop(1, y + 1, lambda r, t: scores(r, slice(0, SPAN), t), tops)
    tops = [jnp.max(t, axis=0, keepdims=True) for t in tops]

    def mix(r, rows, carry):
        totals, acc = carry
        out, weights = [], []
        for h in range(GROUP):
            p = jnp.exp(sc[h, r, rows, :] - tops[h])
            out.append(totals[h] + fold(p, jnp.sum))
            weights.append(p.astype(BF))
        return tuple(out), acc + nn(vt[r, :, rows], jnp.concatenate(weights, 1))

    zero = (
        tuple(jnp.zeros((8, HALF), F32) for _ in range(GROUP)),
        jnp.zeros((HEAD_WIDTH, GROUP * HALF), F32),
    )
    carry = mix(0, own, zero)
    totals, acc = lax.fori_loop(1, y + 1, lambda r, c: mix(r, slice(0, SPAN), c), carry)
    for h in range(GROUP):
        total = jnp.sum(totals[h], axis=0, keepdims=True)
        mixed = acc[:, h * HALF : (h + 1) * HALF] / total
        o_ref[h * HEAD_WIDTH : (h + 1) * HEAD_WIDTH, :] = mixed.astype(BF)
        lse_ref[0, h : h + 1, :] = tops[h] + jnp.log(total)


def attend(half, y, q_t, kvs, seg_q, seg_k):
    rows = GROUP * HEAD_WIDTH
    heads = q_t.shape[0] // rows
    kv_spec = pl.BlockSpec((2, HEAD_WIDTH, SPAN), lambda g: (0, g, 0))
    return pl.pallas_call(
        functools.partial(fwd_kernel, half),
        grid=(heads,),
        in_specs=[
            pl.BlockSpec(memory_space=pltpu.SMEM),
            pl.BlockSpec((rows, HALF), lambda g: (g, half)),
            kv_spec,
            kv_spec,
            kv_spec,
            kv_spec,
            pl.BlockSpec((1, HALF), lambda g: (0, half)),
            pl.BlockSpec((4 * SPAN, 1), lambda g: (0, 0)),
        ],
        out_specs=[
            pl.BlockSpec((rows, HALF), lambda g: (g, 0)),
            pl.BlockSpec((1, 8, HALF), lambda g: (g, 0, 0)),
        ],
        out_shape=[
            jax.ShapeDtypeStruct((q_t.shape[0], HALF), BF),
            jax.ShapeDtypeStruct((heads, 8, HALF), F32),
        ],
        scratch_shapes=[
            pltpu.VMEM((4, SPAN, HALF), F32),
            pltpu.VMEM((4, SPAN, HEAD_WIDTH), BF),
            pltpu.VMEM((4, HEAD_WIDTH, SPAN), BF),
            pltpu.VMEM((GROUP, 4, SPAN, HALF), F32),
        ],
        compiler_params=pltpu.CompilerParams(vmem_limit_bytes=40 << 20),
        cost_estimate=pl.CostEstimate(
            flops=14_000_000_000, bytes_accessed=6_000_000, transcendentals=6_000_000
        ),
    )(y, q_t, *kvs, seg_q, seg_k)


def bwd_kernel(y_ref, q_ref, d_ref, o_0, o_1, lse_0, lse_1, kv0, kv1, kv2, kv3, seg_q, seg_k, dq_ref, g0, g1, g2, g3, bias, kn, vn, kt, dvk):
    y = y_ref[0]
    @pl.when(pl.program_id(0)==0)
    def _(): write_bias(bias, seg_q, seg_k, y, 0)
    for r,kv in enumerate((kv0,kv1,kv2,kv3)):
        def fill(r=r,kv=kv):
            kn[r] = kv[0].T
            vn[r] = kv[1].T
            kt[r] = kv[0]
        pl.when(y>=r)(fill)
    dvk[...] = jnp.zeros_like(dvk)
    scale = jnp.asarray(HEAD_WIDTH**-0.5, BF)
    for b in range(2):
        cols = slice(b*HALF,(b+1)*HALF)
        qs, qn, ds, dn, dots, lses = [],[],[],[],[],[]
        for h in range(GROUP):
            hr = slice(h*HEAD_WIDTH,(h+1)*HEAD_WIDTH)
            q = q_ref[hr, cols]*scale
            qs.append(q); qn.append(q.T)
            d = d_ref[hr, cols]
            ds.append(d); dn.append(d.T)
            dots.append(jnp.sum(d.astype(F32)*(o_0, o_1)[b][hr].astype(F32),axis=0,keepdims=True))
            lses.append((lse_0, lse_1)[b][0, h : h + 1])
        right = []
        for h in range(GROUP):
            none = jnp.zeros_like(dn[h])
            right += [jnp.concatenate([dn[h], none], 1), jnp.concatenate([none, qn[h]], 1)]
        right = jnp.concatenate(right, 0)

        def step(r, rows, carry):
            left = []
            for h in range(GROUP):
                s = nn(kn[r, rows, :], qs[h]) + bias[r, rows, cols]
                p = jnp.exp(s - lses[h])
                dp = nn(vn[r, rows, :], ds[h])
                dsc = (p * (dp - dots[h])).astype(BF)
                left += [p.astype(BF), dsc]
            dvk[r, rows, :] += nn(jnp.concatenate(left, 1), right)
            return carry + nn(kt[r, :, rows], jnp.concatenate(left[1::2], 1))

        carry = step(0, slice(0, (b + 1) * HALF), jnp.zeros((HEAD_WIDTH, GROUP * HALF), F32))
        carry = lax.fori_loop(1, y+1, lambda r,c: step(r, slice(0,SPAN), c), carry)
        for h in range(GROUP):
            dq_ref[h*HEAD_WIDTH:(h+1)*HEAD_WIDTH, cols] = (
                carry[:, h * HALF : (h + 1) * HALF] * HEAD_WIDTH**-0.5
            ).astype(BF)
    for r,g in enumerate((g0,g1,g2,g3)):
        turned = dvk[r].T.astype(BF)
        g[0] = turned[HEAD_WIDTH:]
        g[1] = turned[:HEAD_WIDTH]

def attend_back(first, count, y, q_t, d_t, outs, lses, kvs, seg_q, seg_k):
    rows = GROUP * HEAD_WIDTH
    kv_spec = pl.BlockSpec((2, HEAD_WIDTH, SPAN), lambda g: (0, first + g, 0))
    q_spec = pl.BlockSpec((rows, SPAN), lambda g: (first + g, 0))
    o_spec = pl.BlockSpec((rows, HALF), lambda g: (first + g, 0))
    lse_spec = pl.BlockSpec((1, 8, HALF), lambda g: (first + g, 0, 0))
    kv_shape = jax.ShapeDtypeStruct((2, count * HEAD_WIDTH, SPAN), BF)
    return pl.pallas_call(
        bwd_kernel,
        grid=(count,),
        in_specs=[pl.BlockSpec(memory_space=pltpu.SMEM), q_spec, q_spec]
        + [o_spec, o_spec, lse_spec, lse_spec]
        + [kv_spec] * 4
        + [pl.BlockSpec((1, SPAN), lambda g: (0, 0)), pl.BlockSpec((4 * SPAN, 1), lambda g: (0, 0))],
        out_specs=[pl.BlockSpec((rows, SPAN), lambda g: (g, 0))]
        + [pl.BlockSpec((2, HEAD_WIDTH, SPAN), lambda g: (0, g, 0))] * 4,
        out_shape=[jax.ShapeDtypeStruct((count * rows, SPAN), BF)] + [kv_shape] * 4,
        scratch_shapes=[pltpu.VMEM((4, SPAN, SPAN), F32)]
        + [pltpu.VMEM((4, SPAN, HEAD_WIDTH), BF)] * 2
        + [pltpu.VMEM((4, HEAD_WIDTH, SPAN), BF)]
        + [pltpu.VMEM((4, SPAN, 2 * HEAD_WIDTH), F32)],
        compiler_params=pltpu.CompilerParams(vmem_limit_bytes=60 << 20),
        cost_estimate=pl.CostEstimate(
            flops=150_000_000_000, bytes_accessed=6_000_000, transcendentals=6_000_000
        ),
    )(y, q_t, d_t, *outs, *lses, *kvs, seg_q, seg_k)


def flat(ref):
    return ref[...].reshape(ref.shape[0] * ref.shape[3], ref.shape[4])


def experts_kernel(x_ref, gate_ref, up_ref, down_ref, g_ref, u_ref, inner_ref, out_ref, acc):
    step = pl.program_id(0)
    down_t = flat(down_ref).T

    @pl.when(step == 0)
    def _():
        acc[...] = jnp.zeros_like(acc)

    x = x_ref[...]
    g_ref[...] = nn(x, flat(gate_ref))
    u_ref[...] = nn(x, flat(up_ref))
    for m in range(x_ref.shape[0] // HALF):
        rows = slice(m * HALF, (m + 1) * HALF)
        gate = g_ref[rows]
        inner_ref[rows] = (gate * jax.nn.sigmoid(gate) * u_ref[rows]).astype(BF)
    for n in range(acc.shape[1] // SPAN):
        cols = slice(n * SPAN, (n + 1) * SPAN)
        acc[:, cols] += nn(inner_ref[...], down_t[:, cols])

    @pl.when(step == pl.num_programs(0) - 1)
    def _():
        out_ref[...] = acc[...].astype(BF)


def experts_back_kernel(
    d_ref, g_ref, u_ref, gate_ref, up_ref, down_ref, dg_ref, du_ref, out_ref, acc, inner
):
    step = pl.program_id(0)
    gate_t = flat(gate_ref).T
    up_t = flat(up_ref).T

    @pl.when(step == 0)
    def _():
        acc[...] = jnp.zeros_like(acc)

    inner[...] = nn(d_ref[...], flat(down_ref))
    for m in range(d_ref.shape[0] // HALF):
        rows = slice(m * HALF, (m + 1) * HALF)
        d_inner = inner[rows]
        gate = g_ref[rows]
        sig = jax.nn.sigmoid(gate)
        dg_ref[rows] = (d_inner * u_ref[rows] * sig * (1.0 + gate * (1.0 - sig))).astype(BF)
        du_ref[rows] = (d_inner * gate * sig).astype(BF)
    for n in range(acc.shape[1] // SPAN):
        cols = slice(n * SPAN, (n + 1) * SPAN)
        acc[:, cols] += nn(dg_ref[...], gate_t[:, cols]) + nn(du_ref[...], up_t[:, cols])

    @pl.when(step == pl.num_programs(0) - 1)
    def _():
        out_ref[...] = acc[...].astype(BF)


def expert_grads_kernel(x_ref, d_ref, dg_ref, du_ref, inner_ref, out_ref, x_t, d_t):
    @pl.when(pl.program_id(0) == 0)
    def _():
        x_t[...] = x_ref[...].T
        d_t[...] = d_ref[...].T

    depth = out_ref.shape[3]
    for i, (left, right) in enumerate(((x_t, dg_ref), (x_t, du_ref), (d_t, inner_ref))):
        for y in range(4):
            out_ref[y, 0, i] = nn(left[y * depth : (y + 1) * depth], right[...]).astype(BF)


def expert_specs(rows, width, hidden):
    whole = pl.BlockSpec((rows, width), lambda b: (0, 0))
    weights = [
        pl.BlockSpec(
            (4, 1, 1, width // 4, HALF),
            functools.partial(lambda i, b: (0, b // 2, i, 0, b % 2), i),
        )
        for i in range(3)
    ]
    column = pl.BlockSpec((rows, HALF), lambda b: (0, b))
    return dict(
        grid=(hidden // HALF,),
        scratch_shapes=[pltpu.VMEM((rows, width), F32)],
        compiler_params=pltpu.CompilerParams(vmem_limit_bytes=60 << 20),
        cost_estimate=pl.CostEstimate(
            flops=6 * rows * width * hidden, bytes_accessed=20_000_000, transcendentals=rows * hidden
        ),
    ), whole, weights, column


def run_experts(x, experts_full):
    rows, width = x.shape
    hidden = 2 * experts_full.shape[4]
    common, whole, weights, column = expert_specs(rows, width, hidden)
    common["compiler_params"] = pltpu.CompilerParams(vmem_limit_bytes=40 << 20)
    wide = jax.ShapeDtypeStruct((rows, hidden), F32)
    return pl.pallas_call(
        experts_kernel,
        in_specs=[whole] + weights,
        out_specs=[column, column, column, whole],
        out_shape=[
            wide,
            wide,
            jax.ShapeDtypeStruct((rows, hidden), BF),
            jax.ShapeDtypeStruct((rows, width), BF),
        ],
        **common,
    )(x, experts_full, experts_full, experts_full)


def run_experts_back(d, gate, up, experts_full):
    rows, width = d.shape
    hidden = 2 * experts_full.shape[4]
    common, whole, weights, column = expert_specs(rows, width, hidden)
    low = jax.ShapeDtypeStruct((rows, hidden), BF)
    common["scratch_shapes"] = common["scratch_shapes"] + [pltpu.VMEM((rows, HALF), F32)]
    return pl.pallas_call(
        experts_back_kernel,
        in_specs=[whole, column, column] + weights,
        out_specs=[column, column, whole],
        out_shape=[low, low, jax.ShapeDtypeStruct((rows, width), BF)],
        **common,
    )(d, gate, up, experts_full, experts_full, experts_full)


def expert_grads(x, d, d_gate, d_up, inner):
    rows, width = x.shape
    hidden = inner.shape[1]
    common, whole, _, column = expert_specs(rows, width, hidden)
    common["scratch_shapes"] = [pltpu.VMEM((width, rows), BF)] * 2
    return pl.pallas_call(
        expert_grads_kernel,
        in_specs=[whole, whole, column, column, column],
        out_specs=pl.BlockSpec((4, 1, 3, width // 4, HALF), lambda b: (0, b // 2, 0, 0, b % 2)),
        out_shape=jax.ShapeDtypeStruct((4, 2, 3, width // 4, hidden // 2), BF),
        **common,
    )(x, d, d_gate, d_up, inner)


def grads_kernel(plan, first_axis, core_ref, *refs):
    ins, (own_ref, other_ref, pack) = refs[:-3], refs[-3:]
    at = 0
    turned = {}
    for terms in plan:
        total = None
        for left, right, first in terms:
            if left is None:
                high = ins[right][...].astype(BF).astype(F32)
                rest = ins[right][...] - high
                total = jnp.zeros((384, 128), F32) if total is None else total
                pack[:, at : at + 128] = total
                pack[:, at + 16 : at + 24] = high.T
                pack[:, at + 24 : at + 32] = rest.T
                total = None
                at = at + 128
                continue
            if left not in turned:
                turned[left] = ins[left][...].T
            width = ins[right].shape[1]
            rows = turned[left][:, first : first + width]
            piece = dot(rows, ins[right][...], 1, 1)
            total = piece if total is None else total + piece
        if total is not None:
            pack[:, at : at + total.shape[1]] = total
            at = at + total.shape[1]
    for core in range(2):

        @pl.when(core_ref[0] == core)
        def _(core=core):
            for j in range(2):
                for y in range(4):
                    for ref, c in ((own_ref, core), (other_ref, 1 - core)):
                        row = (2 * j + c) * 96 + y * 24
                        value = pack[row : row + 24, :].astype(BF)
                        if first_axis == "x":
                            ref[j, y, 0] = value
                        else:
                            ref[y, j, 0] = value


def pack_grads(plan, first_axis, arrays, wide, cols, flops):
    specs = []
    for i, value in enumerate(arrays):
        if i in wide:
            specs.append(pl.BlockSpec((value.shape[0], 384), lambda b: (0, b)))
        else:
            specs.append(pl.BlockSpec(value.shape, lambda b: (0, 0)))
    out = jax.ShapeDtypeStruct((4, 4, 2, 24, cols), BF)
    if first_axis == "x":
        out_spec = pl.BlockSpec((2, 4, 1, 24, cols), lambda b: (b % 2, 0, b // 2, 0, 0))
    else:
        out_spec = pl.BlockSpec((4, 2, 1, 24, cols), lambda b: (0, b % 2, b // 2, 0, 0))
    return pl.pallas_call(
        functools.partial(grads_kernel, plan, first_axis),
        grid=(arrays[wide[0]].shape[1] // 384,),
        in_specs=[pl.BlockSpec(memory_space=pltpu.SMEM)] + specs,
        out_specs=[out_spec, out_spec],
        out_shape=[out, out],
        scratch_shapes=[pltpu.VMEM((384, cols), F32)],
        compiler_params=pltpu.CompilerParams(
            vmem_limit_bytes=(60 if len(arrays) > 4 else 40) << 20
        ),
        cost_estimate=pl.CostEstimate(
            flops=flops, bytes_accessed=flops // 2000, transcendentals=0
        ),
    )(jnp.full((1,), lax.axis_index("c"), jnp.int32), *arrays)


def token_grads_kernel(tokens_ref, gain_ref, mine_ref, other_ref, later_ref, out_ref):
    resid = tokens_ref[...].astype(F32)
    scale = rms_scale(resid)
    gained = both(mine_ref[...], other_ref[...]) * gain_ref[...]
    middle = jnp.mean(resid * gained, axis=-1, keepdims=True)
    out_ref[...] = later_ref[...] + (scale * gained - resid * scale * scale * scale * middle)


def token_grads(tokens, gain_row, mine, other, later):
    rows, width = tokens.shape
    block = pl.BlockSpec((128, width), lambda b: (b, 0))
    return pl.pallas_call(
        token_grads_kernel,
        grid=(rows // 128,),
        in_specs=[block, pl.BlockSpec((1, width), lambda b: (0, 0)), block, block, block],
        out_specs=block,
        out_shape=jax.ShapeDtypeStruct((rows, width), F32),
        compiler_params=pltpu.CompilerParams(vmem_limit_bytes=60 << 20),
        cost_estimate=pl.CostEstimate(
            flops=12 * rows * width, bytes_accessed=14 * rows * width, transcendentals=rows
        ),
    )(tokens, gain_row, mine, other, later)


def turned_sum_kernel(left_ref, right_ref, out_ref):
    out_ref[...] = both(left_ref[...], right_ref[...]).T


def turned_sum(left, right):
    rows, cols = left.shape
    return pl.pallas_call(
        turned_sum_kernel,
        out_shape=jax.ShapeDtypeStruct((cols, rows), F32),
        compiler_params=pltpu.CompilerParams(vmem_limit_bytes=16 << 20),
        cost_estimate=pl.CostEstimate(
            flops=2 * rows * cols, bytes_accessed=8 * rows * cols, transcendentals=0
        ),
    )(left, right)


def pair_blocks(own, theirs, axis):
    received = swap(theirs, "c")
    me = lax.axis_index(axis)
    blocks = []
    for r in range(4):
        mine, other = (
            lax.dynamic_index_in_dim(part, (me + r) % 4, 0, keepdims=False)
            for part in (own, received)
        )
        blocks.append(both(mine, other).astype(BF))
    return blocks


def send_blocks(blocks, axis):
    return blocks[:1] + [
        lax.ppermute(blocks[r], axis, [(i, (i + r) % 4) for i in range(4)]) for r in range(1, 4)
    ]


def local(
    tokens,
    teacher,
    segments,
    routes,
    route_weight,
    norm_attn,
    w_query,
    key_weight,
    value_weight,
    w_out,
    norm_ffn,
    w_router,
    w_gate,
    w_up,
    w_down,
):
    tok_rows, feat_width = tokens.shape
    q_width = w_query.shape[1]
    k_width = key_weight.shape[1]
    tix = lax.axis_index("t")
    yix = lax.axis_index("y")

    small = jnp.concatenate(
        [
            w_router,
            norm_attn[:, None],
            norm_ffn[:, None],
            jnp.zeros((w_router.shape[0], 128 - EXPERTS - 2), BF),
        ],
        axis=1,
    )
    experts = jnp.stack([w_gate[0], w_up[0], w_down[0].T])
    by_hy, experts = lax.optimization_barrier(
        (
            gather_hy(
                jnp.concatenate([key_weight, value_weight, small, w_query, w_out.T], axis=1)
            ),
            experts,
        )
    )
    kv_cols = 2 * k_width + 128
    wide_rest = by_hy[:, :, kv_cols:]
    wide_rest = jnp.broadcast_to(wide_rest[None], (4, *wide_rest.shape))
    ring_kv, wide_rest = lax.optimization_barrier((gather_x(by_hy[:, :, :kv_cols]), wide_rest))
    experts_other = swap(experts, "t")
    ring_rest = lax.all_to_all(wide_rest, "x", 0, 0, tiled=True)
    pack = core_gather(ring_kv)
    full_kv = pack[:, : 2 * k_width]
    full_small = pack[:, 2 * k_width :]
    small_rows = dot(jnp.eye(24, 128, dtype=BF), full_small, 1, 1)
    router_rows = small_rows[:EXPERTS].astype(BF)
    gain_one = small_rows[EXPERTS : EXPERTS + 1]
    gain_two = small_rows[EXPERTS + 1 : EXPERTS + 2]

    resid_in = tokens.astype(F32)
    scale_one = rms_scale(resid_in)
    act_one = (resid_in * scale_one * gain_one).astype(BF)
    kv_mine = dot(full_kv, act_one, 0, 1).astype(BF).reshape(2, k_width, tok_rows)
    kvs = [kv_mine] + [
        lax.ppermute(kv_mine, "y", [(i, i + r) for i in range(4 - r)]) for r in (1, 2, 3)
    ]
    experts_other, ring_rest = lax.optimization_barrier((experts_other, ring_rest))
    experts_full = jnp.stack([experts, experts_other])
    *kvs[1:], ring_rest, experts_full = lax.optimization_barrier(
        (*kvs[1:], ring_rest, experts_full)
    )
    rest = core_gather(ring_rest)
    full_query = rest[:, :q_width]
    full_out = rest[:, q_width:]
    query_t = dot(full_query, act_one, 0, 1).astype(BF)

    experts_full = lax.all_gather(experts_full, "y", axis=0)

    seg_blocks = segments[0].reshape(4, tok_rows)
    seg_mine = lax.dynamic_index_in_dim(seg_blocks, yix, 0, keepdims=False)
    seg_keys = jnp.concatenate(
        [lax.dynamic_index_in_dim(seg_blocks, (yix + 4 - r) % 4, 0, keepdims=False) for r in range(4)]
    )[:, None]
    place_y = jnp.full((1,), yix, jnp.int32)
    mixed_0, log_0 = attend(0, place_y, query_t, kvs, seg_mine[None], seg_keys)
    part_0 = dot(mixed_0, full_out, 0, 1).astype(BF)
    mixed_1, log_1 = attend(1, place_y, after(query_t, part_0), kvs, seg_mine[None], seg_keys)
    other_0 = swap(part_0, "t")
    part_1 = dot(after(mixed_1, other_0), full_out, 0, 1).astype(BF)
    other_1 = swap(part_1, "t")
    hidden = resid_in + jnp.concatenate([both(part_0, other_0), both(part_1, other_1)])
    scale_two = rms_scale(hidden)
    act_two = (hidden * scale_two * gain_two).astype(BF)

    logits = dot(router_rows, act_two, 1, 1)
    router = jax.nn.softmax(logits, axis=0)
    route_cols = routes.T
    weight_cols = route_weight.T
    expert_iota = lax.broadcasted_iota(jnp.int32, (EXPERTS, tok_rows), 0)
    named = [expert_iota == route_cols[k : k + 1] for k in range(TOP)]
    taken = (named[0] | named[1]).astype(BF)
    earlier = (
        lax.broadcasted_iota(jnp.int32, (tok_rows, tok_rows), 0)
        < lax.broadcasted_iota(jnp.int32, (tok_rows, tok_rows), 1)
    ).astype(BF)
    count_before = dot(taken, earlier, 1, 0)
    half = CAPACITY // 2
    slot_iota = lax.broadcasted_iota(jnp.int32, (EXPERTS * half, tok_rows), 0)
    picks = []
    gates = []
    for k in range(TOP):
        place = jnp.sum(jnp.where(named[k], count_before, 0.0), axis=0, keepdims=True)
        place = place.astype(jnp.int32) - tix * half
        slot = jnp.where((place >= 0) & (place < half), route_cols[k : k + 1] * half + place, -1)
        picks.append(slot_iota == slot)
        chosen = jnp.sum(jnp.where(named[k], router, 0.0), axis=0, keepdims=True)
        gates.append(chosen * weight_cols[k : k + 1])
    pick = (picks[0] | picks[1]).astype(BF)
    gated_pick = (
        jnp.where(picks[0], gates[0], 0.0) + jnp.where(picks[1], gates[1], 0.0)
    ).astype(BF)

    received, pick_t, gated_pick_t = lax.optimization_barrier(
        (exchange_slots(dot(pick, act_two, 1, 0).astype(BF)), pick.T, gated_pick.T)
    )
    gate_proj, up_proj, inner, slots_out = run_experts(received, experts_full)
    returned = exchange_slots(slots_out)
    part = dot(gated_pick_t, returned, 1, 0).astype(BF)
    output = hidden + both(part, swap(part, "t"))
    valid = (seg_mine != 0).astype(F32)
    difference = output - teacher.astype(F32)
    grad_output = difference * valid[:, None]
    sse = jnp.sum(grad_output * difference)
    count = jnp.sum(valid)
    grad_low = grad_output.astype(BF)
    d_received = exchange_slots(dot(gated_pick, grad_low, 1, 0).astype(BF))

    slot_dots = dot(returned, grad_low, 1, 1)
    d_gates = jnp.concatenate(
        [jnp.sum(jnp.where(picks[k], slot_dots, 0.0), axis=0, keepdims=True) for k in range(TOP)]
    )
    d_gates_other = swap(d_gates, "t")
    d_received = after(d_received, d_gates_other)
    d_gates = d_gates + d_gates_other

    d_gate_proj, d_up_proj, d_slots = run_experts_back(
        d_received, gate_proj, up_proj, experts_full
    )
    d_returned = exchange_slots(d_slots)
    received, d_received = after(received, d_slots), after(d_received, d_slots)

    grad_parts = expert_grads(received, d_received, d_gate_proj, d_up_proj, inner)
    grad_experts = lax.psum_scatter(grad_parts, "y", scatter_dimension=0)
    d_returned = after(d_returned, grad_parts)
    keep, give = grad_experts[0], grad_experts[1]

    d_router = jnp.where(named[0], d_gates[0:1] * weight_cols[0:1], 0.0) + jnp.where(
        named[1], d_gates[1:2] * weight_cols[1:2], 0.0
    )
    d_logits = (
        router * (d_router - jnp.sum(router * d_router, axis=0, keepdims=True))
    ).astype(BF)
    d_route = dot(d_logits, router_rows, 0, 0)
    part = dot(pick_t, d_returned, 1, 0).astype(BF)
    d_act_two = d_route + both(part, after(swap(part, "t"), d_route))
    d_norm_two, grad_gain_two = norm_back(hidden, scale_two, gain_two, d_act_two)
    d_hidden = grad_output + d_norm_two
    d_attn = d_hidden.astype(BF)
    d_mixed_t = dot(full_out, d_attn, 0, 1).astype(BF)

    saved = ((mixed_0, mixed_1), (log_0, log_1), kvs, seg_mine[None], seg_keys)
    half_groups = k_width // HEAD_WIDTH // 2
    back_0 = attend_back(0, half_groups, place_y, query_t, d_mixed_t, *saved)

    def ring_back(parts):
        return [
            lax.ppermute(parts[r], "y", [(i, i - r) for i in range(r, 4)]) for r in (1, 2, 3)
        ]

    *back_0, d_mixed_t, give = lax.optimization_barrier((*back_0, d_mixed_t, give))
    back_1 = attend_back(half_groups, half_groups, place_y, query_t, d_mixed_t, *saved)
    others_0 = ring_back(back_0[1:])
    given_0 = swap(give[:2], "t")
    *back_1, o1, o2, o3, given_0, give, d_attn_late, gain_late, d_logits_late, back_0[0] = (
        lax.optimization_barrier(
            (*back_1, *others_0, given_0, give[2], d_attn, grad_gain_two, d_logits, back_0[0])
        )
    )
    others_0 = [o1, o2, o3]

    others_1 = ring_back(back_1[1:])
    given_1 = swap(give, "t")
    lines = jnp.concatenate(
        [
            gain_late,
            jnp.full((1, feat_width), sse),
            jnp.full((1, feat_width), count),
            jnp.zeros((5, feat_width), F32),
        ]
    )
    logits_pad = jnp.concatenate(
        [d_logits_late, jnp.zeros((128 - EXPERTS, tok_rows), BF)]
    )
    own_one, theirs_one = pack_grads(
        (
            ((0, 4, 0), (0, 5, HALF)),
            ((2, 6, 0), (None, 3, 0)),
            ((1, 7, 0),),
            ((1, 8, 0),),
        ),
        "x",
        (d_attn_late, act_one, act_two, lines, mixed_0, mixed_1, logits_pad, back_0[0], back_1[0]),
        (0, 1, 2, 3),
        feat_width // 2 + 128 + q_width,
        20_000_000_000,
    )
    o1, o2, o3, given_1, own_one, theirs_one, dq_0, dq_1 = lax.optimization_barrier(
        (*others_1, given_1, own_one, theirs_one, back_0[0], back_1[0])
    )

    d_kv_t = jnp.concatenate(
        [added([back_0[1], *others_0]), added([back_1[1], o1, o2, o3])], axis=1
    ).reshape(2 * k_width, tok_rows).astype(BF)
    d_act_part = dot(jnp.concatenate([dq_0, dq_1]), full_query, 0, 1) + dot(d_kv_t, full_kv, 0, 1)
    part = d_act_part.astype(BF)
    blocks_one = pair_blocks(own_one, theirs_one, "x")
    gain_row = jnp.sum(d_act_part * resid_in * scale_one, axis=0, keepdims=True)
    lines = jnp.concatenate(
        [gain_row, jnp.zeros((7, feat_width), F32)]
    )
    own_two, theirs_two = pack_grads(
        (((0, 2, 0),), ((None, 1, 0),)),
        "y",
        (act_one, lines, d_kv_t),
        (0, 1),
        2 * k_width + 128,
        2_000_000_000,
    )
    part, own_two, theirs_two, *blocks_one = lax.optimization_barrier(
        (part, own_two, theirs_two, *blocks_one)
    )
    other = swap(part, "t")
    parts_one = send_blocks(blocks_one, "x")
    paired_two = both(own_two, swap(theirs_two, "c")).astype(BF)
    ring_two = lax.all_to_all(paired_two, "y", 0, 0, tiled=True)
    grad_wide = keep[:2].astype(F32) + given_0.astype(F32)
    own_down = turned_sum(keep[2], given_1)
    *parts_one, ring_two, own_down, other = lax.optimization_barrier(
        (*parts_one, ring_two, own_down, other)
    )
    by_x = added(parts_one).astype(BF)
    by_y = jnp.sum(ring_two.astype(F32), axis=0).astype(BF)
    by_xy = jnp.concatenate(
        [added(axis_parts(by_x, "y", 4)), added(axis_parts(by_y, "x", 4))], axis=2
    ).astype(BF)
    by_xy, other = lax.optimization_barrier((by_xy, other))
    summed = added(axis_parts(by_xy, "h", 2))
    own_kv = summed[:, by_x.shape[3] :]
    own_query = summed[:, feat_width // 2 + 128 : by_x.shape[3]]
    at = feat_width // 2
    own_out = summed[:, :at].T
    own_router = summed[:, at : at + EXPERTS]
    at = at + EXPERTS
    own_gain_two = summed[:, at] + summed[:, at + 8]
    loss_value = (summed[0, at + 1] + summed[0, at + 9]) / (
        feat_width * (summed[0, at + 2] + summed[0, at + 10])
    )
    own_gain_one = own_kv[:, 2 * k_width + EXPERTS] + own_kv[:, 2 * k_width + EXPERTS + 8]
    grad_tokens = token_grads(tokens, gain_one, part, other, d_hidden)
    own_gain_one = own_gain_one + swap(own_gain_one, "t")
    return (
        output,
        loss_value,
        grad_tokens,
        own_gain_one,
        own_query,
        own_kv[:, :k_width],
        own_kv[:, k_width : 2 * k_width],
        own_out,
        own_gain_two,
        own_router,
        grad_wide[0][None],
        grad_wide[1][None],
        own_down[None],
    )


def solution(mesh):
    fine = Mesh(mesh.devices.reshape(2, 4, 2, 4, 2), ("h", "x", "c", "y", "t"))
    fsdp = ("h", "x", "c")
    every = ("h", "x", "c", "y")
    return jax.shard_map(
        local,
        mesh=fine,
        in_specs=(
            P(every, None),
            P(every, None),
            P(fsdp, None),
            P(every, None),
            P(every, None),
            P(every),
            P(every, "t"),
            P(every, "t"),
            P(every, "t"),
            P("t", every),
            P(every),
            P(every, None),
            P(fsdp, "y", "t"),
            P(fsdp, "y", "t"),
            P(fsdp, "t", "y"),
        ),
        out_specs=(
            P(every, None),
            P(),
            P(every, None),
            P(every),
            P(every, "t"),
            P(every, "t"),
            P(every, "t"),
            P("t", every),
            P(every),
            P(every, None),
            P(fsdp, "y", "t"),
            P(fsdp, "y", "t"),
            P(fsdp, "t", "y"),
        ),
        check_vma=False,
    )
```
